256 devices in a mesh: sweep: 4 (over x), dom: 64 (over z, y, core).
Axes of the slice: x: 4, y: 4, z: 8, core: 2. Of those that a mesh axis runs over, the one named last changes fastest.
Arguments:
- fluid_state: float32 [5, 4194304], P(None, ('sweep', 'dom')), parts along dimension 1, may hold values from -6 to 6
- residual_base: float32 [5, 4194304], P(None, ('sweep', 'dom')), parts along dimension 1, may hold values from -6 to 6
- jacobian: bfloat16 [7, 5, 5, 4194304], P(None, None, None, ('sweep', 'dom')), parts along dimension 3, may hold values from -1 to 1
- columns: int32 [7, 4194304], P(None, ('sweep', 'dom')), parts along dimension 1, may hold values from 0 to 19455, as said below
- pseudo_step: float32 [4194304], P(('sweep', 'dom')), parts along dimension 0, may hold values from 0.1 to 1
- send_cells: int32 [1536, 512], P(('sweep', 'dom')), parts along dimension 0, may hold values from 0 to 16383
- interface_face_cell: int32 [1048576], P(('sweep', 'dom')), parts along dimension 0, may hold values from 0 to 16383
- interface_face_area_vector: float32 [3, 1048576], P(None, ('sweep', 'dom')), parts along dimension 1, may hold values from -6 to 6
- mortar_weight: float32 [1048576], P(('sweep', 'dom')), parts along dimension 0, may hold values from 0.5 to 1.5
- face_route: int32 [1048576, 1], P(('sweep', 'dom')), parts along dimension 0, may hold values from 0 to 63; in each aligned block of 4096 rows (0 to 4095, 4096 to 8191, ...) at most 128 rows name the same one
- face_node: int32 [1048576], P(('sweep', 'dom')), parts along dimension 0, may hold values from 0 to 511
- compliance: float32 [1024, 384, 384], P(('sweep', 'dom')), parts along dimension 0, may hold values from -0.3125 to 0.3125
Outputs:
- residual: float32 [5, 4194304], P(None, ('sweep', 'dom')), parts along dimension 1
- displacement: float32 [3, 131072], P(None, ('sweep', 'dom')), parts along dimension 1
- face_motion: float32 [3, 1048576], P(None, ('sweep', 'dom')), parts along dimension 1
The draws below stay inside these ranges and needn't reach their ends.
There are 4 independent parts, one for each index of `sweep`. The reference program is written for one: setup_inputs(seed, part) draws one part's arguments, and reference() takes and returns one part's arrays. A program takes and returns all parts, laid end to end along the dimension named above; each array names one. Nothing has to cross between parts.
Inputs may be any that keep to these rules, and one draw needn't show every extreme that they name: `columns`: a value j >= 16384 refers to halo slot j - 16384, from neighbour group n = (j - 16384) // 512, and only where the neighbour device d + o[n] of the cell's device d exists (0 <= d + o[n] < number of dom devices). For a cell at local position l with row block q = l // 512: a value j < 16384 satisfies q * 512 - 64 <= j < (q + 1) * 512 + 64, and a value j >= 16384 has q * 16 <= (j - 16384) % 512 < (q + 1) * 16. `send_cells`: row p times 6 plus m lists local cells of device p that device p + o[m] reads; rows whose device p + o[m] does not exist are read by nobody. `face_route`: among the faces of one device at most 128 name the same structure device, and in every draw some device's faces name one structure device exactly 128 times.
All inputs are finite; a program needn't handle non-finite values.
Results may differ from the reference program's by a relative error of at most 0.0003.
Values sent between devices are 32-bit elements; how exact they have to be, the bound alone decides.
A program may use at most 128 MiB of HBM per device.

```python
import math
import jax
import jax.numpy as jnp
import numpy as np
from jax import lax

CELL_DEV = 16384
HALO_SLOT = 512
FACE_DEV = 4096
NB = 7
NEIGH = 6
TN = 128
NCELL = 1048576
NFACE = 262144
CAP = 128
SN = 512
NNODE = 32768
NTILES = 256
N_DOM = 64


OFFSETS = (-3, -2, -1, 1, 2, 3)


def draw_columns(key, part):
    key = jax.random.fold_in(key, 11)
    key_local, key_far, key_group, key_slot = jax.random.split(key, 4)
    block_rows = min(512, CELL_DEV)
    reach = block_rows // 8
    slot_width = HALO_SLOT * block_rows // CELL_DEV
    position = jnp.arange(NCELL, dtype=jnp.int32) % CELL_DEV
    row_block = (position // block_rows)[None, :]
    local = row_block * block_rows - reach + jax.random.randint(key_local, (NB, NCELL), 0, block_rows + 2 * reach)
    local = jnp.clip(local, 0, CELL_DEV - 1)
    remote_flag = jax.random.randint(key_far, (NB, NCELL), 0, 100) < 15
    group = jax.random.randint(key_group, (NB, NCELL), 0, NEIGH)
    within = row_block * slot_width + jax.random.randint(key_slot, (NB, NCELL), 0, slot_width)
    device = (jnp.arange(NCELL, dtype=jnp.int32) // CELL_DEV)[None, :]
    group_offsets = jnp.array(np.array(OFFSETS, dtype=np.int32))
    target = device + group_offsets[group]
    missing = (target < 0) | (target >= N_DOM)
    group = jnp.where(missing, NEIGH - 1 - group, group)
    remote = CELL_DEV + group * HALO_SLOT + within
    return jnp.where(remote_flag, remote, local).astype(jnp.int32)


def set_ends(values, rng, smallest, high):
    index_at = [jax.random.randint(jax.random.fold_in(rng, axis), (), 0, length) for axis, length in enumerate(values.shape)]
    main_axis = values.shape.index(max(values.shape))
    next_to = index_at[:main_axis] + [(index_at[main_axis] + 1) % values.shape[main_axis]] + index_at[main_axis + 1:]
    return values.at[tuple(index_at)].set(smallest).at[tuple(next_to)].set(high)


def shard_levels(key, extent, pieces, least, high):
    factor_of = 1.0
    for dim, parts in pieces:
        draws = jax.random.uniform(jax.random.fold_in(jax.random.fold_in(key, 6), dim), (parts,), jnp.float32, least / len(pieces), high / len(pieces))
        factor_of = factor_of * jnp.repeat(jnp.exp(draws), extent[dim] // parts).reshape((-1,) + (1,) * (len(extent) - 1 - dim))
    return factor_of


def deal_out(key, own, number, rows, amount, top, most, skew):
    sequence = jax.random.permutation(key, amount)
    crowded, common = load_shares(amount, rows * top, most, skew, True), load_shares(amount, rows * top, most, skew, False)
    places = jnp.arange(amount)

    def named(sizes, offset_by):
        used = int((sizes > 0).sum())
        fixed = max(1, used // 4)
        moved = fixed + (places - fixed + offset_by * (used - fixed)) % max(1, amount - fixed)
        return jnp.zeros((amount,), jnp.int32).at[sequence[jnp.where(places < fixed, places, moved)]].set(jnp.asarray(sizes, jnp.int32))

    sizes = jnp.where(number % 4 == 0, named(crowded, number // 4), named(common, number - number // 4 - 1))
    mixed = jax.random.permutation(jax.random.fold_in(own, 3), amount)
    source_of, taker = mixed[0:amount // 2 * 2:2], mixed[1:amount // 2 * 2:2]
    room = jnp.minimum(sizes[source_of] - 1, most - sizes[taker]) // 2
    room = jnp.where((source_of == sequence[0]) | (taker == sequence[0]) | (sizes[taker] == 0), 0, jnp.maximum(room, 0))
    moved = jax.random.randint(jax.random.fold_in(own, 4), (amount // 2,), 0, 1 << 20) % (room + 1)
    sizes = sizes.at[source_of].add(-moved).at[taker].add(moved)
    items = jnp.searchsorted(jnp.cumsum(sizes), jnp.arange(rows * top), side="right").astype(jnp.int32)
    grid = items.reshape(top, rows).T
    grid = grid[jax.random.permutation(jax.random.fold_in(own, 1), rows)]
    offset_by = jax.random.randint(jax.random.fold_in(own, 2), (rows, 1), 0, top)
    return jnp.take_along_axis(grid, (jnp.arange(top)[None, :] + offset_by) % top, axis=1)


def load_shares(amount, total, most, skew, full):
    portions = [(1 << 20) // math.isqrt(grade ** skew) + 1 for grade in range(1, amount + 1)]
    largest = most if full else min(most, max(-(-total // amount), total * portions[0] // sum(portions)))
    least = 1 if total - largest >= amount - 1 else 0
    counts, surplus = [largest] + [least] * (amount - 1), total - largest - least * (amount - 1)
    while surplus > 0:
        candidates = [i for i in range(1, amount) if counts[i] < largest] or [i for i in range(1, amount) if counts[i] < most]
        pool, budget = sum([portions[i] for i in candidates]), surplus
        for i in candidates:
            addition = min(most - counts[i], max(1, budget * portions[i] // pool), surplus)
            counts[i] = counts[i] + addition
            surplus = surplus - addition
    return np.array(counts)


def bell_draw(own_key, extent, spread, most, shards=(), kind=jnp.bfloat16):
    values = jax.random.normal(own_key, extent, jnp.float32) * spread
    if len(shards) > 0:
        values = shard_levels(own_key, extent, shards, -0.22, 0.18) * values
    return jnp.clip(values, min=-most, max=most).astype(kind)


def setup_inputs(seed: int = 0, part: int = 0) -> dict:
    key_list = jax.random.split(jax.random.key(seed), 13)
    part_keys = jax.random.split(jax.random.fold_in(key_list[12], part), 13)
    fluid_state = bell_draw(part_keys[0], (5, NCELL), 1.0, 6.0, ((1, 64),), jnp.float32)
    residual_base = bell_draw(part_keys[1], (5, NCELL), 1.0, 6.0, ((1, 64),), jnp.float32)
    jacobian = bell_draw(part_keys[2], (NB, 5, 5, NCELL), (5 * NB) ** -0.5, 1.0, ((3, 64),))
    columns = draw_columns(jax.random.fold_in(jax.random.fold_in(key_list[12], part), 71), part)
    pseudo_step = jnp.clip(jnp.exp(math.log(1.0) - 2.3025851 * jax.random.uniform(part_keys[4], (NCELL,), jnp.float32) ** shard_levels(part_keys[4], (NCELL,), ((0, 64),), -0.2, 0.2)), 0.1, 1.0)
    send_cells = set_ends(jax.random.randint(part_keys[5], (N_DOM * NEIGH, HALO_SLOT), 0, CELL_DEV), jax.random.fold_in(part_keys[5], 1), 0, CELL_DEV - 1).astype(jnp.int32)
    interface_face_cell = set_ends(jax.random.randint(part_keys[6], (NFACE,), 0, CELL_DEV), jax.random.fold_in(part_keys[6], 1), 0, CELL_DEV - 1).astype(jnp.int32)
    interface_face_area_vector = bell_draw(part_keys[7], (3, NFACE), 1.0, 6.0, ((1, 64),), jnp.float32)
    mortar_weight = jnp.clip(0.5 + 1.0 * jax.random.uniform(part_keys[8], (NFACE,), jnp.float32) ** shard_levels(part_keys[8], (NFACE,), ((0, 64),), -0.2, 0.2), 0.5, 1.5)
    face_route_keys = jax.random.split(jax.random.fold_in(part_keys[9], 1), NFACE // FACE_DEV)
    face_route_turns = jax.random.permutation(jax.random.fold_in(part_keys[9], 3), NFACE // FACE_DEV)
    face_route = jax.vmap(lambda own, number: deal_out(jax.random.fold_in(part_keys[9], 2), own, number, FACE_DEV, N_DOM, 1, CAP, 2))(face_route_keys, face_route_turns).reshape((NFACE, 1))
    face_node = set_ends(jax.random.randint(part_keys[10], (NFACE,), 0, SN), jax.random.fold_in(part_keys[10], 1), 0, SN - 1).astype(jnp.int32)
    compliance = bell_draw(part_keys[11], (NTILES, 3 * TN, 3 * TN), (3 * TN) ** -0.5, 0.3125, ((0, 64),), jnp.float32)
    return dict(fluid_state=fluid_state, residual_base=residual_base, jacobian=jacobian, columns=columns, pseudo_step=pseudo_step, send_cells=send_cells, interface_face_cell=interface_face_cell, interface_face_area_vector=interface_face_area_vector, mortar_weight=mortar_weight, face_route=face_route, face_node=face_node, compliance=compliance)


OFFSETS = (-3, -2, -1, 1, 2, 3)


def reference(fluid_state, residual_base, jacobian, columns, pseudo_step, send_cells, interface_face_cell, interface_face_area_vector, mortar_weight, face_route, face_node, compliance):
    group_offsets = jnp.array(np.array(OFFSETS, dtype=np.int32))
    device = (jnp.arange(NCELL, dtype=jnp.int32) // CELL_DEV)[None, :]
    inside = columns < CELL_DEV
    slot = jnp.maximum(columns - CELL_DEV, 0).astype(jnp.int32)
    group = (slot // HALO_SLOT).astype(jnp.int32)
    within = (slot % HALO_SLOT).astype(jnp.int32)
    source = jnp.clip(device + group_offsets[group], 0, N_DOM - 1).astype(jnp.int32)
    row = (source * NEIGH + (NEIGH - 1 - group)).astype(jnp.int32)
    remote = source * CELL_DEV + send_cells[row, within]
    index = jnp.where(inside, device * CELL_DEV + columns, remote).astype(jnp.int32)
    selected_entries = fluid_state[:, index]
    coupled_system = jnp.einsum("idlu,liu->du", jacobian.astype(jnp.float32), selected_entries, precision=lax.Precision.HIGHEST)
    residual = residual_base - coupled_system
    face_owner = jnp.arange(NFACE, dtype=jnp.int32) // FACE_DEV
    cell = (face_owner * CELL_DEV + interface_face_cell).astype(jnp.int32)
    face_state = fluid_state[:, cell] + pseudo_step[cell][None, :] * residual[:, cell]
    pressure = 0.4 * (face_state[4] - 0.8 * face_state[1] + 0.32 * face_state[0])
    load = (mortar_weight * pressure)[None, :] * interface_face_area_vector
    node = (face_route[:, 0] * SN + face_node).astype(jnp.int32)
    node_load = jnp.zeros((3, NNODE), jnp.float32).at[:, node].add(load)
    tiles = node_load.reshape(3, NTILES, TN).transpose(1, 0, 2).reshape(NTILES, 3 * TN)
    moved = jnp.einsum("tij,tj->ti", compliance, tiles, precision=lax.Precision.HIGHEST)
    displacement = moved.reshape(NTILES, 3, TN).transpose(1, 0, 2).reshape(3, NNODE)
    face_motion = mortar_weight[None, :] * displacement[:, node]
    return residual, displacement, face_motion
```

```python
import functools

import jax
import jax.numpy as jnp
from jax import lax
from jax.experimental import pallas as pl
from jax.experimental.pallas import tpu as pltpu
from jax.sharding import PartitionSpec as P

MESH = pl.DeviceIdType.MESH
OFFSETS = (-3, -2, -1, 1, 2, 3)
HIGH = lax.Precision.HIGHEST
F32 = jnp.float32
BF16 = jnp.bfloat16
I32 = jnp.int32
LANES = 128


def pick(row, where_at):
    return jnp.take_along_axis(
        jnp.broadcast_to(row, where_at.shape), where_at, axis=1, mode="promise_in_bounds"
    )


def iota(shape, dim):
    return lax.broadcasted_iota(I32, shape, dim)


def lanes(block):
    return pl.ds(pl.multiple_of(block * LANES, LANES), LANES)


def three_parts(value):
    high = value.astype(BF16)
    rest = value - high.astype(F32)
    middle = rest.astype(BF16)
    low = (rest - middle.astype(F32)).astype(BF16)
    return high, middle, low


def dot_nt(a, b, precision=None):
    return lax.dot_general(
        a, b, (((1,), (1,)), ((), ())), precision=precision, preferred_element_type=F32
    )


def gather_sends(fluid, send, index, out):
    index[0:6, :] = send[...]
    index[6:8, :] = jnp.zeros((2, index.shape[1]), I32)
    cells = [index[:, k * LANES : (k + 1) * LANES] for k in range(4)]
    low = [cell & (LANES - 1) for cell in cells]
    high = [cell >> 7 for cell in cells]

    def step(block, total):
        total = list(total)
        hit = [h == block for h in high]
        for c in range(5):
            row = fluid[pl.ds(c, 1), lanes(block)]
            for k in range(4):
                total[c * 4 + k] = jnp.where(hit[k], pick(row, low[k]), total[c * 4 + k])
        return tuple(total)

    total = lax.fori_loop(
        0, 128, step, tuple(jnp.zeros((8, LANES), F32) for _ in range(20)), unroll=4
    )
    for slot in range(20):
        out[pl.ds(slot, 8, stride=24), :] = total[slot]


def shift_table(fluid, table):
    left = iota((5, LANES), 1) < 64

    def step(block, before):
        here = pltpu.roll(fluid[:, lanes(block)], 64, 1)
        table[block, 0:5, :] = jnp.where(left, before, here)
        return here

    last = lax.fori_loop(0, 128, step, jnp.zeros((5, LANES), F32), unroll=4)
    table[128, 0:5, :] = last


def rank_faces(me, peers, route, relative, onehot, prefix, rank):
    relative[...] = (route[...] - me) & (peers - 1)
    line = iota((peers, LANES), 0)
    for i in range(32):
        hit = jnp.broadcast_to(relative[i : i + 1, :], (peers, LANES)) == line
        onehot[i * peers : (i + 1) * peers, :] = jnp.where(hit, 1.0, 0.0).astype(BF16)
    upto = jnp.where(iota((LANES, LANES), 0) <= iota((LANES, LANES), 1), 1.0, 0.0)
    weights = jnp.concatenate([upto, jnp.ones((LANES, LANES), F32)], axis=1).astype(BF16)

    def count(part, carry):
        rows = pl.ds(pl.multiple_of(part * 512, 512), 512)
        prefix[rows, :] = jnp.dot(onehot[rows, :], weights, preferred_element_type=F32)
        return carry

    lax.fori_loop(0, 32 * peers // 512, count, 0)

    def step(i, before):
        rows = pl.ds(pl.multiple_of(i * peers, peers), peers)
        hit = onehot[rows, :].astype(F32)
        here = prefix[rows, 0:LANES] + before
        rank[pl.ds(i, 1), :] = jnp.sum(hit * here, axis=0, keepdims=True) - 1.0
        return before + prefix[rows, LANES : 2 * LANES]

    lax.fori_loop(0, 32, step, jnp.zeros((peers, LANES), F32), unroll=2)


def compact_faces(peers, onehot, rank, fcell, fnode, weight, area, cell_at, slab, scale_at):
    line = iota((LANES, LANES), 0).astype(F32)
    lane = iota((peers, LANES), 1).astype(F32)

    def step(pair, total):
        left, right = [], []
        for half in range(2):
            i = pair * 2 + half
            hit = onehot[pl.ds(pl.multiple_of(i * peers, peers), peers), :].astype(F32)
            left.append(
                jnp.concatenate(
                    [hit * (i + 1).astype(F32), hit * lane], axis=0
                ).astype(BF16)
            )
            place = jnp.broadcast_to(rank[pl.ds(i, 1), :], (LANES, LANES)) == line
            right.append(jnp.where(place, 1.0, 0.0).astype(BF16))
        return total + dot_nt(jnp.concatenate(left, axis=1), jnp.concatenate(right, axis=1))

    found = lax.fori_loop(0, 16, step, jnp.zeros((2 * peers, LANES), F32))
    high = found[0:peers, :].astype(I32) - 1
    low = found[peers : 2 * peers, :].astype(I32)
    groups = peers // 8
    for g in range(groups):
        h = high[g * 8 : g * 8 + 8, :]
        l = low[g * 8 : g * 8 + 8, :]

        def look(i, total, h=h, l=l):
            hit = h == i
            rows = (
                fcell[pl.ds(i, 1), :],
                fnode[pl.ds(i, 1), :],
                weight[pl.ds(i, 1), :] * area[0:1, lanes(i)],
                weight[pl.ds(i, 1), :] * area[1:2, lanes(i)],
                weight[pl.ds(i, 1), :] * area[2:3, lanes(i)],
            )
            return tuple(jnp.where(hit, pick(row, l), old) for row, old in zip(rows, total))

        none_i = jnp.zeros((8, LANES), I32)
        none_f = jnp.zeros((8, LANES), F32)
        cell, node, *scales = lax.fori_loop(
            0, 32, look, (none_i, none_i, none_f, none_f, none_f), unroll=8
        )
        cell_at[g * 8 : g * 8 + 8, :] = cell
        slab[g * 8 : g * 8 + 8, 3, :] = node.astype(F32)
        for c in range(3):
            scale_at[c, g * 8 : g * 8 + 8, :] = scales[c]


def halo_table(arrived, table):
    line, lane = iota((8, LANES), 0), iota((8, LANES), 1)
    where_at = line * 16 + (lane & 15)
    for c in range(5):
        for quarter in range(4):
            total = jnp.zeros((8, LANES), F32)
            for n in range(6):
                got = pick(arrived[n, c * 4 + quarter : c * 4 + quarter + 1, :], where_at)
                total = jnp.where((lane >> 4) == n, got, total)
            table[c, quarter * 8 : quarter * 8 + 8, :] = total


def apply_system(fluid, base, jac, cols, dt, table, halo, sums, residual, state):
    cells = fluid.shape[1]

    def step(q, carry):
        where_at, chunk = [], []
        for j in range(4):
            col = cols[:, lanes(q * 4 + j)]
            shifted = col + 64 - q * 512
            far = col - cells
            far_at = (far >> 9) * 16 + (far & 511) - q * 16
            inside = col < cells
            where_at.append(jnp.where(inside, shifted, far_at) & (LANES - 1))
            chunk.append(jnp.where(inside, shifted >> 7, 5))
        picked = [[None] * 5 for _ in range(4)]
        for c in range(5):
            rows = [table[q * 4 + k, c : c + 1, :] for k in range(5)]
            rows.append(halo[c, pl.ds(q, 1), :])
            for j in range(4):
                total = pick(rows[0], where_at[j])
                for k in range(1, 6):
                    total = jnp.where(chunk[j] == k, pick(rows[k], where_at[j]), total)
                picked[j][c] = total
        for j in range(4):
            at = lanes(q * 4 + j)
            for r in range(5):
                total = jac[r, 0, :, at].astype(F32) * picked[j][0]
                for c in range(1, 5):
                    total = total + jac[r, c, :, at].astype(F32) * picked[j][c]
                sums[j, r * 8 : r * 8 + 7, :] = total
            coupled = sums[j, pl.ds(0, 5, stride=8), :]
            for b in range(1, 7):
                coupled = coupled + sums[j, pl.ds(b, 5, stride=8), :]
            left = base[:, at] - coupled
            residual[:, at] = left
            block = q * 4 + j
            state[pl.ds(pl.multiple_of(block * 8, 8), 5), :] = (
                fluid[:, at] + dt[pl.ds(block, 1), :] * left
            )
        return carry

    lax.fori_loop(0, cells // 512, step, 0)


def cell_pressures(state, pressure):
    def step(i, carry):
        first = pl.multiple_of(i * 64, 64)
        p0, p1, p4 = (state[pl.ds(first + r, 8, stride=8), :] for r in (0, 1, 4))
        pressure[pl.ds(pl.multiple_of(i * 8, 8), 8), :] = 0.4 * (p4 - 0.8 * p1 + 0.32 * p0)
        return carry

    lax.fori_loop(0, 16, step, 0, unroll=4)


def face_loads(peers, pressure, cell_at, scale_at, slab):
    groups = peers // 8
    cells = [cell_at[g * 8 : g * 8 + 8, :] for g in range(groups)]
    low = [cell & (LANES - 1) for cell in cells]
    high = [cell >> 7 for cell in cells]

    def step(i, total):
        row = pressure[pl.ds(i, 1), :]
        return tuple(jnp.where(high[g] == i, pick(row, low[g]), total[g]) for g in range(groups))

    found = lax.fori_loop(
        0, 128, step, tuple(jnp.zeros((8, LANES), F32) for _ in range(groups)), unroll=4
    )
    for g in range(groups):
        for c in range(3):
            slab[g * 8 : g * 8 + 8, c, :] = scale_at[c, g * 8 : g * 8 + 8, :] * found[g]


def node_sums(peers, got):
    line = iota((LANES, LANES), 0)
    above = iota((8, LANES), 0) >> 2
    width = 8

    def step(part, total):
        left, right = [], []
        for s in range(width):
            piece = got[part * width + s]
            node = piece[3:4, :].astype(I32)
            twice = jnp.concatenate([piece, piece], axis=0)
            high = jnp.broadcast_to(node >> 7, (8, LANES))
            spread = jnp.concatenate(
                [jnp.where(high == above, twice, 0.0), jnp.where(high == above + 2, twice, 0.0)],
                axis=0,
            )
            left.append(jnp.concatenate(three_parts(spread), axis=0))
            hit = jnp.broadcast_to(node & (LANES - 1), (LANES, LANES)) == line
            right.append(jnp.where(hit, 1.0, 0.0).astype(BF16))
        return total + dot_nt(jnp.concatenate(left, axis=1), jnp.concatenate(right, axis=1))

    total = lax.fori_loop(0, peers // width, step, jnp.zeros((48, LANES), F32))
    return total[0:16, :] + total[16:32, :] + total[32:48, :]


def tile_response(sums, compliance, moved, displacement):
    for t in range(4):
        load = jnp.concatenate([sums[t * 4 + c : t * 4 + c + 1, :] for c in range(3)], axis=1)
        out = dot_nt(jnp.broadcast_to(load, (8, load.shape[1])), compliance[t], HIGH)
        for c in range(3):
            row = out[0:1, c * LANES : (c + 1) * LANES]
            moved[c * 4 + t : c * 4 + t + 1, :] = row
            displacement[c : c + 1, t * LANES : (t + 1) * LANES] = row


def make_replies(peers, got, moved, reply):
    def step(g, carry):
        rows = pl.ds(pl.multiple_of(g * 8, 8), 8)
        node = got[rows, 3, :].astype(I32)
        low, high = node & (LANES - 1), node >> 7
        for c in range(3):
            total = pick(moved[c * 4 : c * 4 + 1, :], low)
            for t in range(1, 4):
                total = jnp.where(high == t, pick(moved[c * 4 + t : c * 4 + t + 1, :], low), total)
            reply[rows, c, :] = total
        return carry

    lax.fori_loop(0, peers // 8, step, 0)


def face_motions(peers, answer, relative, rank, weight, motion):
    slot = [rank[g * 8 : g * 8 + 8, :].astype(I32) for g in range(4)]
    peer = [relative[g * 8 : g * 8 + 8, :] for g in range(4)]

    def step(r, total):
        total = list(total)
        for c in range(3):
            row = answer[r, c : c + 1, :]
            for g in range(4):
                total[c * 4 + g] = jnp.where(peer[g] == r, pick(row, slot[g]), total[c * 4 + g])
        return tuple(total)

    total = lax.fori_loop(
        0, peers, step, tuple(jnp.zeros((8, LANES), F32) for _ in range(12)), unroll=4
    )
    for c in range(3):
        for g in range(4):
            out = total[c * 4 + g] * weight[g * 8 : g * 8 + 8, :]
            for s in range(8):
                at = (g * 8 + s) * LANES
                motion[c : c + 1, at : at + LANES] = out[s : s + 1, :]


INPUTS = ("fluid", "base", "jac", "cols", "dt", "send", "fcell", "area", "weight", "route", "fnode", "comp")


def kernel(peers, *refs):
    count = len(INPUTS)
    hbm = dict(zip(INPUTS, refs[:count]))
    residual_out, displacement, motion = refs[count : count + 3]
    refs = refs[count + 3 :]
    v = dict(zip(INPUTS, refs[:count]))
    (
        index, sends, arrived, table, halo, relative, onehot, prefix, rank, cell_at, scale_at,
        slab, got, sums, residual, state, pressure, moved, reply, answer,
        in_sems, out_sem, halo_send, halo_recv, load_send, load_recv, back_send, back_recv,
    ) = refs[count:]
    me = lax.axis_index("dom")
    copies = {
        name: pltpu.make_async_copy(hbm[name], v[name], in_sems.at[i])
        for i, name in enumerate(INPUTS)
    }
    for name in ("fluid", "send", "route", "fcell", "fnode", "weight", "area", "cols", "jac", "base", "dt", "comp"):
        copies[name].start()
    barrier = pltpu.get_barrier_semaphore()

    def greet(r, carry):
        pl.semaphore_signal(
            barrier, inc=1, device_id={"dom": (me + r) & (peers - 1)}, device_id_type=MESH
        )
        return carry

    lax.fori_loop(1, peers, greet, 0)
    copies["send"].wait()
    copies["fluid"].wait()
    gather_sends(v["fluid"], v["send"], index, sends)
    pl.semaphore_wait(barrier, peers - 1)

    halo_copies = []
    for m in range(6):
        copy = pltpu.make_async_remote_copy(
            src_ref=sends.at[pl.ds(24 * m, 24)],
            dst_ref=arrived.at[5 - m],
            send_sem=halo_send.at[m],
            recv_sem=halo_recv.at[5 - m],
            device_id={"dom": (me + OFFSETS[m] + peers) & (peers - 1)},
            device_id_type=MESH,
        )
        copy.start()
        halo_copies.append(copy)

    shift_table(v["fluid"], table)
    copies["route"].wait()
    rank_faces(me, peers, v["route"], relative, onehot, prefix, rank)
    for name in ("fcell", "fnode", "weight", "area"):
        copies[name].wait()
    compact_faces(
        peers, onehot, rank, v["fcell"], v["fnode"], v["weight"], v["area"], cell_at, slab, scale_at
    )
    for copy in halo_copies:
        copy.wait()
    halo_table(arrived, halo)
    for name in ("cols", "jac", "base", "dt"):
        copies[name].wait()
    apply_system(
        v["fluid"], v["base"], v["jac"], v["cols"], v["dt"], table, halo, sums, residual, state
    )
    residual_copy = pltpu.make_async_copy(residual, residual_out, out_sem)
    residual_copy.start()
    cell_pressures(state, pressure)
    face_loads(peers, pressure, cell_at, scale_at, slab)

    def exchange(source, target, send_sem, recv_sem, sign):
        def one(r):
            return pltpu.make_async_remote_copy(
                src_ref=source.at[r],
                dst_ref=target.at[r],
                send_sem=send_sem,
                recv_sem=recv_sem,
                device_id={"dom": (me + sign * r + peers) & (peers - 1)},
                device_id_type=MESH,
            )

        def start(r, carry):
            one(r).start()
            return carry

        lax.fori_loop(1, peers, start, 0)
        target[0] = source[0]
        return pltpu.make_async_remote_copy(
            src_ref=source.at[pl.ds(1, peers - 1)],
            dst_ref=target.at[pl.ds(1, peers - 1)],
            send_sem=send_sem,
            recv_sem=recv_sem,
            device_id={"dom": (me + 1) & (peers - 1)},
            device_id_type=MESH,
        )

    forth = exchange(slab, got, load_send, load_recv, 1)
    copies["comp"].wait()
    forth.wait()
    tile_response(node_sums(peers, got), v["comp"], moved, displacement)
    make_replies(peers, got, moved, reply)
    back = exchange(reply, answer, back_send, back_recv, -1)
    back.wait()
    face_motions(peers, answer, relative, rank, v["weight"], motion)
    residual_copy.wait()


def per_device(
    fluid_state,
    residual_base,
    jacobian,
    columns,
    pseudo_step,
    send_cells,
    interface_face_cell,
    interface_face_area_vector,
    mortar_weight,
    face_route,
    face_node,
    compliance,
):
    peers = lax.axis_size("dom")
    operands = (
        fluid_state,
        residual_base,
        jnp.transpose(jacobian, (1, 2, 0, 3)),
        columns,
        pseudo_step.reshape(-1, LANES),
        send_cells,
        interface_face_cell.reshape(-1, LANES),
        interface_face_area_vector,
        mortar_weight.reshape(-1, LANES),
        face_route.reshape(-1, LANES),
        face_node.reshape(-1, LANES),
        compliance,
    )
    vmem = pltpu.VMEM
    dma = pltpu.SemaphoreType.DMA
    scratch = [vmem(x.shape, x.dtype) for x in operands] + [
        vmem((8, 512), I32),
        vmem((192, LANES), F32),
        vmem((6, 24, LANES), F32),
        vmem((129, 8, LANES), F32),
        vmem((5, 32, LANES), F32),
        vmem((32, LANES), I32),
        vmem((32 * peers, LANES), BF16),
        vmem((32 * peers, 2 * LANES), F32),
        vmem((32, LANES), F32),
        vmem((peers, LANES), I32),
        vmem((3, peers, LANES), F32),
        vmem((peers, 4, LANES), F32),
        vmem((peers, 4, LANES), F32),
        vmem((4, 40, LANES), F32),
        vmem(fluid_state.shape, F32),
        vmem((1024, LANES), F32),
        vmem((LANES, LANES), F32),
        vmem((16, LANES), F32),
        vmem((peers, 4, LANES), F32),
        vmem((peers, 4, LANES), F32),
        dma((len(INPUTS),)),
        dma,
        dma((6,)),
        dma((6,)),
        dma,
        dma,
        dma,
        dma,
    ]
    return pl.pallas_call(
        functools.partial(kernel, peers),
        out_shape=(
            jax.ShapeDtypeStruct(fluid_state.shape, F32),
            jax.ShapeDtypeStruct((3, compliance.shape[0] * LANES), F32),
            jax.ShapeDtypeStruct(interface_face_area_vector.shape, F32),
        ),
        in_specs=[pl.BlockSpec(memory_space=pl.ANY)] * len(operands),
        out_specs=(
            pl.BlockSpec(memory_space=pl.ANY),
            pl.BlockSpec(memory_space=vmem),
            pl.BlockSpec(memory_space=vmem),
        ),
        scratch_shapes=scratch,
        compiler_params=pltpu.CompilerParams(
            collective_id=0, has_side_effects=True, vmem_limit_bytes=56 * 1024 * 1024
        ),
    )(*operands)


def solution(mesh):
    return jax.shard_map(
        per_device,
        mesh=mesh,
        in_specs=(
            P(None, ("sweep", "dom")),
            P(None, ("sweep", "dom")),
            P(None, None, None, ("sweep", "dom")),
            P(None, ("sweep", "dom")),
            P(("sweep", "dom")),
            P(("sweep", "dom"), None),
            P(("sweep", "dom")),
            P(None, ("sweep", "dom")),
            P(("sweep", "dom")),
            P(("sweep", "dom"), None),
            P(("sweep", "dom")),
            P(("sweep", "dom"), None, None),
        ),
        out_specs=(P(None, ("sweep", "dom")), P(None, ("sweep", "dom")), P(None, ("sweep", "dom"))),
        check_vma=False,
    )
```

```python
import functools

import jax
import jax.numpy as jnp
from jax import lax
from jax.experimental import pallas as pl
from jax.experimental.pallas import tpu as pltpu
from jax.sharding import PartitionSpec as P

MESH = pl.DeviceIdType.MESH
OFFSETS = (-3, -2, -1, 1, 2, 3)
HIGH = lax.Precision.HIGHEST
F32 = jnp.float32
BF16 = jnp.bfloat16
I32 = jnp.int32
LANES = 128


def pick(row, where_at):
    return jnp.take_along_axis(
        jnp.broadcast_to(row, where_at.shape), where_at, axis=1, mode="promise_in_bounds"
    )


def iota(shape, dim):
    return lax.broadcasted_iota(I32, shape, dim)


def lanes(block):
    return pl.ds(pl.multiple_of(block * LANES, LANES), LANES)


def three_parts(value):
    high = value.astype(BF16)
    rest = value - high.astype(F32)
    middle = rest.astype(BF16)
    low = (rest - middle.astype(F32)).astype(BF16)
    return high, middle, low


def dot_nt(a, b, precision=None):
    return lax.dot_general(
        a, b, (((1,), (1,)), ((), ())), precision=precision, preferred_element_type=F32
    )


def gather_sends(fluid, send, index, found, out):
    for k in range(4):
        index[pl.ds(k, 6, stride=4), :] = send[:, k * LANES : (k + 1) * LANES]

    def part(g, carry):
        rows = pl.ds(pl.multiple_of(g * 8, 8), 8)
        cell = index[rows, :]
        low, high = cell & (LANES - 1), cell >> 7

        def step(block, total):
            hit = high == block
            return tuple(
                jnp.where(hit, pick(fluid[pl.ds(c, 1), lanes(block)], low), total[c])
                for c in range(5)
            )

        total = lax.fori_loop(0, 128, step, (jnp.zeros((8, LANES), F32),) * 5, unroll=128)
        for c in range(5):
            found[c, rows, :] = total[c]
        return carry

    lax.fori_loop(0, 3, part, 0)
    for m in range(6):
        for c in range(5):
            out[m * 24 + c * 4 : m * 24 + c * 4 + 4, :] = found[c, m * 4 : m * 4 + 4, :]


def shift_table(fluid, table):
    left = iota((5, LANES), 1) < 64

    def step(block, before):
        here = pltpu.roll(fluid[:, lanes(block)], 64, 1)
        table[block, 0:5, :] = jnp.where(left, before, here)
        return here

    last = lax.fori_loop(0, 128, step, jnp.zeros((5, LANES), F32), unroll=32)
    table[128, 0:5, :] = last


def rank_faces(me, peers, route, relative, onehot, prefix, rank):
    relative[...] = (route[...] - me) & (peers - 1)
    line = iota((peers, LANES), 0)
    for i in range(32):
        hit = jnp.broadcast_to(relative[i : i + 1, :], (peers, LANES)) == line
        onehot[i * peers : (i + 1) * peers, :] = jnp.where(hit, 1.0, 0.0).astype(BF16)
    upto = jnp.where(iota((LANES, LANES), 0) <= iota((LANES, LANES), 1), 1.0, 0.0)
    weights = jnp.concatenate([upto, jnp.ones((LANES, LANES), F32)], axis=1).astype(BF16)

    def count(part, carry):
        rows = pl.ds(pl.multiple_of(part * 512, 512), 512)
        prefix[rows, :] = jnp.dot(onehot[rows, :], weights, preferred_element_type=F32)
        return carry

    lax.fori_loop(0, 32 * peers // 512, count, 0)

    def step(i, before):
        rows = pl.ds(pl.multiple_of(i * peers, peers), peers)
        hit = onehot[rows, :].astype(F32)
        here = prefix[rows, 0:LANES] + before
        rank[pl.ds(i, 1), :] = jnp.sum(hit * here, axis=0, keepdims=True) - 1.0
        return before + prefix[rows, LANES : 2 * LANES]

    lax.fori_loop(0, 32, step, jnp.zeros((peers, LANES), F32), unroll=2)


def compact_faces(peers, onehot, rank, fcell, fnode, weight, area, face_at, cell_at, slab, scale_at):
    line = iota((LANES, LANES), 0).astype(F32)
    lane = iota((peers, LANES), 1).astype(F32)

    def step(pair, total):
        left, right = [], []
        for half in range(2):
            i = pair * 2 + half
            hit = onehot[pl.ds(pl.multiple_of(i * peers, peers), peers), :].astype(F32)
            left.append(
                jnp.concatenate(
                    [hit * (i + 1).astype(F32), hit * lane], axis=0
                ).astype(BF16)
            )
            place = jnp.broadcast_to(rank[pl.ds(i, 1), :], (LANES, LANES)) == line
            right.append(jnp.where(place, 1.0, 0.0).astype(BF16))
        return total + dot_nt(jnp.concatenate(left, axis=1), jnp.concatenate(right, axis=1))

    found = lax.fori_loop(0, 16, step, jnp.zeros((2 * peers, LANES), F32))
    high = found[0:peers, :].astype(I32) - 1
    low = found[peers : 2 * peers, :].astype(I32)
    face_at[...] = (high << 7) + low

    def part(g, carry):
        rows = pl.ds(pl.multiple_of(g * 8, 8), 8)
        face = face_at[rows, :]
        h, l = face >> 7, face & (LANES - 1)

        def look(i, total):
            hit = h == i
            pieces = (
                fcell[pl.ds(i, 1), :],
                fnode[pl.ds(i, 1), :],
                weight[pl.ds(i, 1), :] * area[0:1, lanes(i)],
                weight[pl.ds(i, 1), :] * area[1:2, lanes(i)],
                weight[pl.ds(i, 1), :] * area[2:3, lanes(i)],
            )
            return tuple(jnp.where(hit, pick(row, l), old) for row, old in zip(pieces, total))

        none_i = jnp.zeros((8, LANES), I32)
        none_f = jnp.zeros((8, LANES), F32)
        cell, node, *scales = lax.fori_loop(
            0, 32, look, (none_i, none_i, none_f, none_f, none_f), unroll=32
        )
        cell_at[rows, :] = cell
        slab[rows, 3, :] = node.astype(F32)
        for c in range(3):
            scale_at[c, rows, :] = scales[c]
        return carry

    lax.fori_loop(0, peers // 8, part, 0)


def halo_table(arrived, table):
    line, lane = iota((8, LANES), 0), iota((8, LANES), 1)
    where_at = line * 16 + (lane & 15)
    for c in range(5):
        for quarter in range(4):
            total = jnp.zeros((8, LANES), F32)
            for n in range(6):
                got = pick(arrived[n, c * 4 + quarter : c * 4 + quarter + 1, :], where_at)
                total = jnp.where((lane >> 4) == n, got, total)
            table[c, quarter * 8 : quarter * 8 + 8, :] = total


def apply_system(fluid, base, jac, cols, dt, table, halo, sums, residual, state):
    cells = fluid.shape[1]

    def step(q, carry):
        where_at, chunk = [], []
        for j in range(4):
            col = cols[:, lanes(q * 4 + j)]
            shifted = col + 64 - q * 512
            far = col - cells
            far_at = (far >> 9) * 16 + (far & 511) - q * 16
            inside = col < cells
            where_at.append(jnp.where(inside, shifted, far_at) & (LANES - 1))
            chunk.append(jnp.where(inside, shifted >> 7, 5))
        for j in range(4):
            picked = []
            for c in range(5):
                total = pick(table[q * 4, c : c + 1, :], where_at[j])
                for k in range(1, 5):
                    got = pick(table[q * 4 + k, c : c + 1, :], where_at[j])
                    total = jnp.where(chunk[j] == k, got, total)
                got = pick(halo[c, pl.ds(q, 1), :], where_at[j])
                picked.append(jnp.where(chunk[j] == 5, got, total))
            at = lanes(q * 4 + j)
            for r in range(5):
                total = jac[r, 0, :, at].astype(F32) * picked[0]
                for c in range(1, 5):
                    total = total + jac[r, c, :, at].astype(F32) * picked[c]
                sums[j, r * 8 : r * 8 + 7, :] = total
            coupled = sums[j, pl.ds(0, 5, stride=8), :]
            for b in range(1, 7):
                coupled = coupled + sums[j, pl.ds(b, 5, stride=8), :]
            left = base[:, at] - coupled
            residual[:, at] = left
            block = q * 4 + j
            state[pl.ds(pl.multiple_of(block * 8, 8), 5), :] = (
                fluid[:, at] + dt[pl.ds(block, 1), :] * left
            )
        return carry

    lax.fori_loop(0, cells // 512, step, 0)


def cell_pressures(state, pressure):
    def step(i, carry):
        first = pl.multiple_of(i * 64, 64)
        p0, p1, p4 = (state[pl.ds(first + r, 8, stride=8), :] for r in (0, 1, 4))
        pressure[pl.ds(pl.multiple_of(i * 8, 8), 8), :] = 0.4 * (p4 - 0.8 * p1 + 0.32 * p0)
        return carry

    lax.fori_loop(0, 16, step, 0, unroll=4)


def face_loads(peers, pressure, cell_at, scale_at, slab):
    def part(g, carry):
        rows = pl.ds(pl.multiple_of(g * 8, 8), 8)
        cell = cell_at[rows, :]
        low, high = cell & (LANES - 1), cell >> 7

        def step(i, total):
            return jnp.where(high == i, pick(pressure[pl.ds(i, 1), :], low), total)

        found = lax.fori_loop(0, 128, step, jnp.zeros((8, LANES), F32), unroll=128)
        for c in range(3):
            slab[rows, c, :] = scale_at[c, rows, :] * found
        return carry

    lax.fori_loop(0, peers // 8, part, 0)


def node_sums(peers, got):
    line = iota((LANES, LANES), 0)
    above = iota((8, LANES), 0) >> 2
    width = 8

    def step(part, total):
        left, right = [], []
        for s in range(width):
            piece = got[part * width + s]
            node = piece[3:4, :].astype(I32)
            twice = jnp.concatenate([piece, piece], axis=0)
            high = jnp.broadcast_to(node >> 7, (8, LANES))
            spread = jnp.concatenate(
                [jnp.where(high == above, twice, 0.0), jnp.where(high == above + 2, twice, 0.0)],
                axis=0,
            )
            left.append(jnp.concatenate(three_parts(spread), axis=0))
            hit = jnp.broadcast_to(node & (LANES - 1), (LANES, LANES)) == line
            right.append(jnp.where(hit, 1.0, 0.0).astype(BF16))
        return total + dot_nt(jnp.concatenate(left, axis=1), jnp.concatenate(right, axis=1))

    total = lax.fori_loop(0, peers // width, step, jnp.zeros((48, LANES), F32))
    return total[0:16, :] + total[16:32, :] + total[32:48, :]


def tile_response(sums, compliance, moved, displacement):
    for t in range(4):
        load = jnp.concatenate([sums[t * 4 + c : t * 4 + c + 1, :] for c in range(3)], axis=1)
        out = dot_nt(jnp.broadcast_to(load, (8, load.shape[1])), compliance[t], HIGH)
        for c in range(3):
            row = out[0:1, c * LANES : (c + 1) * LANES]
            moved[c * 4 + t : c * 4 + t + 1, :] = row
            displacement[c : c + 1, t * LANES : (t + 1) * LANES] = row


def make_replies(peers, got, moved, reply):
    def step(g, carry):
        rows = pl.ds(pl.multiple_of(g * 8, 8), 8)
        node = got[rows, 3, :].astype(I32)
        low, high = node & (LANES - 1), node >> 7
        for c in range(3):
            total = pick(moved[c * 4 : c * 4 + 1, :], low)
            for t in range(1, 4):
                total = jnp.where(high == t, pick(moved[c * 4 + t : c * 4 + t + 1, :], low), total)
            reply[rows, c, :] = total
        return carry

    lax.fori_loop(0, peers // 8, step, 0)


def face_motions(peers, answer, relative, rank, weight, motion):
    for g in range(4):
        rows = slice(g * 8, g * 8 + 8)
        slot, peer = rank[rows, :].astype(I32), relative[rows, :]

        def step(r, total, slot=slot, peer=peer):
            hit = peer == r
            return tuple(
                jnp.where(hit, pick(answer[r, c : c + 1, :], slot), total[c]) for c in range(3)
            )

        total = lax.fori_loop(0, peers, step, (jnp.zeros((8, LANES), F32),) * 3, unroll=peers)
        for c in range(3):
            out = total[c] * weight[rows, :]
            for s in range(8):
                at = (g * 8 + s) * LANES
                motion[c : c + 1, at : at + LANES] = out[s : s + 1, :]


INPUTS = ("fluid", "base", "jac", "cols", "dt", "send", "fcell", "area", "weight", "route", "fnode", "comp")


def kernel(peers, *refs):
    count = len(INPUTS)
    hbm = dict(zip(INPUTS, refs[:count]))
    residual_out, displacement, motion = refs[count : count + 3]
    refs = refs[count + 3 :]
    v = dict(zip(INPUTS, refs[:count]))
    (
        index, found, sends, arrived, table, halo, relative, onehot, prefix, rank, face_at, cell_at, scale_at,
        slab, got, sums, residual, state, pressure, moved, reply, answer,
        in_sems, out_sem, halo_send, halo_recv, load_send, load_recv, back_send, back_recv,
    ) = refs[count:]
    me = lax.axis_index("dom")
    copies = {
        name: pltpu.make_async_copy(hbm[name], v[name], in_sems.at[i])
        for i, name in enumerate(INPUTS)
    }
    for name in ("fluid", "send", "route", "fcell", "fnode", "weight", "area", "cols", "jac", "base", "dt", "comp"):
        copies[name].start()
    barrier = pltpu.get_barrier_semaphore()

    def greet(r, carry):
        pl.semaphore_signal(
            barrier, inc=1, device_id={"dom": (me + r) & (peers - 1)}, device_id_type=MESH
        )
        return carry

    lax.fori_loop(1, peers, greet, 0)
    copies["send"].wait()
    copies["fluid"].wait()
    gather_sends(v["fluid"], v["send"], index, found, sends)
    pl.semaphore_wait(barrier, peers - 1)

    halo_copies = []
    for m in range(6):
        copy = pltpu.make_async_remote_copy(
            src_ref=sends.at[pl.ds(24 * m, 24)],
            dst_ref=arrived.at[5 - m],
            send_sem=halo_send.at[m],
            recv_sem=halo_recv.at[5 - m],
            device_id={"dom": (me + OFFSETS[m] + peers) & (peers - 1)},
            device_id_type=MESH,
        )
        copy.start()
        halo_copies.append(copy)

    shift_table(v["fluid"], table)
    copies["route"].wait()
    rank_faces(me, peers, v["route"], relative, onehot, prefix, rank)
    for name in ("fcell", "fnode", "weight", "area"):
        copies[name].wait()
    compact_faces(
        peers, onehot, rank, v["fcell"], v["fnode"], v["weight"], v["area"],
        face_at, cell_at, slab, scale_at,
    )
    for copy in halo_copies:
        copy.wait()
    halo_table(arrived, halo)
    for name in ("cols", "jac", "base", "dt"):
        copies[name].wait()
    apply_system(
        v["fluid"], v["base"], v["jac"], v["cols"], v["dt"], table, halo, sums, residual, state
    )
    residual_copy = pltpu.make_async_copy(residual, residual_out, out_sem)
    residual_copy.start()
    cell_pressures(state, pressure)
    face_loads(peers, pressure, cell_at, scale_at, slab)

    def exchange(source, target, send_sem, recv_sem, sign):
        def one(r):
            return pltpu.make_async_remote_copy(
                src_ref=source.at[r],
                dst_ref=target.at[r],
                send_sem=send_sem,
                recv_sem=recv_sem,
                device_id={"dom": (me + sign * r + peers) & (peers - 1)},
                device_id_type=MESH,
            )

        def start(r, carry):
            one(r).start()
            return carry

        lax.fori_loop(1, peers, start, 0)
        target[0] = source[0]
        return pltpu.make_async_remote_copy(
            src_ref=source.at[pl.ds(1, peers - 1)],
            dst_ref=target.at[pl.ds(1, peers - 1)],
            send_sem=send_sem,
            recv_sem=recv_sem,
            device_id={"dom": (me + 1) & (peers - 1)},
            device_id_type=MESH,
        )

    forth = exchange(slab, got, load_send, load_recv, 1)
    copies["comp"].wait()
    forth.wait()
    tile_response(node_sums(peers, got), v["comp"], moved, displacement)
    make_replies(peers, got, moved, reply)
    back = exchange(reply, answer, back_send, back_recv, -1)
    back.wait()
    face_motions(peers, answer, relative, rank, v["weight"], motion)
    residual_copy.wait()


def per_device(
    fluid_state,
    residual_base,
    jacobian,
    columns,
    pseudo_step,
    send_cells,
    interface_face_cell,
    interface_face_area_vector,
    mortar_weight,
    face_route,
    face_node,
    compliance,
):
    peers = lax.axis_size("dom")
    operands = (
        fluid_state,
        residual_base,
        jnp.transpose(jacobian, (1, 2, 0, 3)),
        columns,
        pseudo_step.reshape(-1, LANES),
        send_cells,
        interface_face_cell.reshape(-1, LANES),
        interface_face_area_vector,
        mortar_weight.reshape(-1, LANES),
        face_route.reshape(-1, LANES),
        face_node.reshape(-1, LANES),
        compliance,
    )
    vmem = pltpu.VMEM
    dma = pltpu.SemaphoreType.DMA
    scratch = [vmem(x.shape, x.dtype) for x in operands] + [
        vmem((24, LANES), I32),
        vmem((5, 24, LANES), F32),
        vmem((192, LANES), F32),
        vmem((6, 24, LANES), F32),
        vmem((129, 8, LANES), F32),
        vmem((5, 32, LANES), F32),
        vmem((32, LANES), I32),
        vmem((32 * peers, LANES), BF16),
        vmem((32 * peers, 2 * LANES), F32),
        vmem((32, LANES), F32),
        vmem((peers, LANES), I32),
        vmem((peers, LANES), I32),
        vmem((3, peers, LANES), F32),
        vmem((peers, 4, LANES), F32),
        vmem((peers, 4, LANES), F32),
        vmem((4, 40, LANES), F32),
        vmem(fluid_state.shape, F32),
        vmem((1024, LANES), F32),
        vmem((LANES, LANES), F32),
        vmem((16, LANES), F32),
        vmem((peers, 4, LANES), F32),
        vmem((peers, 4, LANES), F32),
        dma((len(INPUTS),)),
        dma,
        dma((6,)),
        dma((6,)),
        dma,
        dma,
        dma,
        dma,
    ]
    return pl.pallas_call(
        functools.partial(kernel, peers),
        out_shape=(
            jax.ShapeDtypeStruct(fluid_state.shape, F32),
            jax.ShapeDtypeStruct((3, compliance.shape[0] * LANES), F32),
            jax.ShapeDtypeStruct(interface_face_area_vector.shape, F32),
        ),
        in_specs=[pl.BlockSpec(memory_space=pl.ANY)] * len(operands),
        out_specs=(
            pl.BlockSpec(memory_space=pl.ANY),
            pl.BlockSpec(memory_space=vmem),
            pl.BlockSpec(memory_space=vmem),
        ),
        scratch_shapes=scratch,
        compiler_params=pltpu.CompilerParams(
            collective_id=0, has_side_effects=True, vmem_limit_bytes=56 * 1024 * 1024
        ),
    )(*operands)


def solution(mesh):
    return jax.shard_map(
        per_device,
        mesh=mesh,
        in_specs=(
            P(None, ("sweep", "dom")),
            P(None, ("sweep", "dom")),
            P(None, None, None, ("sweep", "dom")),
            P(None, ("sweep", "dom")),
            P(("sweep", "dom")),
            P(("sweep", "dom"), None),
            P(("sweep", "dom")),
            P(None, ("sweep", "dom")),
            P(("sweep", "dom")),
            P(("sweep", "dom"), None),
            P(("sweep", "dom")),
            P(("sweep", "dom"), None, None),
        ),
        out_specs=(P(None, ("sweep", "dom")), P(None, ("sweep", "dom")), P(None, ("sweep", "dom"))),
        check_vma=False,
    )
```

```python
import functools

import jax
import jax.numpy as jnp
from jax import lax
from jax.experimental import pallas as pl
from jax.experimental.pallas import tpu as pltpu
from jax.sharding import PartitionSpec as P

MESH = pl.DeviceIdType.MESH
OFFSETS = (-3, -2, -1, 1, 2, 3)
HIGH = lax.Precision.HIGHEST
F32 = jnp.float32
BF16 = jnp.bfloat16
I32 = jnp.int32
LANES = 128


def pick(row, where_at):
    return jnp.take_along_axis(
        jnp.broadcast_to(row, where_at.shape), where_at, axis=1, mode="promise_in_bounds"
    )


def iota(shape, dim):
    return lax.broadcasted_iota(I32, shape, dim)


def lanes(block):
    return pl.ds(pl.multiple_of(block * LANES, LANES), LANES)


def three_parts(value):
    high = value.astype(BF16)
    rest = value - high.astype(F32)
    middle = rest.astype(BF16)
    low = (rest - middle.astype(F32)).astype(BF16)
    return high, middle, low


def dot_nt(a, b, precision=None):
    return lax.dot_general(
        a, b, (((1,), (1,)), ((), ())), precision=precision, preferred_element_type=F32
    )


def offset_of(group, place):
    side = place // 2
    dz = 4 + (1 - 2 * (group % 2)) * ((group + 1) // 2)
    dy = 2 + (1 - 2 * (side % 2)) * ((side + 1) // 2)
    return dz, dy, 1 - place % 2


def slot_of(me, route):
    dz = ((route >> 3) - (me >> 3)) & 7
    dy = ((route >> 1) - (me >> 1)) & 3
    dc = (route - me) & 1
    group = jnp.where(dz < 4, 7 - 2 * dz, 2 * dz - 8)
    side = jnp.where(dy < 2, 3 - 2 * dy, 2 * dy - 4)
    return group * 8 + side * 2 + (1 - dc)


def gather_sends(fluid, send, index, found, out):
    for k in range(4):
        index[pl.ds(k, 6, stride=4), :] = send[:, k * LANES : (k + 1) * LANES]

    def part(g, carry):
        rows = pl.ds(pl.multiple_of(g * 8, 8), 8)
        cell = index[rows, :]
        low, high = cell & (LANES - 1), cell >> 7

        def step(block, total):
            hit = high == block
            return tuple(
                jnp.where(hit, pick(fluid[pl.ds(c, 1), lanes(block)], low), total[c])
                for c in range(5)
            )

        total = lax.fori_loop(0, 128, step, (jnp.zeros((8, LANES), F32),) * 5, unroll=128)
        for c in range(5):
            found[c, rows, :] = total[c]
        return carry

    lax.fori_loop(0, 3, part, 0)
    for m in range(6):
        for c in range(5):
            out[m * 24 + c * 4 : m * 24 + c * 4 + 4, :] = found[c, m * 4 : m * 4 + 4, :]


def shift_table(fluid, table):
    left = iota((5, LANES), 1) < 64

    def step(block, before):
        here = pltpu.roll(fluid[:, lanes(block)], 64, 1)
        table[block, 0:5, :] = jnp.where(left, before, here)
        return here

    last = lax.fori_loop(0, 128, step, jnp.zeros((5, LANES), F32), unroll=32)
    table[128, 0:5, :] = last


def rank_faces(me, peers, route, relative, onehot, prefix, rank):
    relative[...] = slot_of(me, route[...])
    line = iota((peers, LANES), 0)
    for i in range(32):
        hit = jnp.broadcast_to(relative[i : i + 1, :], (peers, LANES)) == line
        onehot[i * peers : (i + 1) * peers, :] = jnp.where(hit, 1.0, 0.0).astype(BF16)
    upto = jnp.where(iota((LANES, LANES), 0) <= iota((LANES, LANES), 1), 1.0, 0.0)
    weights = jnp.concatenate([upto, jnp.ones((LANES, LANES), F32)], axis=1).astype(BF16)

    def count(part, carry):
        rows = pl.ds(pl.multiple_of(part * 512, 512), 512)
        prefix[rows, :] = jnp.dot(onehot[rows, :], weights, preferred_element_type=F32)
        return carry

    lax.fori_loop(0, 32 * peers // 512, count, 0)

    def step(i, before):
        rows = pl.ds(pl.multiple_of(i * peers, peers), peers)
        hit = onehot[rows, :].astype(F32)
        here = prefix[rows, 0:LANES] + before
        rank[pl.ds(i, 1), :] = jnp.sum(hit * here, axis=0, keepdims=True) - 1.0
        return before + prefix[rows, LANES : 2 * LANES]

    lax.fori_loop(0, 32, step, jnp.zeros((peers, LANES), F32), unroll=2)


def compact_faces(peers, onehot, rank, fnode, weight, area, face_at, slab, scale):
    line = iota((LANES, LANES), 0).astype(F32)
    lane = iota((peers, LANES), 1).astype(F32)

    def step(pair, total):
        left, right = [], []
        for half in range(2):
            i = pair * 2 + half
            hit = onehot[pl.ds(pl.multiple_of(i * peers, peers), peers), :].astype(F32)
            left.append(
                jnp.concatenate(
                    [hit * (i + 1).astype(F32), hit * lane], axis=0
                ).astype(BF16)
            )
            place = jnp.broadcast_to(rank[pl.ds(i, 1), :], (LANES, LANES)) == line
            right.append(jnp.where(place, 1.0, 0.0).astype(BF16))
        return total + dot_nt(jnp.concatenate(left, axis=1), jnp.concatenate(right, axis=1))

    found = lax.fori_loop(0, 16, step, jnp.zeros((2 * peers, LANES), F32), unroll=COMPACT_UNROLL)
    high = found[0:peers, :].astype(I32) - 1
    low = found[peers : 2 * peers, :].astype(I32)
    face_at[...] = (high << 7) + low

    def part(g, carry):
        rows = pl.ds(pl.multiple_of(g * 8, 8), 8)
        face = face_at[rows, :]
        h, l = face >> 7, face & (LANES - 1)

        def look(i, total):
            return jnp.where(h == i, pick(fnode[pl.ds(i, 1), :], l), total)

        node = lax.fori_loop(0, 32, look, jnp.zeros((8, LANES), I32), unroll=32)
        slab[rows, 3, :] = node.astype(F32)
        return carry

    lax.fori_loop(0, peers // 8, part, 0, unroll=2)

    def weigh(i, carry):
        scale[pl.ds(i, 3, stride=32), :] = weight[pl.ds(i, 1), :] * area[:, lanes(i)]
        return carry

    lax.fori_loop(0, 32, weigh, 0, unroll=8)


def halo_table(arrived, table):
    line, lane = iota((8, LANES), 0), iota((8, LANES), 1)
    where_at = line * 16 + (lane & 15)
    for c in range(5):
        for quarter in range(4):
            total = jnp.zeros((8, LANES), F32)
            for n in range(6):
                got = pick(arrived[n, c * 4 + quarter : c * 4 + quarter + 1, :], where_at)
                total = jnp.where((lane >> 4) == n, got, total)
            table[c, quarter * 8 : quarter * 8 + 8, :] = total


def apply_system(fluid, base, jac, cols, dt, table, halo, sums, picks, residual, state):
    cells = fluid.shape[1]
    sums[...] = jnp.zeros(sums.shape, F32)

    def step(q, carry):
        where_at, chunk = [], []
        for j in range(4):
            col = cols[:, lanes(q * 4 + j)]
            shifted = col + 64 - q * 512
            far = col - cells
            far_at = (far >> 9) * 16 + (far & 511) - q * 16
            inside = col < cells
            where_at.append(jnp.where(inside, shifted, far_at) & (LANES - 1))
            chunk.append(jnp.where(inside, shifted >> 7, 5))
        for j in range(4):
            picked = []
            for c in range(5):
                total = pick(table[q * 4, c : c + 1, :], where_at[j])
                for k in range(1, 5):
                    got = pick(table[q * 4 + k, c : c + 1, :], where_at[j])
                    total = jnp.where(chunk[j] == k, got, total)
                got = pick(halo[c, pl.ds(q, 1), :], where_at[j])
                picked.append(jnp.where(chunk[j] == 5, got, total))
            at = lanes(q * 4 + j)
            for c in range(5):
                picks[c, q * 4 + j, 0:7, :] = picked[c]
            for r in (0, 1, 4):
                total = jac[r, 0, :, at].astype(F32) * picked[0]
                for c in range(1, 5):
                    total = total + jac[r, c, :, at].astype(F32) * picked[c]
                sums[j, r * 8 : r * 8 + 7, :] = total
            coupled = sums[j, pl.ds(0, 5, stride=8), :]
            for b in range(1, 7):
                coupled = coupled + sums[j, pl.ds(b, 5, stride=8), :]
            left = base[:, at] - coupled
            residual[:, at] = left
            block = q * 4 + j
            state[pl.ds(pl.multiple_of(block * 8, 8), 5), :] = (
                fluid[:, at] + dt[pl.ds(block, 1), :] * left
            )
        return carry

    lax.fori_loop(0, cells // 512, step, 0, unroll=APPLY_UNROLL)


def apply_rest(base, jac, picks, sums, residual):
    def step(quad, carry):
        for j in range(4):
            block = quad * 4 + j
            at = lanes(block)
            for r in (2, 3):
                total = jac[r, 0, :, at].astype(F32) * picks[0, block, 0:7, :]
                for c in range(1, 5):
                    total = total + jac[r, c, :, at].astype(F32) * picks[c, block, 0:7, :]
                sums[j, r * 8 : r * 8 + 7, :] = total
            coupled = sums[j, pl.ds(0, 5, stride=8), :]
            for b in range(1, 7):
                coupled = coupled + sums[j, pl.ds(b, 5, stride=8), :]
            residual[2:4, at] = (base[:, at] - coupled)[2:4, :]
        return carry

    lax.fori_loop(0, 32, step, 0)


def cell_pressures(state, pressure):
    def step(i, carry):
        first = pl.multiple_of(i * 64, 64)
        p0, p1, p4 = (state[pl.ds(first + r, 8, stride=8), :] for r in (0, 1, 4))
        pressure[pl.ds(pl.multiple_of(i * 8, 8), 8), :] = 0.4 * (p4 - 0.8 * p1 + 0.32 * p0)
        return carry

    lax.fori_loop(0, 16, step, 0, unroll=4)


def face_loads(pressure, fcell, scale, loads):
    def part(g, carry):
        first = pl.multiple_of(g * 8, 8)
        cell = fcell[pl.ds(first, 8), :]
        low, high = cell & (LANES - 1), cell >> 7

        def step(i, total):
            return jnp.where(high == i, pick(pressure[pl.ds(i, 1), :], low), total)

        found = lax.fori_loop(0, 128, step, jnp.zeros((8, LANES), F32), unroll=128)
        for c in range(3):
            rows = pl.ds(first + c * 32, 8)
            loads[rows, :] = scale[rows, :] * found
        return carry

    lax.fori_loop(0, 4, part, 0)


def fill_slabs(g, loads, face_at, slab):
    rows = pl.ds(pl.multiple_of(g * 8, 8), 8)
    face = face_at[rows, :]
    h, l = face >> 7, face & (LANES - 1)

    def look(i, total):
        hit = h == i
        return tuple(
            jnp.where(hit, pick(loads[pl.ds(c * 32 + i, 1), :], l), total[c]) for c in range(3)
        )

    total = lax.fori_loop(0, 32, look, (jnp.zeros((8, LANES), F32),) * 3, unroll=32)
    for c in range(3):
        slab[rows, c, :] = total[c]


def node_sums(g, got):
    line = iota((LANES, LANES), 0)
    above = iota((8, LANES), 0) >> 2
    left, right = [], []
    for s in range(8):
        piece = got[g * 8 + s]
        node = piece[3:4, :].astype(I32)
        twice = jnp.concatenate([piece, piece], axis=0)
        high = jnp.broadcast_to(node >> 7, (8, LANES))
        spread = jnp.concatenate(
            [jnp.where(high == above, twice, 0.0), jnp.where(high == above + 2, twice, 0.0)],
            axis=0,
        )
        left.append(jnp.concatenate(three_parts(spread), axis=0))
        hit = jnp.broadcast_to(node & (LANES - 1), (LANES, LANES)) == line
        right.append(jnp.where(hit, 1.0, 0.0).astype(BF16))
    return dot_nt(jnp.concatenate(left, axis=1), jnp.concatenate(right, axis=1))


def split_compliance(compliance, high, middle):
    def step(i, carry):
        t, rows = i // 4, pl.ds(pl.multiple_of((i % 4) * 96, 96), 96)
        value = compliance[t, rows, :]
        top = value.astype(BF16)
        high[t, rows, :] = top
        middle[t, rows, :] = (value - top.astype(F32)).astype(BF16)
        return carry

    lax.fori_loop(0, 16, step, 0)


def tile_response(total, high, middle, moved, displacement):
    sums = total[0:16, :] + total[16:32, :] + total[32:48, :]
    for t in range(4):
        load = jnp.concatenate([sums[t * 4 + c : t * 4 + c + 1, :] for c in range(3)], axis=1)
        parts = jnp.concatenate(
            [jnp.broadcast_to(part, (16, part.shape[1])) for part in three_parts(load)], axis=0
        )
        first = dot_nt(parts, high[t])
        second = dot_nt(parts[0:32], middle[t])
        out = first[0:1] + ((first[16:17] + second[0:1]) + (first[32:33] + second[16:17]))
        for c in range(3):
            row = out[:, c * LANES : (c + 1) * LANES]
            moved[c * 4 + t : c * 4 + t + 1, :] = row
            displacement[c : c + 1, t * LANES : (t + 1) * LANES] = row


def make_replies(g, got, moved, reply):
    rows = pl.ds(pl.multiple_of(g * 8, 8), 8)
    node = got[rows, 3, :].astype(I32)
    low, high = node & (LANES - 1), node >> 7
    for c in range(3):
        total = pick(moved[c * 4 : c * 4 + 1, :], low)
        for t in range(1, 4):
            total = jnp.where(high == t, pick(moved[c * 4 + t : c * 4 + t + 1, :], low), total)
        reply[rows, c, :] = total


def face_motions(g, total, answer, relative, rank):
    total = list(total)
    for f in range(4):
        rows = slice(f * 8, f * 8 + 8)
        slot, peer = rank[rows, :].astype(I32), relative[rows, :]
        for s in range(8):
            hit = peer == g * 8 + s
            for c in range(3):
                row = answer[g * 8 + s, c : c + 1, :]
                total[c * 4 + f] = jnp.where(hit, pick(row, slot), total[c * 4 + f])
    return tuple(total)


def store_motions(total, weight, motion):
    for f in range(4):
        for c in range(3):
            out = total[c * 4 + f] * weight[f * 8 : f * 8 + 8, :]
            for s in range(8):
                at = (f * 8 + s) * LANES
                motion[c : c + 1, at : at + LANES] = out[s : s + 1, :]


APPLY_UNROLL = 4
COMPACT_UNROLL = 16
INPUTS = ("fluid", "base", "jac", "cols", "dt", "send", "fcell", "area", "weight", "route", "fnode", "comp")


def kernel(peers, *refs):
    count = len(INPUTS)
    hbm = dict(zip(INPUTS, refs[:count]))
    residual_out, displacement, motion = refs[count : count + 3]
    refs = refs[count + 3 :]
    v = dict(zip(INPUTS, refs[:count]))
    (
        index, found, sends, arrived, table, halo, relative, onehot, prefix, rank, face_at, scale,
        loads, slab, got, sums, picks, residual, state, pressure, comp_high, comp_middle, moved,
        reply, answer,
        in_sems, out_sem, halo_send, halo_recv, load_send, load_recv, back_send, back_recv,
    ) = refs[count:]
    me = lax.axis_index("dom")
    copies = {
        name: pltpu.make_async_copy(hbm[name], v[name], in_sems.at[i])
        for i, name in enumerate(INPUTS)
    }
    for name in ("fluid", "send", "route", "fcell", "fnode", "weight", "area", "cols", "jac", "base", "dt", "comp"):
        copies[name].start()
    barrier = pltpu.get_barrier_semaphore()

    def greet(r, carry):
        pl.semaphore_signal(
            barrier, inc=1, device_id={"dom": (me + r) & (peers - 1)}, device_id_type=MESH
        )
        return carry

    lax.fori_loop(1, peers, greet, 0)
    copies["send"].wait()
    copies["fluid"].wait()
    gather_sends(v["fluid"], v["send"], index, found, sends)
    pl.semaphore_wait(barrier, peers - 1)

    halo_copies = []
    for m in range(6):
        copy = pltpu.make_async_remote_copy(
            src_ref=sends.at[pl.ds(24 * m, 24)],
            dst_ref=arrived.at[5 - m],
            send_sem=halo_send.at[m],
            recv_sem=halo_recv.at[5 - m],
            device_id={"dom": (me + OFFSETS[m] + peers) & (peers - 1)},
            device_id_type=MESH,
        )
        copy.start()
        halo_copies.append(copy)

    shift_table(v["fluid"], table)
    copies["route"].wait()
    rank_faces(me, peers, v["route"], relative, onehot, prefix, rank)
    for name in ("fnode", "weight", "area"):
        copies[name].wait()
    compact_faces(
        peers, onehot, rank, v["fnode"], v["weight"], v["area"], face_at, slab, scale
    )
    for copy in halo_copies:
        copy.wait()
    halo_table(arrived, halo)
    for name in ("cols", "jac", "base", "dt", "fcell"):
        copies[name].wait()
    apply_system(
        v["fluid"], v["base"], v["jac"], v["cols"], v["dt"], table, halo, sums, picks, residual, state
    )
    cell_pressures(state, pressure)
    face_loads(pressure, v["fcell"], scale, loads)

    def copy_of(source, target, send_sem, recv_sem, slots, to, group):
        return pltpu.make_async_remote_copy(
            src_ref=source.at[slots],
            dst_ref=target.at[slots],
            send_sem=send_sem,
            recv_sem=recv_sem.at[group],
            device_id={"dom": to},
            device_id_type=MESH,
        )

    def send_group(source, target, send_sem, recv_sem, sign, group, amount):
        for place in range(amount):
            dz, dy, dc = offset_of(group, place)
            to = (
                (((me >> 3) + sign * dz + 8) & 7) * 8
                + (((me >> 1) + sign * dy + 4) & 3) * 2
                + ((me + dc) & 1)
            )
            copy_of(source, target, send_sem, recv_sem, group * 8 + place, to, group).start()

    def received(source, target, send_sem, recv_sem, group, amount):
        slots = pl.ds(group * 8, amount)
        copy_of(source, target, send_sem, recv_sem, slots, me ^ 1, group).wait_recv()

    forth = (slab, got, load_send, load_recv)
    back = (reply, answer, back_send, back_recv)

    def send_loads(g, carry):
        fill_slabs(g, loads, face_at, slab)
        send_group(*forth, 1, g, 8)
        return carry

    lax.fori_loop(0, 7, send_loads, 0)
    fill_slabs(7, loads, face_at, slab)
    send_group(*forth, 1, 7, 7)
    got[63] = slab[63]

    apply_rest(v["base"], v["jac"], picks, sums, residual)
    residual_copy = pltpu.make_async_copy(residual, residual_out, out_sem)
    residual_copy.start()
    copies["comp"].wait()
    split_compliance(v["comp"], comp_high, comp_middle)

    received(*forth, 7, 7)
    total = node_sums(7, got)

    def take_loads(i, total):
        received(*forth, 6 - i, 8)
        return total + node_sums(6 - i, got)

    total = lax.fori_loop(0, 7, take_loads, total)
    tile_response(total, comp_high, comp_middle, moved, displacement)

    def send_replies(g, carry):
        make_replies(g, got, moved, reply)
        send_group(*back, -1, g, 8)
        return carry

    lax.fori_loop(0, 7, send_replies, 0)
    make_replies(7, got, moved, reply)
    send_group(*back, -1, 7, 7)
    answer[63] = reply[63]

    received(*back, 7, 7)
    motions = face_motions(7, (jnp.zeros((8, LANES), F32),) * 12, answer, relative, rank)

    def take_replies(i, total):
        received(*back, 6 - i, 8)
        return face_motions(6 - i, total, answer, relative, rank)

    motions = lax.fori_loop(0, 7, take_replies, motions)
    store_motions(motions, v["weight"], motion)
    for source, target, send_sem, recv_sem in (forth, back):
        copy_of(source, target, send_sem, recv_sem, pl.ds(0, 63), me ^ 1, 0).wait_send()
    residual_copy.wait()


def per_device(
    fluid_state,
    residual_base,
    jacobian,
    columns,
    pseudo_step,
    send_cells,
    interface_face_cell,
    interface_face_area_vector,
    mortar_weight,
    face_route,
    face_node,
    compliance,
):
    peers = lax.axis_size("dom")
    operands = (
        fluid_state,
        residual_base,
        jnp.transpose(jacobian, (1, 2, 0, 3)),
        columns,
        pseudo_step.reshape(-1, LANES),
        send_cells,
        interface_face_cell.reshape(-1, LANES),
        interface_face_area_vector,
        mortar_weight.reshape(-1, LANES),
        face_route.reshape(-1, LANES),
        face_node.reshape(-1, LANES),
        compliance,
    )
    vmem = pltpu.VMEM
    dma = pltpu.SemaphoreType.DMA
    scratch = [vmem(x.shape, x.dtype) for x in operands] + [
        vmem((24, LANES), I32),
        vmem((5, 24, LANES), F32),
        vmem((192, LANES), F32),
        vmem((6, 24, LANES), F32),
        vmem((129, 8, LANES), F32),
        vmem((5, 32, LANES), F32),
        vmem((32, LANES), I32),
        vmem((32 * peers, LANES), BF16),
        vmem((32 * peers, 2 * LANES), F32),
        vmem((32, LANES), F32),
        vmem((peers, LANES), I32),
        vmem((96, LANES), F32),
        vmem((96, LANES), F32),
        vmem((peers, 4, LANES), F32),
        vmem((peers, 4, LANES), F32),
        vmem((4, 40, LANES), F32),
        vmem((5, 128, 8, LANES), F32),
        vmem(fluid_state.shape, F32),
        vmem((1024, LANES), F32),
        vmem((LANES, LANES), F32),
        vmem(compliance.shape, BF16),
        vmem(compliance.shape, BF16),
        vmem((16, LANES), F32),
        vmem((peers, 4, LANES), F32),
        vmem((peers, 4, LANES), F32),
        dma((len(INPUTS),)),
        dma,
        dma((6,)),
        dma((6,)),
        dma,
        dma((8,)),
        dma,
        dma((8,)),
    ]
    return pl.pallas_call(
        functools.partial(kernel, peers),
        out_shape=(
            jax.ShapeDtypeStruct(fluid_state.shape, F32),
            jax.ShapeDtypeStruct((3, compliance.shape[0] * LANES), F32),
            jax.ShapeDtypeStruct(interface_face_area_vector.shape, F32),
        ),
        in_specs=[pl.BlockSpec(memory_space=pl.ANY)] * len(operands),
        out_specs=(
            pl.BlockSpec(memory_space=pl.ANY),
            pl.BlockSpec(memory_space=vmem),
            pl.BlockSpec(memory_space=vmem),
        ),
        scratch_shapes=scratch,
        compiler_params=pltpu.CompilerParams(
            collective_id=0, has_side_effects=True, vmem_limit_bytes=56 * 1024 * 1024
        ),
    )(*operands)


def solution(mesh):
    return jax.shard_map(
        per_device,
        mesh=mesh,
        in_specs=(
            P(None, ("sweep", "dom")),
            P(None, ("sweep", "dom")),
            P(None, None, None, ("sweep", "dom")),
            P(None, ("sweep", "dom")),
            P(("sweep", "dom")),
            P(("sweep", "dom"), None),
            P(("sweep", "dom")),
            P(None, ("sweep", "dom")),
            P(("sweep", "dom")),
            P(("sweep", "dom"), None),
            P(("sweep", "dom")),
            P(("sweep", "dom"), None, None),
        ),
        out_specs=(P(None, ("sweep", "dom")), P(None, ("sweep", "dom")), P(None, ("sweep", "dom"))),
        check_vma=False,
    )
```

```python
import functools

import jax
import jax.numpy as jnp
from jax import lax
from jax.experimental import pallas as pl
from jax.experimental.pallas import tpu as pltpu
from jax.sharding import PartitionSpec as P

MESH = pl.DeviceIdType.MESH
OFFSETS = (-3, -2, -1, 1, 2, 3)
HIGH = lax.Precision.HIGHEST
F32 = jnp.float32
BF16 = jnp.bfloat16
I32 = jnp.int32
LANES = 128


def pick(row, where_at):
    return jnp.take_along_axis(
        jnp.broadcast_to(row, where_at.shape), where_at, axis=1, mode="promise_in_bounds"
    )


def iota(shape, dim):
    return lax.broadcasted_iota(I32, shape, dim)


def lanes(block):
    return pl.ds(pl.multiple_of(block * LANES, LANES), LANES)


def three_parts(value):
    high = value.astype(BF16)
    rest = value - high.astype(F32)
    middle = rest.astype(BF16)
    low = (rest - middle.astype(F32)).astype(BF16)
    return high, middle, low


def dot_nt(a, b, precision=None):
    return lax.dot_general(
        a, b, (((1,), (1,)), ((), ())), precision=precision, preferred_element_type=F32
    )


def offset_of(group, place):
    side = place // 2
    dz = 4 + (1 - 2 * (group % 2)) * ((group + 1) // 2)
    dy = 2 + (1 - 2 * (side % 2)) * ((side + 1) // 2)
    return dz, dy, 1 - place % 2


def slot_of(me, route):
    dz = ((route >> 3) - (me >> 3)) & 7
    dy = ((route >> 1) - (me >> 1)) & 3
    dc = (route - me) & 1
    group = jnp.where(dz < 4, 7 - 2 * dz, 2 * dz - 8)
    side = jnp.where(dy < 2, 3 - 2 * dy, 2 * dy - 4)
    return group * 8 + side * 2 + (1 - dc)


def gather_sends(fluid, send, index, found, out):
    for k in range(4):
        index[pl.ds(k, 6, stride=4), :] = send[:, k * LANES : (k + 1) * LANES]

    def part(g, carry):
        rows = pl.ds(pl.multiple_of(g * 8, 8), 8)
        cell = index[rows, :]
        low, high = cell & (LANES - 1), cell >> 7

        def step(block, total):
            hit = high == block
            return tuple(
                jnp.where(hit, pick(fluid[pl.ds(c, 1), lanes(block)], low), total[c])
                for c in range(5)
            )

        total = lax.fori_loop(0, 128, step, (jnp.zeros((8, LANES), F32),) * 5, unroll=128)
        for c in range(5):
            found[c, rows, :] = total[c]
        return carry

    lax.fori_loop(0, 3, part, 0)
    for m in range(6):
        for c in range(5):
            out[m * 24 + c * 4 : m * 24 + c * 4 + 4, :] = found[c, m * 4 : m * 4 + 4, :]


def shift_table(fluid, table):
    left = iota((5, LANES), 1) < 64

    def step(block, before):
        here = pltpu.roll(fluid[:, lanes(block)], 64, 1)
        table[block, 0:5, :] = jnp.where(left, before, here)
        return here

    last = lax.fori_loop(0, 128, step, jnp.zeros((5, LANES), F32), unroll=32)
    table[128, 0:5, :] = last


def rank_faces(me, peers, route, relative, onehot, prefix, rank):
    relative[...] = slot_of(me, route[...])
    line = iota((peers, LANES), 0)
    for i in range(32):
        hit = jnp.broadcast_to(relative[i : i + 1, :], (peers, LANES)) == line
        onehot[i * peers : (i + 1) * peers, :] = jnp.where(hit, 1.0, 0.0).astype(BF16)
    upto = jnp.where(iota((LANES, LANES), 0) <= iota((LANES, LANES), 1), 1.0, 0.0)
    weights = jnp.concatenate([upto, jnp.ones((LANES, LANES), F32)], axis=1).astype(BF16)

    def count(part, carry):
        rows = pl.ds(pl.multiple_of(part * 512, 512), 512)
        prefix[rows, :] = jnp.dot(onehot[rows, :], weights, preferred_element_type=F32)
        return carry

    lax.fori_loop(0, 32 * peers // 512, count, 0)

    def step(i, before):
        rows = pl.ds(pl.multiple_of(i * peers, peers), peers)
        hit = onehot[rows, :].astype(F32)
        here = prefix[rows, 0:LANES] + before
        rank[pl.ds(i, 1), :] = jnp.sum(hit * here, axis=0, keepdims=True) - 1.0
        return before + prefix[rows, LANES : 2 * LANES]

    lax.fori_loop(0, 32, step, jnp.zeros((peers, LANES), F32), unroll=2)


def compact_faces(peers, onehot, rank, fnode, weight, area, face_at, slab, scale):
    line = iota((LANES, LANES), 0).astype(F32)
    lane = iota((peers, LANES), 1).astype(F32)

    def step(pair, total):
        left, right = [], []
        for half in range(2):
            i = pair * 2 + half
            hit = onehot[pl.ds(pl.multiple_of(i * peers, peers), peers), :].astype(F32)
            left.append(
                jnp.concatenate(
                    [hit * (i + 1).astype(F32), hit * lane], axis=0
                ).astype(BF16)
            )
            place = jnp.broadcast_to(rank[pl.ds(i, 1), :], (LANES, LANES)) == line
            right.append(jnp.where(place, 1.0, 0.0).astype(BF16))
        return total + dot_nt(jnp.concatenate(left, axis=1), jnp.concatenate(right, axis=1))

    found = lax.fori_loop(0, 16, step, jnp.zeros((2 * peers, LANES), F32), unroll=COMPACT_UNROLL)
    high = found[0:peers, :].astype(I32) - 1
    low = found[peers : 2 * peers, :].astype(I32)
    face_at[...] = (high << 7) + low

    def part(g, carry):
        rows = pl.ds(pl.multiple_of(g * 8, 8), 8)
        face = face_at[rows, :]
        h, l = face >> 7, face & (LANES - 1)

        def look(i, total):
            return jnp.where(h == i, pick(fnode[pl.ds(i, 1), :], l), total)

        node = lax.fori_loop(0, 32, look, jnp.zeros((8, LANES), I32), unroll=32)
        slab[rows, 3, :] = node.astype(F32)
        return carry

    lax.fori_loop(0, peers // 8, part, 0, unroll=2)

    def weigh(i, carry):
        scale[pl.ds(i, 3, stride=32), :] = weight[pl.ds(i, 1), :] * area[:, lanes(i)]
        return carry

    lax.fori_loop(0, 32, weigh, 0, unroll=8)


def halo_table(arrived, table):
    line, lane = iota((8, LANES), 0), iota((8, LANES), 1)
    where_at = line * 16 + (lane & 15)
    for c in range(5):
        for quarter in range(4):
            total = jnp.zeros((8, LANES), F32)
            for n in range(6):
                got = pick(arrived[n, c * 4 + quarter : c * 4 + quarter + 1, :], where_at)
                total = jnp.where((lane >> 4) == n, got, total)
            table[c, quarter * 8 : quarter * 8 + 8, :] = total


def window(cols, cells, q, j):
    col = cols[:, lanes(q * 4 + j)]
    shifted = col + 64 - q * 512
    far = col - cells
    far_at = (far >> 9) * 16 + (far & 511) - q * 16
    inside = col < cells
    where_at = jnp.where(inside, shifted, far_at) & (LANES - 1)
    return where_at, jnp.where(inside, shifted >> 7, 5)


def pick_local(c, where_at, chunk, table, q):
    total = pick(table[q * 4, c : c + 1, :], where_at)
    for k in range(1, 5):
        got = pick(table[q * 4 + k, c : c + 1, :], where_at)
        total = jnp.where(chunk == k, got, total)
    return total


def early_picks(cells, cols, table, picks):
    def step(q, carry):
        for j in range(4):
            where_at, chunk = window(cols, cells, q, j)
            for c in range(5):
                picks[c, q * 4 + j, 0:7, :] = pick_local(c, where_at, chunk, table, q)
        return carry

    lax.fori_loop(0, EARLY, step, 0, unroll=6)


def apply_system(fluid, base, jac, cols, dt, table, halo, sums, picks, residual, state):
    cells = fluid.shape[1]
    sums[...] = jnp.zeros(sums.shape, F32)

    def step(q, carry, early):
        for j in range(4):
            where_at, chunk = window(cols, cells, q, j)
            block = q * 4 + j
            at = lanes(block)
            picked = []
            for c in range(5):
                if early:
                    total = picks[c, block, 0:7, :]
                else:
                    total = pick_local(c, where_at, chunk, table, q)
                got = pick(halo[c, pl.ds(q, 1), :], where_at)
                picked.append(jnp.where(chunk == 5, got, total))
            for c in range(5):
                picks[c, block, 0:7, :] = picked[c]
            for r in (0, 1, 4):
                total = jac[r, 0, :, at].astype(F32) * picked[0]
                for c in range(1, 5):
                    total = total + jac[r, c, :, at].astype(F32) * picked[c]
                sums[j, r * 8 : r * 8 + 7, :] = total
            coupled = sums[j, pl.ds(0, 5, stride=8), :]
            for b in range(1, 7):
                coupled = coupled + sums[j, pl.ds(b, 5, stride=8), :]
            left = base[:, at] - coupled
            residual[:, at] = left
            state[pl.ds(pl.multiple_of(block * 8, 8), 5), :] = (
                fluid[:, at] + dt[pl.ds(block, 1), :] * left
            )
        return carry

    lax.fori_loop(0, EARLY, functools.partial(step, early=True), 0, unroll=6)
    lax.fori_loop(EARLY, cells // 512, functools.partial(step, early=False), 0, unroll=10)


def apply_rest(base, jac, picks, sums, residual):
    def step(quad, carry):
        for j in range(4):
            block = quad * 4 + j
            at = lanes(block)
            for r in (2, 3):
                total = jac[r, 0, :, at].astype(F32) * picks[0, block, 0:7, :]
                for c in range(1, 5):
                    total = total + jac[r, c, :, at].astype(F32) * picks[c, block, 0:7, :]
                sums[j, r * 8 : r * 8 + 7, :] = total
            coupled = sums[j, pl.ds(0, 5, stride=8), :]
            for b in range(1, 7):
                coupled = coupled + sums[j, pl.ds(b, 5, stride=8), :]
            residual[2:4, at] = (base[:, at] - coupled)[2:4, :]
        return carry

    lax.fori_loop(0, 32, step, 0)


def cell_pressures(state, pressure):
    def step(i, carry):
        first = pl.multiple_of(i * 64, 64)
        p0, p1, p4 = (state[pl.ds(first + r, 8, stride=8), :] for r in (0, 1, 4))
        pressure[pl.ds(pl.multiple_of(i * 8, 8), 8), :] = 0.4 * (p4 - 0.8 * p1 + 0.32 * p0)
        return carry

    lax.fori_loop(0, 16, step, 0, unroll=4)


def face_loads(pressure, fcell, scale, loads):
    def part(g, carry):
        first = pl.multiple_of(g * 8, 8)
        cell = fcell[pl.ds(first, 8), :]
        low, high = cell & (LANES - 1), cell >> 7

        def step(i, total):
            return jnp.where(high == i, pick(pressure[pl.ds(i, 1), :], low), total)

        found = lax.fori_loop(0, 128, step, jnp.zeros((8, LANES), F32), unroll=128)
        for c in range(3):
            rows = pl.ds(first + c * 32, 8)
            loads[rows, :] = scale[rows, :] * found
        return carry

    lax.fori_loop(0, 4, part, 0)


def fill_slabs(g, loads, face_at, slab):
    rows = pl.ds(pl.multiple_of(g * 8, 8), 8)
    face = face_at[rows, :]
    h, l = face >> 7, face & (LANES - 1)

    def look(i, total):
        hit = h == i
        return tuple(
            jnp.where(hit, pick(loads[pl.ds(c * 32 + i, 1), :], l), total[c]) for c in range(3)
        )

    total = lax.fori_loop(0, 32, look, (jnp.zeros((8, LANES), F32),) * 3, unroll=32)
    for c in range(3):
        slab[rows, c, :] = total[c]


def node_sums(g, got):
    line = iota((LANES, LANES), 0)
    above = iota((8, LANES), 0) >> 2
    left, right = [], []
    for s in range(8):
        piece = got[g * 8 + s]
        node = piece[3:4, :].astype(I32)
        twice = jnp.concatenate([piece, piece], axis=0)
        high = jnp.broadcast_to(node >> 7, (8, LANES))
        spread = jnp.concatenate(
            [jnp.where(high == above, twice, 0.0), jnp.where(high == above + 2, twice, 0.0)],
            axis=0,
        )
        left.append(jnp.concatenate(three_parts(spread), axis=0))
        hit = jnp.broadcast_to(node & (LANES - 1), (LANES, LANES)) == line
        right.append(jnp.where(hit, 1.0, 0.0).astype(BF16))
    return dot_nt(jnp.concatenate(left, axis=1), jnp.concatenate(right, axis=1))


def split_compliance(compliance, high, middle):
    def step(i, carry):
        t, rows = i // 4, pl.ds(pl.multiple_of((i % 4) * 96, 96), 96)
        value = compliance[t, rows, :]
        top = value.astype(BF16)
        high[t, rows, :] = top
        middle[t, rows, :] = (value - top.astype(F32)).astype(BF16)
        return carry

    lax.fori_loop(0, 16, step, 0)


def tile_response(total, high, middle, moved, displacement):
    sums = total[0:16, :] + total[16:32, :] + total[32:48, :]
    for t in range(4):
        load = jnp.concatenate([sums[t * 4 + c : t * 4 + c + 1, :] for c in range(3)], axis=1)
        parts = jnp.concatenate(
            [jnp.broadcast_to(part, (16, part.shape[1])) for part in three_parts(load)], axis=0
        )
        first = dot_nt(parts, high[t])
        second = dot_nt(parts[0:32], middle[t])
        out = first[0:1] + ((first[16:17] + second[0:1]) + (first[32:33] + second[16:17]))
        for c in range(3):
            row = out[:, c * LANES : (c + 1) * LANES]
            moved[c * 4 + t : c * 4 + t + 1, :] = row
            displacement[c : c + 1, t * LANES : (t + 1) * LANES] = row


def make_replies(g, got, moved, reply):
    rows = pl.ds(pl.multiple_of(g * 8, 8), 8)
    node = got[rows, 3, :].astype(I32)
    low, high = node & (LANES - 1), node >> 7
    for c in range(3):
        total = pick(moved[c * 4 : c * 4 + 1, :], low)
        for t in range(1, 4):
            total = jnp.where(high == t, pick(moved[c * 4 + t : c * 4 + t + 1, :], low), total)
        reply[rows, c, :] = total


def face_motions(g, total, answer, relative, rank):
    total = list(total)
    for f in range(4):
        rows = slice(f * 8, f * 8 + 8)
        slot, peer = rank[rows, :].astype(I32), relative[rows, :]
        for s in range(8):
            hit = peer == g * 8 + s
            for c in range(3):
                row = answer[g * 8 + s, c : c + 1, :]
                total[c * 4 + f] = jnp.where(hit, pick(row, slot), total[c * 4 + f])
    return tuple(total)


def store_motions(total, weight, motion):
    for f in range(4):
        for c in range(3):
            out = total[c * 4 + f] * weight[f * 8 : f * 8 + 8, :]
            for s in range(8):
                at = (f * 8 + s) * LANES
                motion[c : c + 1, at : at + LANES] = out[s : s + 1, :]


EARLY = 12
COMPACT_UNROLL = 16
INPUTS = ("fluid", "base", "jac", "cols", "dt", "send", "fcell", "area", "weight", "route", "fnode", "comp")


def kernel(peers, *refs):
    count = len(INPUTS)
    hbm = dict(zip(INPUTS, refs[:count]))
    residual_out, displacement, motion = refs[count : count + 3]
    refs = refs[count + 3 :]
    v = dict(zip(INPUTS, refs[:count]))
    (
        index, found, sends, arrived, table, halo, relative, onehot, prefix, rank, face_at, scale,
        loads, slab, got, sums, picks, residual, state, pressure, comp_high, comp_middle, moved,
        reply, answer,
        in_sems, out_sem, halo_send, halo_recv, load_send, load_recv, back_send, back_recv,
    ) = refs[count:]
    me = lax.axis_index("dom")
    copies = {
        name: pltpu.make_async_copy(hbm[name], v[name], in_sems.at[i])
        for i, name in enumerate(INPUTS)
    }
    copies["fluid"].start()
    copies["send"].start()
    barrier = pltpu.get_barrier_semaphore()

    def greet(r, carry):
        pl.semaphore_signal(
            barrier, inc=1, device_id={"dom": (me + r) & (peers - 1)}, device_id_type=MESH
        )
        return carry

    lax.fori_loop(1, peers, greet, 0)
    for name in ("route", "fnode", "weight", "area", "cols", "fcell", "jac", "base", "dt", "comp"):
        copies[name].start()
    copies["send"].wait()
    copies["fluid"].wait()
    gather_sends(v["fluid"], v["send"], index, found, sends)
    pl.semaphore_wait(barrier, peers - 1)

    halo_copies = []
    for m in range(6):
        copy = pltpu.make_async_remote_copy(
            src_ref=sends.at[pl.ds(24 * m, 24)],
            dst_ref=arrived.at[5 - m],
            send_sem=halo_send.at[m],
            recv_sem=halo_recv.at[5 - m],
            device_id={"dom": (me + OFFSETS[m] + peers) & (peers - 1)},
            device_id_type=MESH,
        )
        copy.start()
        halo_copies.append(copy)

    shift_table(v["fluid"], table)
    copies["route"].wait()
    rank_faces(me, peers, v["route"], relative, onehot, prefix, rank)
    for name in ("fnode", "weight", "area"):
        copies[name].wait()
    compact_faces(
        peers, onehot, rank, v["fnode"], v["weight"], v["area"], face_at, slab, scale
    )
    copies["cols"].wait()
    early_picks(v["fluid"].shape[1], v["cols"], table, picks)
    for copy in halo_copies:
        copy.wait()
    halo_table(arrived, halo)
    for name in ("jac", "base", "dt", "fcell"):
        copies[name].wait()
    apply_system(
        v["fluid"], v["base"], v["jac"], v["cols"], v["dt"], table, halo, sums, picks, residual, state
    )
    cell_pressures(state, pressure)
    face_loads(pressure, v["fcell"], scale, loads)

    def copy_of(source, target, send_sem, recv_sem, height, slots, to, group):
        rows = pl.ds(0, height)
        return pltpu.make_async_remote_copy(
            src_ref=source.at[slots, rows],
            dst_ref=target.at[slots, rows],
            send_sem=send_sem,
            recv_sem=recv_sem.at[group],
            device_id={"dom": to},
            device_id_type=MESH,
        )

    def send_group(source, target, send_sem, recv_sem, height, sign, group, amount):
        for place in range(amount):
            dz, dy, dc = offset_of(group, place)
            to = (
                (((me >> 3) + sign * dz + 8) & 7) * 8
                + (((me >> 1) + sign * dy + 4) & 3) * 2
                + ((me + dc) & 1)
            )
            slot = group * 8 + place
            copy_of(source, target, send_sem, recv_sem, height, slot, to, group).start()

    def received(source, target, send_sem, recv_sem, height, group, amount):
        slots = pl.ds(group * 8, amount)
        copy_of(source, target, send_sem, recv_sem, height, slots, me ^ 1, group).wait_recv()

    forth = (slab, got, load_send, load_recv, 4)
    back = (reply, answer, back_send, back_recv, 3)

    def send_loads(g, carry):
        fill_slabs(g, loads, face_at, slab)
        send_group(*forth, 1, g, 8)
        return carry

    lax.fori_loop(0, 7, send_loads, 0)
    fill_slabs(7, loads, face_at, slab)
    send_group(*forth, 1, 7, 7)
    got[63] = slab[63]

    apply_rest(v["base"], v["jac"], picks, sums, residual)
    residual_copy = pltpu.make_async_copy(residual, residual_out, out_sem)
    residual_copy.start()
    copies["comp"].wait()
    split_compliance(v["comp"], comp_high, comp_middle)

    received(*forth, 7, 7)
    total = node_sums(7, got)

    def take_loads(i, total):
        received(*forth, 6 - i, 8)
        return total + node_sums(6 - i, got)

    total = lax.fori_loop(0, 7, take_loads, total)
    tile_response(total, comp_high, comp_middle, moved, displacement)

    def send_replies(g, carry):
        make_replies(g, got, moved, reply)
        send_group(*back, -1, g, 8)
        return carry

    lax.fori_loop(0, 7, send_replies, 0)
    make_replies(7, got, moved, reply)
    send_group(*back, -1, 7, 7)
    answer[63] = reply[63]

    received(*back, 7, 7)
    motions = face_motions(7, (jnp.zeros((8, LANES), F32),) * 12, answer, relative, rank)

    def take_replies(i, total):
        received(*back, 6 - i, 8)
        return face_motions(6 - i, total, answer, relative, rank)

    motions = lax.fori_loop(0, 7, take_replies, motions)
    store_motions(motions, v["weight"], motion)
    for way in (forth, back):
        copy_of(*way, pl.ds(0, 63), me ^ 1, 0).wait_send()
    residual_copy.wait()


def per_device(
    fluid_state,
    residual_base,
    jacobian,
    columns,
    pseudo_step,
    send_cells,
    interface_face_cell,
    interface_face_area_vector,
    mortar_weight,
    face_route,
    face_node,
    compliance,
):
    peers = lax.axis_size("dom")
    operands = (
        fluid_state,
        residual_base,
        jnp.transpose(jacobian, (1, 2, 0, 3)),
        columns,
        pseudo_step.reshape(-1, LANES),
        send_cells,
        interface_face_cell.reshape(-1, LANES),
        interface_face_area_vector,
        mortar_weight.reshape(-1, LANES),
        face_route.reshape(-1, LANES),
        face_node.reshape(-1, LANES),
        compliance,
    )
    vmem = pltpu.VMEM
    dma = pltpu.SemaphoreType.DMA
    scratch = [vmem(x.shape, x.dtype) for x in operands] + [
        vmem((24, LANES), I32),
        vmem((5, 24, LANES), F32),
        vmem((192, LANES), F32),
        vmem((6, 24, LANES), F32),
        vmem((129, 8, LANES), F32),
        vmem((5, 32, LANES), F32),
        vmem((32, LANES), I32),
        vmem((32 * peers, LANES), BF16),
        vmem((32 * peers, 2 * LANES), F32),
        vmem((32, LANES), F32),
        vmem((peers, LANES), I32),
        vmem((96, LANES), F32),
        vmem((96, LANES), F32),
        vmem((peers, 4, LANES), F32),
        vmem((peers, 4, LANES), F32),
        vmem((4, 40, LANES), F32),
        vmem((5, 128, 8, LANES), F32),
        vmem(fluid_state.shape, F32),
        vmem((1024, LANES), F32),
        vmem((LANES, LANES), F32),
        vmem(compliance.shape, BF16),
        vmem(compliance.shape, BF16),
        vmem((16, LANES), F32),
        vmem((peers, 4, LANES), F32),
        vmem((peers, 4, LANES), F32),
        dma((len(INPUTS),)),
        dma,
        dma((6,)),
        dma((6,)),
        dma,
        dma((8,)),
        dma,
        dma((8,)),
    ]
    results = pl.pallas_call(
        functools.partial(kernel, peers),
        out_shape=(
            jax.ShapeDtypeStruct(fluid_state.shape, F32),
            jax.ShapeDtypeStruct((3, compliance.shape[0] * LANES), F32),
            jax.ShapeDtypeStruct(interface_face_area_vector.shape, F32),
        ),
        in_specs=[pl.BlockSpec(memory_space=pl.ANY)] * len(operands),
        out_specs=(
            pl.BlockSpec(memory_space=pl.ANY),
            pl.BlockSpec(memory_space=vmem),
            pl.BlockSpec(memory_space=vmem),
        ),
        scratch_shapes=scratch,
        compiler_params=pltpu.CompilerParams(
            collective_id=0, has_side_effects=True, vmem_limit_bytes=56 * 1024 * 1024
        ),
    )(*operands)
    return hand_over(*results)


def hand_over_kernel(*refs):
    sems = refs[-1]
    copies = [pltpu.make_async_copy(refs[i], refs[3 + i], sems.at[i]) for i in range(3)]
    for copy in copies:
        copy.start()
    for copy in copies:
        copy.wait()


def hand_over(*results):
    return pl.pallas_call(
        hand_over_kernel,
        out_shape=[jax.ShapeDtypeStruct(x.shape, x.dtype) for x in results],
        in_specs=[pl.BlockSpec(memory_space=pl.ANY)] * 3,
        out_specs=[pl.BlockSpec(memory_space=pl.ANY)] * 3,
        scratch_shapes=[pltpu.SemaphoreType.DMA((3,))],
        compiler_params=pltpu.CompilerParams(vmem_limit_bytes=60 * 1024 * 1024),
    )(*results)


def solution(mesh):
    return jax.shard_map(
        per_device,
        mesh=mesh,
        in_specs=(
            P(None, ("sweep", "dom")),
            P(None, ("sweep", "dom")),
            P(None, None, None, ("sweep", "dom")),
            P(None, ("sweep", "dom")),
            P(("sweep", "dom")),
            P(("sweep", "dom"), None),
            P(("sweep", "dom")),
            P(None, ("sweep", "dom")),
            P(("sweep", "dom")),
            P(("sweep", "dom"), None),
            P(("sweep", "dom")),
            P(("sweep", "dom"), None, None),
        ),
        out_specs=(P(None, ("sweep", "dom")), P(None, ("sweep", "dom")), P(None, ("sweep", "dom"))),
        check_vma=False,
    )
```

```python
import functools

import jax
import jax.numpy as jnp
from jax import lax
from jax.experimental import pallas as pl
from jax.experimental.pallas import tpu as pltpu
from jax.sharding import PartitionSpec as P

MESH = pl.DeviceIdType.MESH
OFFSETS = (-3, -2, -1, 1, 2, 3)
HIGH = lax.Precision.HIGHEST
F32 = jnp.float32
BF16 = jnp.bfloat16
I32 = jnp.int32
LANES = 128


def pick(row, where_at):
    return jnp.take_along_axis(
        jnp.broadcast_to(row, where_at.shape), where_at, axis=1, mode="promise_in_bounds"
    )


def iota(shape, dim):
    return lax.broadcasted_iota(I32, shape, dim)


def lanes(block):
    return pl.ds(pl.multiple_of(block * LANES, LANES), LANES)


def three_parts(value):
    high = value.astype(BF16)
    rest = value - high.astype(F32)
    middle = rest.astype(BF16)
    low = (rest - middle.astype(F32)).astype(BF16)
    return high, middle, low


def dot_nt(a, b, precision=None):
    return lax.dot_general(
        a, b, (((1,), (1,)), ((), ())), precision=precision, preferred_element_type=F32
    )


def offset_of(group, place):
    side = place // 2
    dz = 4 + (1 - 2 * (group % 2)) * ((group + 1) // 2)
    dy = 2 + (1 - 2 * (side % 2)) * ((side + 1) // 2)
    return dz, dy, 1 - place % 2


def slot_of(me, route):
    dz = ((route >> 3) - (me >> 3)) & 7
    dy = ((route >> 1) - (me >> 1)) & 3
    dc = (route - me) & 1
    group = jnp.where(dz < 4, 7 - 2 * dz, 2 * dz - 8)
    side = jnp.where(dy < 2, 3 - 2 * dy, 2 * dy - 4)
    return group * 8 + side * 2 + (1 - dc)


def gather_sends(fluid, send, index, found, out):
    for k in range(4):
        index[pl.ds(k, 6, stride=4), :] = send[:, k * LANES : (k + 1) * LANES]

    def part(g, carry):
        rows = pl.ds(pl.multiple_of(g * 8, 8), 8)
        cell = index[rows, :]
        low, high = cell & (LANES - 1), cell >> 7

        def step(block, total):
            hit = high == block
            return tuple(
                jnp.where(hit, pick(fluid[pl.ds(c, 1), lanes(block)], low), total[c])
                for c in range(5)
            )

        total = lax.fori_loop(0, 128, step, (jnp.zeros((8, LANES), F32),) * 5, unroll=128)
        for c in range(5):
            found[c, rows, :] = total[c]
        return carry

    lax.fori_loop(0, 3, part, 0)
    for m in range(6):
        for c in range(5):
            out[m * 24 + c * 4 : m * 24 + c * 4 + 4, :] = found[c, m * 4 : m * 4 + 4, :]


def shift_table(fluid, table):
    left = iota((5, LANES), 1) < 64

    def step(block, before):
        here = pltpu.roll(fluid[:, lanes(block)], 64, 1)
        table[block, 0:5, :] = jnp.where(left, before, here)
        return here

    last = lax.fori_loop(0, 128, step, jnp.zeros((5, LANES), F32), unroll=32)
    table[128, 0:5, :] = last


def rank_faces(me, peers, route, relative, onehot, prefix, rank):
    relative[...] = slot_of(me, route[...])
    line = iota((peers, LANES), 0)
    for i in range(32):
        hit = jnp.broadcast_to(relative[i : i + 1, :], (peers, LANES)) == line
        onehot[i * peers : (i + 1) * peers, :] = jnp.where(hit, 1.0, 0.0).astype(BF16)
    upto = jnp.where(iota((LANES, LANES), 0) <= iota((LANES, LANES), 1), 1.0, 0.0)
    weights = jnp.concatenate([upto, jnp.ones((LANES, LANES), F32)], axis=1).astype(BF16)

    def count(part, carry):
        rows = pl.ds(pl.multiple_of(part * 512, 512), 512)
        prefix[rows, :] = jnp.dot(onehot[rows, :], weights, preferred_element_type=F32)
        return carry

    lax.fori_loop(0, 32 * peers // 512, count, 0)

    def step(i, before):
        rows = pl.ds(pl.multiple_of(i * peers, peers), peers)
        hit = onehot[rows, :].astype(F32)
        here = prefix[rows, 0:LANES] + before
        rank[pl.ds(i, 1), :] = jnp.sum(hit * here, axis=0, keepdims=True) - 1.0
        return before + prefix[rows, LANES : 2 * LANES]

    lax.fori_loop(0, 32, step, jnp.zeros((peers, LANES), F32), unroll=2)


def compact_faces(peers, onehot, rank, fnode, weight, area, face_at, slab, scale):
    line = iota((LANES, LANES), 0).astype(F32)
    lane = iota((peers, LANES), 1).astype(F32)

    def step(pair, total):
        left, right = [], []
        for half in range(2):
            i = pair * 2 + half
            hit = onehot[pl.ds(pl.multiple_of(i * peers, peers), peers), :].astype(F32)
            left.append(
                jnp.concatenate(
                    [hit * (i + 1).astype(F32), hit * lane], axis=0
                ).astype(BF16)
            )
            place = jnp.broadcast_to(rank[pl.ds(i, 1), :], (LANES, LANES)) == line
            right.append(jnp.where(place, 1.0, 0.0).astype(BF16))
        return total + dot_nt(jnp.concatenate(left, axis=1), jnp.concatenate(right, axis=1))

    found = lax.fori_loop(0, 16, step, jnp.zeros((2 * peers, LANES), F32), unroll=COMPACT_UNROLL)
    high = found[0:peers, :].astype(I32) - 1
    low = found[peers : 2 * peers, :].astype(I32)
    face_at[...] = (high << 7) + low

    def part(g, carry):
        rows = pl.ds(pl.multiple_of(g * 8, 8), 8)
        face = face_at[rows, :]
        h, l = face >> 7, face & (LANES - 1)

        def look(i, total):
            return jnp.where(h == i, pick(fnode[pl.ds(i, 1), :], l), total)

        node = lax.fori_loop(0, 32, look, jnp.zeros((8, LANES), I32), unroll=32)
        slab[rows, 3, :] = node.astype(F32)
        return carry

    lax.fori_loop(0, peers // 8, part, 0, unroll=2)

    def weigh(i, carry):
        scale[pl.ds(i, 3, stride=32), :] = weight[pl.ds(i, 1), :] * area[:, lanes(i)]
        return carry

    lax.fori_loop(0, 32, weigh, 0, unroll=8)


def halo_table(arrived, table):
    line, lane = iota((8, LANES), 0), iota((8, LANES), 1)
    where_at = line * 16 + (lane & 15)
    for c in range(5):
        for quarter in range(4):
            total = jnp.zeros((8, LANES), F32)
            for n in range(6):
                got = pick(arrived[n, c * 4 + quarter : c * 4 + quarter + 1, :], where_at)
                total = jnp.where((lane >> 4) == n, got, total)
            table[c, quarter * 8 : quarter * 8 + 8, :] = total


def window(cols, cells, q, j):
    col = cols[:, lanes(q * 4 + j)]
    shifted = col + 64 - q * 512
    far = col - cells
    far_at = (far >> 9) * 16 + (far & 511) - q * 16
    inside = col < cells
    where_at = jnp.where(inside, shifted, far_at) & (LANES - 1)
    return where_at, jnp.where(inside, shifted >> 7, 5)


def pick_local(c, where_at, chunk, table, q):
    total = pick(table[q * 4, c : c + 1, :], where_at)
    for k in range(1, 5):
        got = pick(table[q * 4 + k, c : c + 1, :], where_at)
        total = jnp.where(chunk == k, got, total)
    return total


def early_picks(cells, cols, table, picks):
    def step(q, carry):
        for j in range(4):
            where_at, chunk = window(cols, cells, q, j)
            for c in range(5):
                picks[c, q * 4 + j, 0:7, :] = pick_local(c, where_at, chunk, table, q)
        return carry

    lax.fori_loop(0, EARLY, step, 0, unroll=6)


def apply_system(fluid, base, jac, cols, dt, table, halo, sums, picks, residual, state):
    cells = fluid.shape[1]
    sums[...] = jnp.zeros(sums.shape, F32)

    def step(q, carry, early):
        for j in range(4):
            where_at, chunk = window(cols, cells, q, j)
            block = q * 4 + j
            at = lanes(block)
            picked = []
            for c in range(5):
                if early:
                    total = picks[c, block, 0:7, :]
                else:
                    total = pick_local(c, where_at, chunk, table, q)
                got = pick(halo[c, pl.ds(q, 1), :], where_at)
                picked.append(jnp.where(chunk == 5, got, total))
            for c in range(5):
                picks[c, block, 0:7, :] = picked[c]
            for r in (0, 1, 4):
                total = jac[r, 0, :, at].astype(F32) * picked[0]
                for c in range(1, 5):
                    total = total + jac[r, c, :, at].astype(F32) * picked[c]
                sums[j, r * 8 : r * 8 + 7, :] = total
            coupled = sums[j, pl.ds(0, 5, stride=8), :]
            for b in range(1, 7):
                coupled = coupled + sums[j, pl.ds(b, 5, stride=8), :]
            left = base[:, at] - coupled
            residual[:, at] = left
            state[pl.ds(pl.multiple_of(block * 8, 8), 5), :] = (
                fluid[:, at] + dt[pl.ds(block, 1), :] * left
            )
        return carry

    lax.fori_loop(0, EARLY, functools.partial(step, early=True), 0, unroll=6)
    lax.fori_loop(EARLY, cells // 512, functools.partial(step, early=False), 0, unroll=10)


def apply_rest(base, jac, picks, sums, residual):
    def step(quad, carry):
        for j in range(4):
            block = quad * 4 + j
            at = lanes(block)
            for r in (2, 3):
                total = jac[r, 0, :, at].astype(F32) * picks[0, block, 0:7, :]
                for c in range(1, 5):
                    total = total + jac[r, c, :, at].astype(F32) * picks[c, block, 0:7, :]
                sums[j, r * 8 : r * 8 + 7, :] = total
            coupled = sums[j, pl.ds(0, 5, stride=8), :]
            for b in range(1, 7):
                coupled = coupled + sums[j, pl.ds(b, 5, stride=8), :]
            residual[2:4, at] = (base[:, at] - coupled)[2:4, :]
        return carry

    lax.fori_loop(0, 32, step, 0)


def cell_pressures(state, pressure):
    def step(i, carry):
        first = pl.multiple_of(i * 64, 64)
        p0, p1, p4 = (state[pl.ds(first + r, 8, stride=8), :] for r in (0, 1, 4))
        pressure[pl.ds(pl.multiple_of(i * 8, 8), 8), :] = 0.4 * (p4 - 0.8 * p1 + 0.32 * p0)
        return carry

    lax.fori_loop(0, 16, step, 0, unroll=4)


def face_loads(pressure, fcell, scale, loads):
    def part(g, carry):
        first = pl.multiple_of(g * 8, 8)
        cell = fcell[pl.ds(first, 8), :]
        low, high = cell & (LANES - 1), cell >> 7

        def step(i, total):
            return jnp.where(high == i, pick(pressure[pl.ds(i, 1), :], low), total)

        found = lax.fori_loop(0, 128, step, jnp.zeros((8, LANES), F32), unroll=128)
        for c in range(3):
            rows = pl.ds(first + c * 32, 8)
            loads[rows, :] = scale[rows, :] * found
        return carry

    lax.fori_loop(0, 4, part, 0)


def fill_slabs(g, loads, face_at, slab):
    rows = pl.ds(pl.multiple_of(g * 8, 8), 8)
    face = face_at[rows, :]
    h, l = face >> 7, face & (LANES - 1)

    def look(i, total):
        hit = h == i
        return tuple(
            jnp.where(hit, pick(loads[pl.ds(c * 32 + i, 1), :], l), total[c]) for c in range(3)
        )

    total = lax.fori_loop(0, 32, look, (jnp.zeros((8, LANES), F32),) * 3, unroll=32)
    for c in range(3):
        slab[rows, c, :] = total[c]


def node_sums(g, got):
    line = iota((LANES, LANES), 0)
    above = iota((8, LANES), 0) >> 2
    left, right = [], []
    for s in range(8):
        piece = got[g * 8 + s]
        node = piece[3:4, :].astype(I32)
        twice = jnp.concatenate([piece, piece], axis=0)
        high = jnp.broadcast_to(node >> 7, (8, LANES))
        spread = jnp.concatenate(
            [jnp.where(high == above, twice, 0.0), jnp.where(high == above + 2, twice, 0.0)],
            axis=0,
        )
        left.append(jnp.concatenate(three_parts(spread), axis=0))
        hit = jnp.broadcast_to(node & (LANES - 1), (LANES, LANES)) == line
        right.append(jnp.where(hit, 1.0, 0.0).astype(BF16))
    return dot_nt(jnp.concatenate(left, axis=1), jnp.concatenate(right, axis=1))


def split_compliance(compliance, high, middle):
    def step(i, carry):
        t, rows = i // 4, pl.ds(pl.multiple_of((i % 4) * 96, 96), 96)
        value = compliance[t, rows, :]
        top = value.astype(BF16)
        high[t, rows, :] = top
        middle[t, rows, :] = (value - top.astype(F32)).astype(BF16)
        return carry

    lax.fori_loop(0, 16, step, 0)


def tile_response(total, high, middle, moved, displacement):
    sums = total[0:16, :] + total[16:32, :] + total[32:48, :]
    for t in range(4):
        load = jnp.concatenate([sums[t * 4 + c : t * 4 + c + 1, :] for c in range(3)], axis=1)
        parts = jnp.concatenate(
            [jnp.broadcast_to(part, (16, part.shape[1])) for part in three_parts(load)], axis=0
        )
        first = dot_nt(parts, high[t])
        second = dot_nt(parts[0:32], middle[t])
        out = first[0:1] + ((first[16:17] + second[0:1]) + (first[32:33] + second[16:17]))
        for c in range(3):
            row = out[:, c * LANES : (c + 1) * LANES]
            moved[c * 4 + t : c * 4 + t + 1, :] = row
            displacement[c : c + 1, t * LANES : (t + 1) * LANES] = row


def make_replies(g, got, moved, reply):
    rows = pl.ds(pl.multiple_of(g * 8, 8), 8)
    node = got[rows, 3, :].astype(I32)
    low, high = node & (LANES - 1), node >> 7
    for c in range(3):
        total = pick(moved[c * 4 : c * 4 + 1, :], low)
        for t in range(1, 4):
            total = jnp.where(high == t, pick(moved[c * 4 + t : c * 4 + t + 1, :], low), total)
        reply[rows, c, :] = total


def face_motions(g, total, answer, relative, rank):
    total = list(total)
    for f in range(4):
        rows = slice(f * 8, f * 8 + 8)
        slot, peer = rank[rows, :].astype(I32), relative[rows, :]
        for s in range(8):
            hit = peer == g * 8 + s
            for c in range(3):
                row = answer[g * 8 + s, c : c + 1, :]
                total[c * 4 + f] = jnp.where(hit, pick(row, slot), total[c * 4 + f])
    return tuple(total)


def store_motions(total, weight, motion):
    for f in range(4):
        for c in range(3):
            out = total[c * 4 + f] * weight[f * 8 : f * 8 + 8, :]
            for s in range(8):
                at = (f * 8 + s) * LANES
                motion[c : c + 1, at : at + LANES] = out[s : s + 1, :]


EARLY = 12
COMPACT_UNROLL = 16
INPUTS = ("fluid", "base", "jac", "cols", "dt", "send", "fcell", "area", "weight", "route", "fnode", "comp")


def kernel(peers, *refs):
    count = len(INPUTS)
    hbm = dict(zip(INPUTS, refs[:count]))
    residual_out, displacement, motion = refs[count : count + 3]
    refs = refs[count + 3 :]
    v = dict(zip(INPUTS, refs[:count]))
    (
        index, found, sends, arrived, table, halo, relative, onehot, prefix, rank, face_at, scale,
        loads, slab, got, sums, picks, residual, state, pressure, comp_high, comp_middle, moved,
        reply, answer,
        in_sems, out_sem, halo_send, halo_recv, load_send, load_recv, back_send, back_recv,
    ) = refs[count:]
    me = lax.axis_index("dom")
    copies = {
        name: pltpu.make_async_copy(hbm[name], v[name], in_sems.at[i])
        for i, name in enumerate(INPUTS)
    }
    copies["fluid"].start()
    copies["send"].start()
    barrier = pltpu.get_barrier_semaphore()

    def greet(r, carry):
        pl.semaphore_signal(
            barrier, inc=1, device_id={"dom": (me + r) & (peers - 1)}, device_id_type=MESH
        )
        return carry

    lax.fori_loop(1, peers, greet, 0)
    for name in ("route", "fnode", "weight", "area", "cols", "fcell", "jac", "base", "dt", "comp"):
        copies[name].start()
    copies["send"].wait()
    copies["fluid"].wait()
    gather_sends(v["fluid"], v["send"], index, found, sends)
    pl.semaphore_wait(barrier, peers - 1)

    halo_copies = []
    for m in range(6):
        copy = pltpu.make_async_remote_copy(
            src_ref=sends.at[pl.ds(24 * m, 24)],
            dst_ref=arrived.at[5 - m],
            send_sem=halo_send.at[m],
            recv_sem=halo_recv.at[5 - m],
            device_id={"dom": (me + OFFSETS[m] + peers) & (peers - 1)},
            device_id_type=MESH,
        )
        copy.start()
        halo_copies.append(copy)

    shift_table(v["fluid"], table)
    copies["route"].wait()
    rank_faces(me, peers, v["route"], relative, onehot, prefix, rank)
    for name in ("fnode", "weight", "area"):
        copies[name].wait()
    compact_faces(
        peers, onehot, rank, v["fnode"], v["weight"], v["area"], face_at, slab, scale
    )
    copies["cols"].wait()
    early_picks(v["fluid"].shape[1], v["cols"], table, picks)
    for copy in halo_copies:
        copy.wait()
    halo_table(arrived, halo)
    for name in ("jac", "base", "dt", "fcell"):
        copies[name].wait()
    apply_system(
        v["fluid"], v["base"], v["jac"], v["cols"], v["dt"], table, halo, sums, picks, residual, state
    )
    cell_pressures(state, pressure)
    face_loads(pressure, v["fcell"], scale, loads)

    def copy_of(source, target, send_sem, recv_sem, height, slots, to, group):
        rows = pl.ds(0, height)
        return pltpu.make_async_remote_copy(
            src_ref=source.at[slots, rows],
            dst_ref=target.at[slots, rows],
            send_sem=send_sem,
            recv_sem=recv_sem.at[group],
            device_id={"dom": to},
            device_id_type=MESH,
        )

    def send_group(source, target, send_sem, recv_sem, height, sign, group, amount):
        for place in range(amount):
            dz, dy, dc = offset_of(group, place)
            to = (
                (((me >> 3) + sign * dz + 8) & 7) * 8
                + (((me >> 1) + sign * dy + 4) & 3) * 2
                + ((me + dc) & 1)
            )
            slot = group * 8 + place
            copy_of(source, target, send_sem, recv_sem, height, slot, to, group).start()

    def received(source, target, send_sem, recv_sem, height, group, amount):
        slots = pl.ds(group * 8, amount)
        copy_of(source, target, send_sem, recv_sem, height, slots, me ^ 1, group).wait_recv()

    forth = (slab, got, load_send, load_recv, 4)
    back = (reply, answer, back_send, back_recv, 3)

    def send_loads(g, carry):
        fill_slabs(g, loads, face_at, slab)
        send_group(*forth, 1, g, 8)
        return carry

    lax.fori_loop(0, 7, send_loads, 0)
    fill_slabs(7, loads, face_at, slab)
    send_group(*forth, 1, 7, 7)
    got[63] = slab[63]

    apply_rest(v["base"], v["jac"], picks, sums, residual)
    residual_copy = pltpu.make_async_copy(residual, residual_out, out_sem)
    residual_copy.start()
    copies["comp"].wait()
    split_compliance(v["comp"], comp_high, comp_middle)

    received(*forth, 7, 7)
    total = node_sums(7, got)

    def take_loads(i, total):
        received(*forth, 6 - i, 8)
        return total + node_sums(6 - i, got)

    total = lax.fori_loop(0, 7, take_loads, total)
    tile_response(total, comp_high, comp_middle, moved, displacement)

    def send_replies(g, carry):
        make_replies(g, got, moved, reply)
        send_group(*back, -1, g, 8)
        return carry

    lax.fori_loop(0, 7, send_replies, 0)
    make_replies(7, got, moved, reply)
    send_group(*back, -1, 7, 7)
    answer[63] = reply[63]

    received(*back, 7, 7)
    motions = face_motions(7, (jnp.zeros((8, LANES), F32),) * 12, answer, relative, rank)

    def take_replies(i, total):
        received(*back, 6 - i, 8)
        return face_motions(6 - i, total, answer, relative, rank)

    motions = lax.fori_loop(0, 7, take_replies, motions)
    store_motions(motions, v["weight"], motion)
    for way in (forth, back):
        copy_of(*way, pl.ds(0, 63), me ^ 1, 0).wait_send()
    residual_copy.wait()


def per_device(
    fluid_state,
    residual_base,
    jacobian,
    columns,
    pseudo_step,
    send_cells,
    interface_face_cell,
    interface_face_area_vector,
    mortar_weight,
    face_route,
    face_node,
    compliance,
):
    peers = lax.axis_size("dom")
    operands = (
        fluid_state,
        residual_base,
        jnp.transpose(jacobian, (1, 2, 0, 3)),
        columns,
        pseudo_step.reshape(-1, LANES),
        send_cells,
        interface_face_cell.reshape(-1, LANES),
        interface_face_area_vector,
        mortar_weight.reshape(-1, LANES),
        face_route.reshape(-1, LANES),
        face_node.reshape(-1, LANES),
        compliance,
    )
    vmem = pltpu.VMEM
    dma = pltpu.SemaphoreType.DMA
    scratch = [vmem(x.shape, x.dtype) for x in operands] + [
        vmem((24, LANES), I32),
        vmem((5, 24, LANES), F32),
        vmem((192, LANES), F32),
        vmem((6, 24, LANES), F32),
        vmem((129, 8, LANES), F32),
        vmem((5, 32, LANES), F32),
        vmem((32, LANES), I32),
        vmem((32 * peers, LANES), BF16),
        vmem((32 * peers, 2 * LANES), F32),
        vmem((32, LANES), F32),
        vmem((peers, LANES), I32),
        vmem((96, LANES), F32),
        vmem((96, LANES), F32),
        vmem((peers, 4, LANES), F32),
        vmem((peers, 4, LANES), F32),
        vmem((4, 40, LANES), F32),
        vmem((5, 128, 8, LANES), F32),
        vmem(fluid_state.shape, F32),
        vmem((1024, LANES), F32),
        vmem((LANES, LANES), F32),
        vmem(compliance.shape, BF16),
        vmem(compliance.shape, BF16),
        vmem((16, LANES), F32),
        vmem((peers, 4, LANES), F32),
        vmem((peers, 4, LANES), F32),
        dma((len(INPUTS),)),
        dma,
        dma((6,)),
        dma((6,)),
        dma,
        dma((8,)),
        dma,
        dma((8,)),
    ]
    results = pl.pallas_call(
        functools.partial(kernel, peers),
        out_shape=(
            jax.ShapeDtypeStruct(fluid_state.shape, F32),
            jax.ShapeDtypeStruct((3, compliance.shape[0] * LANES), F32),
            jax.ShapeDtypeStruct(interface_face_area_vector.shape, F32),
        ),
        in_specs=[pl.BlockSpec(memory_space=pl.ANY)] * len(operands),
        out_specs=(
            pl.BlockSpec(memory_space=pl.ANY),
            pl.BlockSpec(memory_space=vmem),
            pl.BlockSpec(memory_space=vmem),
        ),
        scratch_shapes=scratch,
        compiler_params=pltpu.CompilerParams(
            collective_id=0, has_side_effects=True, vmem_limit_bytes=56 * 1024 * 1024
        ),
    )(*operands)
    return hand_over(*results)


def hand_over_kernel(*refs):
    sources, targets, holds, (sems_in, sems_out) = refs[:3], refs[3:6], refs[6:9], refs[9:]
    pieces = []
    for which, count in ((0, 4), (1, 1), (2, 1)):
        width = sources[which].shape[1] // count
        for piece in range(count):
            at = (slice(None), pl.ds(piece * width, width))
            n = len(pieces)
            pieces.append(
                (
                    pltpu.make_async_copy(
                        sources[which].at[at], holds[which].at[at], sems_in.at[n]
                    ),
                    pltpu.make_async_copy(
                        holds[which].at[at], targets[which].at[at], sems_out.at[n]
                    ),
                )
            )
    for copy_in, _ in pieces:
        copy_in.start()
    for copy_in, copy_out in pieces:
        copy_in.wait()
        copy_out.start()
    for _, copy_out in pieces:
        copy_out.wait()


def hand_over(*results):
    return pl.pallas_call(
        hand_over_kernel,
        out_shape=[jax.ShapeDtypeStruct(x.shape, x.dtype) for x in results],
        in_specs=[pl.BlockSpec(memory_space=pl.ANY)] * 3,
        out_specs=[pl.BlockSpec(memory_space=pl.ANY)] * 3,
        scratch_shapes=[pltpu.VMEM(x.shape, x.dtype) for x in results]
        + [pltpu.SemaphoreType.DMA((6,))] * 2,
        compiler_params=pltpu.CompilerParams(vmem_limit_bytes=60 * 1024 * 1024),
    )(*results)


def solution(mesh):
    return jax.shard_map(
        per_device,
        mesh=mesh,
        in_specs=(
            P(None, ("sweep", "dom")),
            P(None, ("sweep", "dom")),
            P(None, None, None, ("sweep", "dom")),
            P(None, ("sweep", "dom")),
            P(("sweep", "dom")),
            P(("sweep", "dom"), None),
            P(("sweep", "dom")),
            P(None, ("sweep", "dom")),
            P(("sweep", "dom")),
            P(("sweep", "dom"), None),
            P(("sweep", "dom")),
            P(("sweep", "dom"), None, None),
        ),
        out_specs=(P(None, ("sweep", "dom")), P(None, ("sweep", "dom")), P(None, ("sweep", "dom"))),
        check_vma=False,
    )
```

```python
import functools

import jax
import jax.numpy as jnp
from jax import lax
from jax.experimental import pallas as pl
from jax.experimental.pallas import tpu as pltpu
from jax.sharding import PartitionSpec as P

MESH = pl.DeviceIdType.MESH
OFFSETS = (-3, -2, -1, 1, 2, 3)
HIGH = lax.Precision.HIGHEST
F32 = jnp.float32
BF16 = jnp.bfloat16
I32 = jnp.int32
LANES = 128


def pick(row, where_at):
    return jnp.take_along_axis(
        jnp.broadcast_to(row, where_at.shape), where_at, axis=1, mode="promise_in_bounds"
    )


def iota(shape, dim):
    return lax.broadcasted_iota(I32, shape, dim)


def lanes(block):
    return pl.ds(pl.multiple_of(block * LANES, LANES), LANES)


def three_parts(value):
    high = value.astype(BF16)
    rest = value - high.astype(F32)
    middle = rest.astype(BF16)
    low = (rest - middle.astype(F32)).astype(BF16)
    return high, middle, low


def dot_nt(a, b, precision=None):
    return lax.dot_general(
        a, b, (((1,), (1,)), ((), ())), precision=precision, preferred_element_type=F32
    )


def offset_of(group, place):
    side = place // 2
    dz = 4 + (1 - 2 * (group % 2)) * ((group + 1) // 2)
    dy = 2 + (1 - 2 * (side % 2)) * ((side + 1) // 2)
    return dz, dy, 1 - place % 2


def slot_of(me, route):
    dz = ((route >> 3) - (me >> 3)) & 7
    dy = ((route >> 1) - (me >> 1)) & 3
    dc = (route - me) & 1
    group = jnp.where(dz < 4, 7 - 2 * dz, 2 * dz - 8)
    side = jnp.where(dy < 2, 3 - 2 * dy, 2 * dy - 4)
    return group * 8 + side * 2 + (1 - dc)


def gather_sends(fluid, send, index, found, out):
    for k in range(4):
        index[pl.ds(k, 6, stride=4), :] = send[:, k * LANES : (k + 1) * LANES]

    def part(g, carry):
        rows = pl.ds(pl.multiple_of(g * 8, 8), 8)
        cell = index[rows, :]
        low, high = cell & (LANES - 1), cell >> 7

        def step(block, total):
            hit = high == block
            return tuple(
                jnp.where(hit, pick(fluid[pl.ds(c, 1), lanes(block)], low), total[c])
                for c in range(5)
            )

        total = lax.fori_loop(0, 128, step, (jnp.zeros((8, LANES), F32),) * 5, unroll=128)
        for c in range(5):
            found[c, rows, :] = total[c]
        return carry

    lax.fori_loop(0, 3, part, 0)
    for m in range(6):
        for c in range(5):
            out[m * 24 + c * 4 : m * 24 + c * 4 + 4, :] = found[c, m * 4 : m * 4 + 4, :]


def shift_table(fluid, table):
    left = iota((5, LANES), 1) < 64

    def step(block, before):
        here = pltpu.roll(fluid[:, lanes(block)], 64, 1)
        table[block, 0:5, :] = jnp.where(left, before, here)
        return here

    last = lax.fori_loop(0, 128, step, jnp.zeros((5, LANES), F32), unroll=32)
    table[128, 0:5, :] = last


def rank_faces(me, peers, route, relative, onehot, prefix, rank):
    relative[...] = slot_of(me, route[...])
    line = iota((peers, LANES), 0)
    for i in range(32):
        hit = jnp.broadcast_to(relative[i : i + 1, :], (peers, LANES)) == line
        onehot[i * peers : (i + 1) * peers, :] = jnp.where(hit, 1.0, 0.0).astype(BF16)
    upto = jnp.where(iota((LANES, LANES), 0) <= iota((LANES, LANES), 1), 1.0, 0.0)
    weights = jnp.concatenate([upto, jnp.ones((LANES, LANES), F32)], axis=1).astype(BF16)

    def count(part, carry):
        rows = pl.ds(pl.multiple_of(part * 512, 512), 512)
        prefix[rows, :] = jnp.dot(onehot[rows, :], weights, preferred_element_type=F32)
        return carry

    lax.fori_loop(0, 32 * peers // 512, count, 0)

    def step(i, before):
        rows = pl.ds(pl.multiple_of(i * peers, peers), peers)
        hit = onehot[rows, :].astype(F32)
        here = prefix[rows, 0:LANES] + before
        rank[pl.ds(i, 1), :] = jnp.sum(hit * here, axis=0, keepdims=True) - 1.0
        return before + prefix[rows, LANES : 2 * LANES]

    lax.fori_loop(0, 32, step, jnp.zeros((peers, LANES), F32), unroll=2)


def compact_faces(peers, onehot, rank, fnode, weight, area, face_at, slab, scale):
    line = iota((LANES, LANES), 0).astype(F32)
    lane = iota((peers, LANES), 1).astype(F32)

    def step(pair, total):
        left, right = [], []
        for half in range(2):
            i = pair * 2 + half
            hit = onehot[pl.ds(pl.multiple_of(i * peers, peers), peers), :].astype(F32)
            left.append(
                jnp.concatenate(
                    [hit * (i + 1).astype(F32), hit * lane], axis=0
                ).astype(BF16)
            )
            place = jnp.broadcast_to(rank[pl.ds(i, 1), :], (LANES, LANES)) == line
            right.append(jnp.where(place, 1.0, 0.0).astype(BF16))
        return total + dot_nt(jnp.concatenate(left, axis=1), jnp.concatenate(right, axis=1))

    found = lax.fori_loop(0, 16, step, jnp.zeros((2 * peers, LANES), F32), unroll=COMPACT_UNROLL)
    high = found[0:peers, :].astype(I32) - 1
    low = found[peers : 2 * peers, :].astype(I32)
    face_at[...] = (high << 7) + low

    def part(g, carry):
        rows = pl.ds(pl.multiple_of(g * 8, 8), 8)
        face = face_at[rows, :]
        h, l = face >> 7, face & (LANES - 1)

        def look(i, total):
            return jnp.where(h == i, pick(fnode[pl.ds(i, 1), :], l), total)

        node = lax.fori_loop(0, 32, look, jnp.zeros((8, LANES), I32), unroll=32)
        slab[rows, 3, :] = node.astype(F32)
        return carry

    lax.fori_loop(0, peers // 8, part, 0, unroll=2)

    def weigh(i, carry):
        scale[pl.ds(i, 3, stride=32), :] = weight[pl.ds(i, 1), :] * area[:, lanes(i)]
        return carry

    lax.fori_loop(0, 32, weigh, 0, unroll=8)


def halo_table(arrived, table):
    line, lane = iota((8, LANES), 0), iota((8, LANES), 1)
    where_at = line * 16 + (lane & 15)
    for c in range(5):
        for quarter in range(4):
            total = jnp.zeros((8, LANES), F32)
            for n in range(6):
                got = pick(arrived[n, c * 4 + quarter : c * 4 + quarter + 1, :], where_at)
                total = jnp.where((lane >> 4) == n, got, total)
            table[c, quarter * 8 : quarter * 8 + 8, :] = total


def window(cols, cells, q, j):
    col = cols[:, lanes(q * 4 + j)]
    shifted = col + 64 - q * 512
    far = col - cells
    far_at = (far >> 9) * 16 + (far & 511) - q * 16
    inside = col < cells
    where_at = jnp.where(inside, shifted, far_at) & (LANES - 1)
    return where_at, jnp.where(inside, shifted >> 7, 5)


def pick_local(c, where_at, chunk, table, q):
    total = pick(table[q * 4, c : c + 1, :], where_at)
    for k in range(1, 5):
        got = pick(table[q * 4 + k, c : c + 1, :], where_at)
        total = jnp.where(chunk == k, got, total)
    return total


def early_picks(cells, cols, table, picks):
    def step(q, carry):
        for j in range(4):
            where_at, chunk = window(cols, cells, q, j)
            for c in range(5):
                picks[c, q * 4 + j, 0:7, :] = pick_local(c, where_at, chunk, table, q)
        return carry

    lax.fori_loop(0, EARLY, step, 0, unroll=6)


def apply_system(fluid, base, jac, cols, dt, table, halo, sums, picks, residual, state):
    cells = fluid.shape[1]
    sums[...] = jnp.zeros(sums.shape, F32)

    def step(q, carry, early):
        for j in range(4):
            where_at, chunk = window(cols, cells, q, j)
            block = q * 4 + j
            at = lanes(block)
            picked = []
            for c in range(5):
                if early:
                    total = picks[c, block, 0:7, :]
                else:
                    total = pick_local(c, where_at, chunk, table, q)
                got = pick(halo[c, pl.ds(q, 1), :], where_at)
                picked.append(jnp.where(chunk == 5, got, total))
            for c in range(5):
                picks[c, block, 0:7, :] = picked[c]
            for r in (0, 1, 4):
                total = jac[r, 0, :, at].astype(F32) * picked[0]
                for c in range(1, 5):
                    total = total + jac[r, c, :, at].astype(F32) * picked[c]
                sums[j, r * 8 : r * 8 + 7, :] = total
            coupled = sums[j, pl.ds(0, 5, stride=8), :]
            for b in range(1, 7):
                coupled = coupled + sums[j, pl.ds(b, 5, stride=8), :]
            left = base[:, at] - coupled
            residual[:, at] = left
            state[pl.ds(pl.multiple_of(block * 8, 8), 5), :] = (
                fluid[:, at] + dt[pl.ds(block, 1), :] * left
            )
        return carry

    lax.fori_loop(0, EARLY, functools.partial(step, early=True), 0, unroll=6)
    lax.fori_loop(EARLY, cells // 512, functools.partial(step, early=False), 0, unroll=10)


def apply_rest(base, jac, picks, sums, residual):
    def step(quad, carry):
        for j in range(4):
            block = quad * 4 + j
            at = lanes(block)
            for r in (2, 3):
                total = jac[r, 0, :, at].astype(F32) * picks[0, block, 0:7, :]
                for c in range(1, 5):
                    total = total + jac[r, c, :, at].astype(F32) * picks[c, block, 0:7, :]
                sums[j, r * 8 : r * 8 + 7, :] = total
            coupled = sums[j, pl.ds(0, 5, stride=8), :]
            for b in range(1, 7):
                coupled = coupled + sums[j, pl.ds(b, 5, stride=8), :]
            residual[2:4, at] = (base[:, at] - coupled)[2:4, :]
        return carry

    lax.fori_loop(0, 32, step, 0)


def cell_pressures(state, pressure):
    def step(i, carry):
        first = pl.multiple_of(i * 64, 64)
        p0, p1, p4 = (state[pl.ds(first + r, 8, stride=8), :] for r in (0, 1, 4))
        pressure[pl.ds(pl.multiple_of(i * 8, 8), 8), :] = 0.4 * (p4 - 0.8 * p1 + 0.32 * p0)
        return carry

    lax.fori_loop(0, 16, step, 0, unroll=4)


def face_loads(pressure, fcell, scale, loads):
    def part(g, carry):
        first = pl.multiple_of(g * 8, 8)
        cell = fcell[pl.ds(first, 8), :]
        low, high = cell & (LANES - 1), cell >> 7

        def step(i, total):
            return jnp.where(high == i, pick(pressure[pl.ds(i, 1), :], low), total)

        found = lax.fori_loop(0, 128, step, jnp.zeros((8, LANES), F32), unroll=128)
        for c in range(3):
            rows = pl.ds(first + c * 32, 8)
            loads[rows, :] = scale[rows, :] * found
        return carry

    lax.fori_loop(0, 4, part, 0, unroll=2)


def fill_slabs(g, loads, face_at, slab):
    rows = pl.ds(pl.multiple_of(g * 8, 8), 8)
    face = face_at[rows, :]
    h, l = face >> 7, face & (LANES - 1)

    def look(i, total):
        hit = h == i
        return tuple(
            jnp.where(hit, pick(loads[pl.ds(c * 32 + i, 1), :], l), total[c]) for c in range(3)
        )

    total = lax.fori_loop(0, 32, look, (jnp.zeros((8, LANES), F32),) * 3, unroll=32)
    for c in range(3):
        slab[rows, c, :] = total[c]


def node_sums(groups, got):
    line = iota((LANES, LANES), 0)
    above = iota((8, LANES), 0) >> 2
    total = jnp.zeros((48, LANES), F32)
    for g in groups:
        left, right = [], []
        for s in range(8):
            piece = got[g * 8 + s]
            node = piece[3:4, :].astype(I32)
            twice = jnp.concatenate([piece, piece], axis=0)
            high = jnp.broadcast_to(node >> 7, (8, LANES))
            spread = jnp.concatenate(
                [jnp.where(high == above, twice, 0.0), jnp.where(high == above + 2, twice, 0.0)],
                axis=0,
            )
            left.append(jnp.concatenate(three_parts(spread), axis=0))
            hit = jnp.broadcast_to(node & (LANES - 1), (LANES, LANES)) == line
            right.append(jnp.where(hit, 1.0, 0.0).astype(BF16))
        total = total + dot_nt(jnp.concatenate(left, axis=1), jnp.concatenate(right, axis=1))
    return total


def split_compliance(compliance, high, middle):
    def step(i, carry):
        t, rows = i // 4, pl.ds(pl.multiple_of((i % 4) * 96, 96), 96)
        value = compliance[t, rows, :]
        top = value.astype(BF16)
        high[t, rows, :] = top
        middle[t, rows, :] = (value - top.astype(F32)).astype(BF16)
        return carry

    lax.fori_loop(0, 16, step, 0)


def tile_response(total, high, middle, moved, displacement):
    sums = total[0:16, :] + total[16:32, :] + total[32:48, :]
    for t in range(4):
        load = jnp.concatenate([sums[t * 4 + c : t * 4 + c + 1, :] for c in range(3)], axis=1)
        top, rest, last = (
            jnp.broadcast_to(part.astype(F32), (16, part.shape[1])) for part in three_parts(load)
        )
        line = iota(top.shape, 0)
        parts = jnp.where(line == 0, top, jnp.where(line == 1, rest, last)).astype(BF16)
        first = dot_nt(parts, high[t])
        second = dot_nt(parts, middle[t])
        out = first[0:1] + ((first[1:2] + second[0:1]) + (first[2:3] + second[1:2]))
        for c in range(3):
            row = out[:, c * LANES : (c + 1) * LANES]
            moved[c * 4 + t : c * 4 + t + 1, :] = row
            displacement[c : c + 1, t * LANES : (t + 1) * LANES] = row


def make_replies(g, got, moved, reply):
    rows = pl.ds(pl.multiple_of(g * 8, 8), 8)
    node = got[rows, 3, :].astype(I32)
    low, high = node & (LANES - 1), node >> 7
    for c in range(3):
        total = pick(moved[c * 4 : c * 4 + 1, :], low)
        for t in range(1, 4):
            total = jnp.where(high == t, pick(moved[c * 4 + t : c * 4 + t + 1, :], low), total)
        reply[rows, c, :] = total


def face_motions(groups, total, answer, relative, rank):
    total = list(total)
    for f in range(4):
        rows = slice(f * 8, f * 8 + 8)
        slot, peer = rank[rows, :].astype(I32), relative[rows, :]
        for g in groups:
            for s in range(8):
                hit = peer == g * 8 + s
                for c in range(3):
                    row = answer[g * 8 + s, c : c + 1, :]
                    total[c * 4 + f] = jnp.where(hit, pick(row, slot), total[c * 4 + f])
    return tuple(total)


def store_motions(total, weight, motion):
    for f in range(4):
        for c in range(3):
            out = total[c * 4 + f] * weight[f * 8 : f * 8 + 8, :]
            for s in range(8):
                at = (f * 8 + s) * LANES
                motion[c : c + 1, at : at + LANES] = out[s : s + 1, :]


EARLY = 12
BATCHES = ((7, 6, 5, 4), (3, 2, 1, 0))
COMPACT_UNROLL = 16
INPUTS = ("fluid", "base", "jac", "cols", "dt", "send", "fcell", "area", "weight", "route", "fnode", "comp")


def kernel(peers, *refs):
    count = len(INPUTS)
    hbm = dict(zip(INPUTS, refs[:count]))
    residual_out, displacement, motion = refs[count : count + 3]
    refs = refs[count + 3 :]
    v = dict(zip(INPUTS, refs[:count]))
    (
        index, found, sends, arrived, table, halo, relative, onehot, prefix, rank, face_at, scale,
        loads, slab, got, sums, picks, residual, state, pressure, comp_high, comp_middle, moved,
        reply, answer,
        in_sems, out_sem, halo_send, halo_recv, load_send, load_recv, back_send, back_recv,
    ) = refs[count:]
    me = lax.axis_index("dom")
    copies = {
        name: pltpu.make_async_copy(hbm[name], v[name], in_sems.at[i])
        for i, name in enumerate(INPUTS)
    }
    copies["fluid"].start()
    copies["send"].start()
    barrier = pltpu.get_barrier_semaphore()


    def peer_at(slot, sign):
        dz, dy, dc = offset_of(slot // 8, slot % 8)
        return (
            (((me >> 3) + sign * dz + 8) & 7) * 8
            + (((me >> 1) + sign * dy + 4) & 3) * 2
            + ((me + dc) & 1)
        )

    for slot in range(peers - 1):
        pl.semaphore_signal(
            barrier, inc=1, device_id={"dom": peer_at(slot, 1)}, device_id_type=MESH
        )
    for name in ("route", "fnode", "weight", "area", "cols", "fcell", "jac", "base", "dt", "comp"):
        copies[name].start()
    copies["send"].wait()
    copies["fluid"].wait()
    gather_sends(v["fluid"], v["send"], index, found, sends)
    pl.semaphore_wait(barrier, peers - 1)

    halo_copies = []
    for m in range(6):
        copy = pltpu.make_async_remote_copy(
            src_ref=sends.at[pl.ds(24 * m, 24)],
            dst_ref=arrived.at[5 - m],
            send_sem=halo_send.at[m],
            recv_sem=halo_recv.at[5 - m],
            device_id={"dom": (me + OFFSETS[m] + peers) & (peers - 1)},
            device_id_type=MESH,
        )
        copy.start()
        halo_copies.append(copy)

    shift_table(v["fluid"], table)
    copies["route"].wait()
    rank_faces(me, peers, v["route"], relative, onehot, prefix, rank)
    for name in ("fnode", "weight", "area"):
        copies[name].wait()
    compact_faces(
        peers, onehot, rank, v["fnode"], v["weight"], v["area"], face_at, slab, scale
    )
    copies["cols"].wait()
    early_picks(v["fluid"].shape[1], v["cols"], table, picks)
    for copy in halo_copies:
        copy.wait()
    halo_table(arrived, halo)
    for name in ("jac", "base", "dt", "fcell"):
        copies[name].wait()
    apply_system(
        v["fluid"], v["base"], v["jac"], v["cols"], v["dt"], table, halo, sums, picks, residual, state
    )
    cell_pressures(state, pressure)
    face_loads(pressure, v["fcell"], scale, loads)

    def copy_of(source, target, send_sem, recv_sem, height, slots, to, group):
        rows = pl.ds(0, height)
        return pltpu.make_async_remote_copy(
            src_ref=source.at[slots, rows],
            dst_ref=target.at[slots, rows],
            send_sem=send_sem,
            recv_sem=recv_sem.at[group],
            device_id={"dom": to},
            device_id_type=MESH,
        )

    def send_group(source, target, send_sem, recv_sem, height, sign, group, amount):
        for place in range(amount):
            slot = group * 8 + place
            to = peer_at(slot, sign)
            copy_of(source, target, send_sem, recv_sem, height, slot, to, group).start()

    def received(source, target, send_sem, recv_sem, height, group, amount):
        slots = pl.ds(group * 8, amount)
        copy_of(source, target, send_sem, recv_sem, height, slots, me ^ 1, group).wait_recv()

    forth = (slab, got, load_send, load_recv, 4)
    back = (reply, answer, back_send, back_recv, 3)

    def send_loads(g, carry):
        fill_slabs(g, loads, face_at, slab)
        send_group(*forth, 1, g, 8)
        return carry

    lax.fori_loop(0, 7, send_loads, 0)
    fill_slabs(7, loads, face_at, slab)
    send_group(*forth, 1, 7, 7)
    got[63] = slab[63]

    apply_rest(v["base"], v["jac"], picks, sums, residual)
    residual_copy = pltpu.make_async_copy(residual, residual_out, out_sem)
    residual_copy.start()
    copies["comp"].wait()
    split_compliance(v["comp"], comp_high, comp_middle)

    total = jnp.zeros((48, LANES), F32)
    for groups in BATCHES:
        for g in groups:
            received(*forth, g, 8 if g < 7 else 7)
        total = total + node_sums(groups, got)
    tile_response(total, comp_high, comp_middle, moved, displacement)

    def send_replies(g, carry):
        make_replies(g, got, moved, reply)
        send_group(*back, -1, g, 8)
        return carry

    lax.fori_loop(0, 7, send_replies, 0)
    make_replies(7, got, moved, reply)
    send_group(*back, -1, 7, 7)
    answer[63] = reply[63]

    motions = (jnp.zeros((8, LANES), F32),) * 12
    for groups in BATCHES:
        for g in groups:
            received(*back, g, 8 if g < 7 else 7)
        motions = face_motions(groups, motions, answer, relative, rank)
    store_motions(motions, v["weight"], motion)
    for way in (forth, back):
        copy_of(*way, pl.ds(0, 63), me ^ 1, 0).wait_send()
    residual_copy.wait()


def per_device(
    fluid_state,
    residual_base,
    jacobian,
    columns,
    pseudo_step,
    send_cells,
    interface_face_cell,
    interface_face_area_vector,
    mortar_weight,
    face_route,
    face_node,
    compliance,
):
    peers = lax.axis_size("dom")
    operands = (
        fluid_state,
        residual_base,
        jnp.transpose(jacobian, (1, 2, 0, 3)),
        columns,
        pseudo_step.reshape(-1, LANES),
        send_cells,
        interface_face_cell.reshape(-1, LANES),
        interface_face_area_vector,
        mortar_weight.reshape(-1, LANES),
        face_route.reshape(-1, LANES),
        face_node.reshape(-1, LANES),
        compliance,
    )
    vmem = pltpu.VMEM
    dma = pltpu.SemaphoreType.DMA
    scratch = [vmem(x.shape, x.dtype) for x in operands] + [
        vmem((24, LANES), I32),
        vmem((5, 24, LANES), F32),
        vmem((192, LANES), F32),
        vmem((6, 24, LANES), F32),
        vmem((129, 8, LANES), F32),
        vmem((5, 32, LANES), F32),
        vmem((32, LANES), I32),
        vmem((32 * peers, LANES), BF16),
        vmem((32 * peers, 2 * LANES), F32),
        vmem((32, LANES), F32),
        vmem((peers, LANES), I32),
        vmem((96, LANES), F32),
        vmem((96, LANES), F32),
        vmem((peers, 4, LANES), F32),
        vmem((peers, 4, LANES), F32),
        vmem((4, 40, LANES), F32),
        vmem((5, 128, 8, LANES), F32),
        vmem(fluid_state.shape, F32),
        vmem((1024, LANES), F32),
        vmem((LANES, LANES), F32),
        vmem(compliance.shape, BF16),
        vmem(compliance.shape, BF16),
        vmem((16, LANES), F32),
        vmem((peers, 4, LANES), F32),
        vmem((peers, 4, LANES), F32),
        dma((len(INPUTS),)),
        dma,
        dma((6,)),
        dma((6,)),
        dma,
        dma((8,)),
        dma,
        dma((8,)),
    ]
    results = pl.pallas_call(
        functools.partial(kernel, peers),
        out_shape=(
            jax.ShapeDtypeStruct(fluid_state.shape, F32),
            jax.ShapeDtypeStruct((3, compliance.shape[0] * LANES), F32),
            jax.ShapeDtypeStruct(interface_face_area_vector.shape, F32),
        ),
        in_specs=[pl.BlockSpec(memory_space=pl.ANY)] * len(operands),
        out_specs=(
            pl.BlockSpec(memory_space=pl.ANY),
            pl.BlockSpec(memory_space=vmem),
            pl.BlockSpec(memory_space=vmem),
        ),
        scratch_shapes=scratch,
        compiler_params=pltpu.CompilerParams(
            collective_id=0, has_side_effects=True, vmem_limit_bytes=56 * 1024 * 1024
        ),
    )(*operands)
    return hand_over(*results)


def hand_over_kernel(*refs):
    sources, targets, holds, (sems_in, sems_out) = refs[:3], refs[3:6], refs[6:9], refs[9:]
    pieces = []
    for which, count in ((0, 4), (1, 1), (2, 1)):
        width = sources[which].shape[1] // count
        for piece in range(count):
            at = (slice(None), pl.ds(piece * width, width))
            n = len(pieces)
            pieces.append(
                (
                    pltpu.make_async_copy(
                        sources[which].at[at], holds[which].at[at], sems_in.at[n]
                    ),
                    pltpu.make_async_copy(
                        holds[which].at[at], targets[which].at[at], sems_out.at[n]
                    ),
                )
            )
    for copy_in, _ in pieces:
        copy_in.start()
    for copy_in, copy_out in pieces:
        copy_in.wait()
        copy_out.start()
    for _, copy_out in pieces:
        copy_out.wait()


def hand_over(*results):
    return pl.pallas_call(
        hand_over_kernel,
        out_shape=[jax.ShapeDtypeStruct(x.shape, x.dtype) for x in results],
        in_specs=[pl.BlockSpec(memory_space=pl.ANY)] * 3,
        out_specs=[pl.BlockSpec(memory_space=pl.ANY)] * 3,
        scratch_shapes=[pltpu.VMEM(x.shape, x.dtype) for x in results]
        + [pltpu.SemaphoreType.DMA((6,))] * 2,
        compiler_params=pltpu.CompilerParams(vmem_limit_bytes=60 * 1024 * 1024),
    )(*results)


def solution(mesh):
    return jax.shard_map(
        per_device,
        mesh=mesh,
        in_specs=(
            P(None, ("sweep", "dom")),
            P(None, ("sweep", "dom")),
            P(None, None, None, ("sweep", "dom")),
            P(None, ("sweep", "dom")),
            P(("sweep", "dom")),
            P(("sweep", "dom"), None),
            P(("sweep", "dom")),
            P(None, ("sweep", "dom")),
            P(("sweep", "dom")),
            P(("sweep", "dom"), None),
            P(("sweep", "dom")),
            P(("sweep", "dom"), None, None),
        ),
        out_specs=(P(None, ("sweep", "dom")), P(None, ("sweep", "dom")), P(None, ("sweep", "dom"))),
        check_vma=False,
    )
```

```python
import functools

import jax
import jax.numpy as jnp
from jax import lax
from jax.experimental import pallas as pl
from jax.experimental.pallas import tpu as pltpu
from jax.sharding import PartitionSpec as P

MESH = pl.DeviceIdType.MESH
OFFSETS = (-3, -2, -1, 1, 2, 3)
HIGH = lax.Precision.HIGHEST
F32 = jnp.float32
BF16 = jnp.bfloat16
I32 = jnp.int32
LANES = 128


def pick(row, where_at):
    return jnp.take_along_axis(
        jnp.broadcast_to(row, where_at.shape), where_at, axis=1, mode="promise_in_bounds"
    )


def iota(shape, dim):
    return lax.broadcasted_iota(I32, shape, dim)


def lanes(block):
    return pl.ds(pl.multiple_of(block * LANES, LANES), LANES)


def three_parts(value):
    high = value.astype(BF16)
    rest = value - high.astype(F32)
    middle = rest.astype(BF16)
    low = (rest - middle.astype(F32)).astype(BF16)
    return high, middle, low


def dot_nt(a, b, precision=None):
    return lax.dot_general(
        a, b, (((1,), (1,)), ((), ())), precision=precision, preferred_element_type=F32
    )


def offset_of(group, place):
    side = place // 2
    dz = 4 + (1 - 2 * (group % 2)) * ((group + 1) // 2)
    dy = 2 + (1 - 2 * (side % 2)) * ((side + 1) // 2)
    return dz, dy, 1 - place % 2


def slot_of(me, route):
    dz = ((route >> 3) - (me >> 3)) & 7
    dy = ((route >> 1) - (me >> 1)) & 3
    dc = (route - me) & 1
    group = jnp.where(dz < 4, 7 - 2 * dz, 2 * dz - 8)
    side = jnp.where(dy < 2, 3 - 2 * dy, 2 * dy - 4)
    return group * 8 + side * 2 + (1 - dc)


def gather_sends(fluid, send, index, found, out):
    for k in range(4):
        index[pl.ds(k, 6, stride=4), :] = send[:, k * LANES : (k + 1) * LANES]

    def part(g, carry):
        rows = pl.ds(pl.multiple_of(g * 8, 8), 8)
        cell = index[rows, :]
        low, high = cell & (LANES - 1), cell >> 7

        def step(block, total):
            hit = high == block
            return tuple(
                jnp.where(hit, pick(fluid[pl.ds(c, 1), lanes(block)], low), total[c])
                for c in range(5)
            )

        total = lax.fori_loop(0, 128, step, (jnp.zeros((8, LANES), F32),) * 5, unroll=128)
        for c in range(5):
            found[c, rows, :] = total[c]
        return carry

    lax.fori_loop(0, 3, part, 0)
    for m in range(6):
        for c in range(5):
            out[m * 24 + c * 4 : m * 24 + c * 4 + 4, :] = found[c, m * 4 : m * 4 + 4, :]


def shift_table(fluid, table):
    left = iota((5, LANES), 1) < 64

    def step(block, before):
        here = pltpu.roll(fluid[:, lanes(block)], 64, 1)
        table[block, 0:5, :] = jnp.where(left, before, here)
        return here

    last = lax.fori_loop(0, 128, step, jnp.zeros((5, LANES), F32), unroll=32)
    table[128, 0:5, :] = last


def rank_faces(me, peers, route, relative, onehot, prefix, rank):
    relative[...] = slot_of(me, route[...])
    line = iota((peers, LANES), 0)
    for i in range(32):
        hit = jnp.broadcast_to(relative[i : i + 1, :], (peers, LANES)) == line
        onehot[i * peers : (i + 1) * peers, :] = jnp.where(hit, 1.0, 0.0).astype(BF16)
    upto = jnp.where(iota((LANES, LANES), 0) <= iota((LANES, LANES), 1), 1.0, 0.0)
    weights = jnp.concatenate([upto, jnp.ones((LANES, LANES), F32)], axis=1).astype(BF16)

    def count(part, carry):
        rows = pl.ds(pl.multiple_of(part * 512, 512), 512)
        prefix[rows, :] = jnp.dot(onehot[rows, :], weights, preferred_element_type=F32)
        return carry

    lax.fori_loop(0, 32 * peers // 512, count, 0, unroll=4)

    def step(i, before):
        rows = pl.ds(pl.multiple_of(i * peers, peers), peers)
        hit = onehot[rows, :].astype(F32)
        here = prefix[rows, 0:LANES] + before
        rank[pl.ds(i, 1), :] = jnp.sum(hit * here, axis=0, keepdims=True) - 1.0
        return before + prefix[rows, LANES : 2 * LANES]

    lax.fori_loop(0, 32, step, jnp.zeros((peers, LANES), F32), unroll=16)


def compact_faces(peers, onehot, rank, fnode, weight, area, face_at, slab, scale):
    line = iota((LANES, LANES), 0).astype(F32)
    lane = iota((peers, LANES), 1).astype(F32)

    def step(pair, total):
        left, right = [], []
        for half in range(2):
            i = pair * 2 + half
            hit = onehot[pl.ds(pl.multiple_of(i * peers, peers), peers), :].astype(F32)
            left.append(
                jnp.concatenate(
                    [hit * (i + 1).astype(F32), hit * lane], axis=0
                ).astype(BF16)
            )
            place = jnp.broadcast_to(rank[pl.ds(i, 1), :], (LANES, LANES)) == line
            right.append(jnp.where(place, 1.0, 0.0).astype(BF16))
        return total + dot_nt(jnp.concatenate(left, axis=1), jnp.concatenate(right, axis=1))

    found = lax.fori_loop(0, 16, step, jnp.zeros((2 * peers, LANES), F32), unroll=COMPACT_UNROLL)
    high = found[0:peers, :].astype(I32) - 1
    low = found[peers : 2 * peers, :].astype(I32)
    face_at[...] = (high << 7) + low

    def part(g, carry):
        rows = pl.ds(pl.multiple_of(g * 8, 8), 8)
        face = face_at[rows, :]
        h, l = face >> 7, face & (LANES - 1)

        def look(i, total):
            return jnp.where(h == i, pick(fnode[pl.ds(i, 1), :], l), total)

        node = lax.fori_loop(0, 32, look, jnp.zeros((8, LANES), I32), unroll=32)
        slab[rows, 3, :] = node.astype(F32)
        return carry

    lax.fori_loop(0, peers // 8, part, 0, unroll=2)

    def weigh(i, carry):
        scale[pl.ds(i, 3, stride=32), :] = weight[pl.ds(i, 1), :] * area[:, lanes(i)]
        return carry

    lax.fori_loop(0, 32, weigh, 0, unroll=8)


def halo_table(arrived, table):
    line, lane = iota((8, LANES), 0), iota((8, LANES), 1)
    where_at = line * 16 + (lane & 15)
    for c in range(5):
        for quarter in range(4):
            total = jnp.zeros((8, LANES), F32)
            for n in range(6):
                got = pick(arrived[n, c * 4 + quarter : c * 4 + quarter + 1, :], where_at)
                total = jnp.where((lane >> 4) == n, got, total)
            table[c, quarter * 8 : quarter * 8 + 8, :] = total


def window(cols, cells, q, j):
    col = cols[:, lanes(q * 4 + j)]
    shifted = col + 64 - q * 512
    far = col - cells
    far_at = (far >> 9) * 16 + (far & 511) - q * 16
    inside = col < cells
    where_at = jnp.where(inside, shifted, far_at) & (LANES - 1)
    return where_at, jnp.where(inside, shifted >> 7, 5)


def pick_local(c, where_at, chunk, table, q):
    total = pick(table[q * 4, c : c + 1, :], where_at)
    for k in range(1, 5):
        got = pick(table[q * 4 + k, c : c + 1, :], where_at)
        total = jnp.where(chunk == k, got, total)
    return total


def early_picks(cells, cols, table, picks):
    def step(q, carry):
        for j in range(4):
            where_at, chunk = window(cols, cells, q, j)
            for c in range(5):
                picks[c, q * 4 + j, 0:7, :] = pick_local(c, where_at, chunk, table, q)
        return carry

    lax.fori_loop(0, EARLY, step, 0, unroll=6)


def apply_system(fluid, base, jac, cols, dt, table, halo, sums, picks, residual, state):
    cells = fluid.shape[1]
    sums[...] = jnp.zeros(sums.shape, F32)

    def step(q, carry, early):
        for j in range(4):
            where_at, chunk = window(cols, cells, q, j)
            block = q * 4 + j
            at = lanes(block)
            picked = []
            for c in range(5):
                if early:
                    total = picks[c, block, 0:7, :]
                else:
                    total = pick_local(c, where_at, chunk, table, q)
                got = pick(halo[c, pl.ds(q, 1), :], where_at)
                picked.append(jnp.where(chunk == 5, got, total))
            for c in range(5):
                picks[c, block, 0:7, :] = picked[c]
            for r in (0, 1, 4):
                total = jac[r, 0, :, at].astype(F32) * picked[0]
                for c in range(1, 5):
                    total = total + jac[r, c, :, at].astype(F32) * picked[c]
                sums[j, r * 8 : r * 8 + 7, :] = total
            coupled = sums[j, pl.ds(0, 5, stride=8), :]
            for b in range(1, 7):
                coupled = coupled + sums[j, pl.ds(b, 5, stride=8), :]
            left = base[:, at] - coupled
            residual[:, at] = left
            state[pl.ds(pl.multiple_of(block * 8, 8), 5), :] = (
                fluid[:, at] + dt[pl.ds(block, 1), :] * left
            )
        return carry

    lax.fori_loop(0, EARLY, functools.partial(step, early=True), 0, unroll=6)
    lax.fori_loop(EARLY, cells // 512, functools.partial(step, early=False), 0, unroll=7)


def apply_rest(base, jac, picks, sums, residual):
    def step(quad, carry):
        for j in range(4):
            block = quad * 4 + j
            at = lanes(block)
            for r in (2, 3):
                total = jac[r, 0, :, at].astype(F32) * picks[0, block, 0:7, :]
                for c in range(1, 5):
                    total = total + jac[r, c, :, at].astype(F32) * picks[c, block, 0:7, :]
                sums[j, r * 8 : r * 8 + 7, :] = total
            coupled = sums[j, pl.ds(0, 5, stride=8), :]
            for b in range(1, 7):
                coupled = coupled + sums[j, pl.ds(b, 5, stride=8), :]
            residual[2:4, at] = (base[:, at] - coupled)[2:4, :]
        return carry

    lax.fori_loop(0, 32, step, 0)


def cell_pressures(state, pressure):
    def step(i, carry):
        first = pl.multiple_of(i * 64, 64)
        p0, p1, p4 = (state[pl.ds(first + r, 8, stride=8), :] for r in (0, 1, 4))
        pressure[pl.ds(pl.multiple_of(i * 8, 8), 8), :] = 0.4 * (p4 - 0.8 * p1 + 0.32 * p0)
        return carry

    lax.fori_loop(0, 16, step, 0, unroll=4)


def face_loads(pressure, fcell, scale, loads):
    def part(g, carry):
        first = pl.multiple_of(g * 8, 8)
        cell = fcell[pl.ds(first, 8), :]
        low, high = cell & (LANES - 1), cell >> 7

        def step(i, total):
            return jnp.where(high == i, pick(pressure[pl.ds(i, 1), :], low), total)

        found = lax.fori_loop(0, 128, step, jnp.zeros((8, LANES), F32), unroll=128)
        for c in range(3):
            rows = pl.ds(first + c * 32, 8)
            loads[rows, :] = scale[rows, :] * found
        return carry

    lax.fori_loop(0, 4, part, 0, unroll=2)


def fill_slabs(g, loads, face_at, slab):
    rows = pl.ds(pl.multiple_of(g * 8, 8), 8)
    face = face_at[rows, :]
    h, l = face >> 7, face & (LANES - 1)

    def look(i, total):
        hit = h == i
        return tuple(
            jnp.where(hit, pick(loads[pl.ds(c * 32 + i, 1), :], l), total[c]) for c in range(3)
        )

    total = lax.fori_loop(0, 32, look, (jnp.zeros((8, LANES), F32),) * 3, unroll=32)
    for c in range(3):
        slab[rows, c, :] = total[c]


def node_sums(groups, got):
    line = iota((LANES, LANES), 0)
    above = iota((8, LANES), 0) >> 2
    total = jnp.zeros((48, LANES), F32)
    for g in groups:
        left, right = [], []
        for s in range(8):
            piece = got[g * 8 + s]
            node = piece[3:4, :].astype(I32)
            twice = jnp.concatenate([piece, piece], axis=0)
            high = jnp.broadcast_to(node >> 7, (8, LANES))
            spread = jnp.concatenate(
                [jnp.where(high == above, twice, 0.0), jnp.where(high == above + 2, twice, 0.0)],
                axis=0,
            )
            left.append(jnp.concatenate(three_parts(spread), axis=0))
            hit = jnp.broadcast_to(node & (LANES - 1), (LANES, LANES)) == line
            right.append(jnp.where(hit, 1.0, 0.0).astype(BF16))
        total = total + dot_nt(jnp.concatenate(left, axis=1), jnp.concatenate(right, axis=1))
    return total


def split_compliance(compliance, high, middle):
    def step(i, carry):
        t, rows = i // 4, pl.ds(pl.multiple_of((i % 4) * 96, 96), 96)
        value = compliance[t, rows, :]
        top = value.astype(BF16)
        high[t, rows, :] = top
        middle[t, rows, :] = (value - top.astype(F32)).astype(BF16)
        return carry

    lax.fori_loop(0, 16, step, 0)


def tile_response(total, high, middle, moved, displacement):
    sums = total[0:16, :] + total[16:32, :] + total[32:48, :]
    for t in range(4):
        load = jnp.concatenate([sums[t * 4 + c : t * 4 + c + 1, :] for c in range(3)], axis=1)
        top, rest, last = (
            jnp.broadcast_to(part.astype(F32), (16, part.shape[1])) for part in three_parts(load)
        )
        line = iota(top.shape, 0)
        parts = jnp.where(line == 0, top, jnp.where(line == 1, rest, last)).astype(BF16)
        first = dot_nt(parts, high[t])
        second = dot_nt(parts, middle[t])
        out = first[0:1] + ((first[1:2] + second[0:1]) + (first[2:3] + second[1:2]))
        for c in range(3):
            row = out[:, c * LANES : (c + 1) * LANES]
            moved[c * 4 + t : c * 4 + t + 1, :] = row
            displacement[c : c + 1, t * LANES : (t + 1) * LANES] = row


def make_replies(g, got, moved, reply):
    rows = pl.ds(pl.multiple_of(g * 8, 8), 8)
    node = got[rows, 3, :].astype(I32)
    low, high = node & (LANES - 1), node >> 7
    for c in range(3):
        total = pick(moved[c * 4 : c * 4 + 1, :], low)
        for t in range(1, 4):
            total = jnp.where(high == t, pick(moved[c * 4 + t : c * 4 + t + 1, :], low), total)
        reply[rows, c, :] = total


def face_motions(groups, total, answer, relative, rank):
    total = list(total)
    for f in range(4):
        rows = slice(f * 8, f * 8 + 8)
        slot, peer = rank[rows, :].astype(I32), relative[rows, :]
        for g in groups:
            for s in range(8):
                hit = peer == g * 8 + s
                for c in range(3):
                    row = answer[g * 8 + s, c : c + 1, :]
                    total[c * 4 + f] = jnp.where(hit, pick(row, slot), total[c * 4 + f])
    return tuple(total)


def store_motions(total, weight, motion):
    for f in range(4):
        for c in range(3):
            out = total[c * 4 + f] * weight[f * 8 : f * 8 + 8, :]
            for s in range(8):
                at = (f * 8 + s) * LANES
                motion[c : c + 1, at : at + LANES] = out[s : s + 1, :]


EARLY = 18
BATCHES = ((7, 6, 5, 4), (3, 2, 1, 0))
COMPACT_UNROLL = 16
INPUTS = ("fluid", "base", "jac", "cols", "dt", "send", "fcell", "area", "weight", "route", "fnode", "comp")


def kernel(peers, *refs):
    count = len(INPUTS)
    hbm = dict(zip(INPUTS, refs[:count]))
    residual_out, displacement, motion = refs[count : count + 3]
    refs = refs[count + 3 :]
    v = dict(zip(INPUTS, refs[:count]))
    (
        index, found, sends, arrived, table, halo, relative, onehot, prefix, rank, face_at, scale,
        loads, slab, got, sums, picks, residual, state, pressure, comp_high, comp_middle, moved,
        reply, answer,
        in_sems, out_sem, halo_send, halo_recv, load_send, load_recv, back_send, back_recv,
    ) = refs[count:]
    me = lax.axis_index("dom")
    copies = {
        name: pltpu.make_async_copy(hbm[name], v[name], in_sems.at[i])
        for i, name in enumerate(INPUTS)
    }
    copies["fluid"].start()
    copies["send"].start()
    barrier = pltpu.get_barrier_semaphore()


    def peer_at(slot, sign):
        dz, dy, dc = offset_of(slot // 8, slot % 8)
        return (
            (((me >> 3) + sign * dz + 8) & 7) * 8
            + (((me >> 1) + sign * dy + 4) & 3) * 2
            + ((me + dc) & 1)
        )

    for slot in range(peers - 1):
        pl.semaphore_signal(
            barrier, inc=1, device_id={"dom": peer_at(slot, 1)}, device_id_type=MESH
        )
    for name in ("route", "fnode", "weight", "area", "cols", "fcell", "jac", "base", "dt", "comp"):
        copies[name].start()
    copies["send"].wait()
    copies["fluid"].wait()
    gather_sends(v["fluid"], v["send"], index, found, sends)
    pl.semaphore_wait(barrier, peers - 1)

    halo_copies = []
    for m in range(6):
        copy = pltpu.make_async_remote_copy(
            src_ref=sends.at[pl.ds(24 * m, 24)],
            dst_ref=arrived.at[5 - m],
            send_sem=halo_send.at[m],
            recv_sem=halo_recv.at[5 - m],
            device_id={"dom": (me + OFFSETS[m] + peers) & (peers - 1)},
            device_id_type=MESH,
        )
        copy.start()
        halo_copies.append(copy)

    shift_table(v["fluid"], table)
    copies["route"].wait()
    rank_faces(me, peers, v["route"], relative, onehot, prefix, rank)
    for name in ("fnode", "weight", "area"):
        copies[name].wait()
    compact_faces(
        peers, onehot, rank, v["fnode"], v["weight"], v["area"], face_at, slab, scale
    )
    copies["cols"].wait()
    early_picks(v["fluid"].shape[1], v["cols"], table, picks)
    for copy in halo_copies:
        copy.wait()
    halo_table(arrived, halo)
    for name in ("jac", "base", "dt", "fcell"):
        copies[name].wait()
    apply_system(
        v["fluid"], v["base"], v["jac"], v["cols"], v["dt"], table, halo, sums, picks, residual, state
    )
    cell_pressures(state, pressure)
    face_loads(pressure, v["fcell"], scale, loads)

    def copy_of(source, target, send_sem, recv_sem, height, slots, to, group):
        rows = pl.ds(0, height)
        return pltpu.make_async_remote_copy(
            src_ref=source.at[slots, rows],
            dst_ref=target.at[slots, rows],
            send_sem=send_sem,
            recv_sem=recv_sem.at[group],
            device_id={"dom": to},
            device_id_type=MESH,
        )

    def send_group(source, target, send_sem, recv_sem, height, sign, group, amount):
        for place in range(amount):
            slot = group * 8 + place
            to = peer_at(slot, sign)
            copy_of(source, target, send_sem, recv_sem, height, slot, to, group).start()

    def received(source, target, send_sem, recv_sem, height, group, amount):
        slots = pl.ds(group * 8, amount)
        copy_of(source, target, send_sem, recv_sem, height, slots, me ^ 1, group).wait_recv()

    forth = (slab, got, load_send, load_recv, 4)
    back = (reply, answer, back_send, back_recv, 3)

    def send_loads(g, carry):
        fill_slabs(g, loads, face_at, slab)
        send_group(*forth, 1, g, 8)
        return carry

    lax.fori_loop(0, 7, send_loads, 0)
    fill_slabs(7, loads, face_at, slab)
    send_group(*forth, 1, 7, 7)
    got[63] = slab[63]

    apply_rest(v["base"], v["jac"], picks, sums, residual)
    residual_copy = pltpu.make_async_copy(residual, residual_out, out_sem)
    residual_copy.start()
    copies["comp"].wait()
    split_compliance(v["comp"], comp_high, comp_middle)

    total = jnp.zeros((48, LANES), F32)
    for groups in BATCHES:
        for g in groups:
            received(*forth, g, 8 if g < 7 else 7)
        total = total + node_sums(groups, got)
    tile_response(total, comp_high, comp_middle, moved, displacement)

    def send_replies(g, carry):
        make_replies(g, got, moved, reply)
        send_group(*back, -1, g, 8)
        return carry

    lax.fori_loop(0, 7, send_replies, 0)
    make_replies(7, got, moved, reply)
    send_group(*back, -1, 7, 7)
    answer[63] = reply[63]

    motions = (jnp.zeros((8, LANES), F32),) * 12
    for groups in BATCHES:
        for g in groups:
            received(*back, g, 8 if g < 7 else 7)
        motions = face_motions(groups, motions, answer, relative, rank)
    store_motions(motions, v["weight"], motion)
    for way in (forth, back):
        copy_of(*way, pl.ds(0, 63), me ^ 1, 0).wait_send()
    residual_copy.wait()


def per_device(
    fluid_state,
    residual_base,
    jacobian,
    columns,
    pseudo_step,
    send_cells,
    interface_face_cell,
    interface_face_area_vector,
    mortar_weight,
    face_route,
    face_node,
    compliance,
):
    peers = lax.axis_size("dom")
    operands = (
        fluid_state,
        residual_base,
        jnp.transpose(jacobian, (1, 2, 0, 3)),
        columns,
        pseudo_step.reshape(-1, LANES),
        send_cells,
        interface_face_cell.reshape(-1, LANES),
        interface_face_area_vector,
        mortar_weight.reshape(-1, LANES),
        face_route.reshape(-1, LANES),
        face_node.reshape(-1, LANES),
        compliance,
    )
    vmem = pltpu.VMEM
    dma = pltpu.SemaphoreType.DMA
    scratch = [vmem(x.shape, x.dtype) for x in operands] + [
        vmem((24, LANES), I32),
        vmem((5, 24, LANES), F32),
        vmem((192, LANES), F32),
        vmem((6, 24, LANES), F32),
        vmem((129, 8, LANES), F32),
        vmem((5, 32, LANES), F32),
        vmem((32, LANES), I32),
        vmem((32 * peers, LANES), BF16),
        vmem((32 * peers, 2 * LANES), F32),
        vmem((32, LANES), F32),
        vmem((peers, LANES), I32),
        vmem((96, LANES), F32),
        vmem((96, LANES), F32),
        vmem((peers, 4, LANES), F32),
        vmem((peers, 4, LANES), F32),
        vmem((4, 40, LANES), F32),
        vmem((5, 128, 8, LANES), F32),
        vmem(fluid_state.shape, F32),
        vmem((1024, LANES), F32),
        vmem((LANES, LANES), F32),
        vmem(compliance.shape, BF16),
        vmem(compliance.shape, BF16),
        vmem((16, LANES), F32),
        vmem((peers, 4, LANES), F32),
        vmem((peers, 4, LANES), F32),
        dma((len(INPUTS),)),
        dma,
        dma((6,)),
        dma((6,)),
        dma,
        dma((8,)),
        dma,
        dma((8,)),
    ]
    results = pl.pallas_call(
        functools.partial(kernel, peers),
        out_shape=(
            jax.ShapeDtypeStruct(fluid_state.shape, F32),
            jax.ShapeDtypeStruct((3, compliance.shape[0] * LANES), F32),
            jax.ShapeDtypeStruct(interface_face_area_vector.shape, F32),
        ),
        in_specs=[pl.BlockSpec(memory_space=pl.ANY)] * len(operands),
        out_specs=(
            pl.BlockSpec(memory_space=pl.ANY),
            pl.BlockSpec(memory_space=vmem),
            pl.BlockSpec(memory_space=vmem),
        ),
        scratch_shapes=scratch,
        compiler_params=pltpu.CompilerParams(
            collective_id=0, has_side_effects=True, vmem_limit_bytes=56 * 1024 * 1024
        ),
    )(*operands)
    return hand_over(*results)


def hand_over_kernel(*refs):
    sources, targets, holds, (sems_in, sems_out) = refs[:3], refs[3:6], refs[6:9], refs[9:]
    pieces = []
    for which, count in ((0, 4), (1, 1), (2, 1)):
        width = sources[which].shape[1] // count
        for piece in range(count):
            at = (slice(None), pl.ds(piece * width, width))
            n = len(pieces)
            pieces.append(
                (
                    pltpu.make_async_copy(
                        sources[which].at[at], holds[which].at[at], sems_in.at[n]
                    ),
                    pltpu.make_async_copy(
                        holds[which].at[at], targets[which].at[at], sems_out.at[n]
                    ),
                )
            )
    for copy_in, _ in pieces:
        copy_in.start()
    for copy_in, copy_out in pieces:
        copy_in.wait()
        copy_out.start()
    for _, copy_out in pieces:
        copy_out.wait()


def hand_over(*results):
    return pl.pallas_call(
        hand_over_kernel,
        out_shape=[jax.ShapeDtypeStruct(x.shape, x.dtype) for x in results],
        in_specs=[pl.BlockSpec(memory_space=pl.ANY)] * 3,
        out_specs=[pl.BlockSpec(memory_space=pl.ANY)] * 3,
        scratch_shapes=[pltpu.VMEM(x.shape, x.dtype) for x in results]
        + [pltpu.SemaphoreType.DMA((6,))] * 2,
        compiler_params=pltpu.CompilerParams(vmem_limit_bytes=60 * 1024 * 1024),
    )(*results)


def solution(mesh):
    return jax.shard_map(
        per_device,
        mesh=mesh,
        in_specs=(
            P(None, ("sweep", "dom")),
            P(None, ("sweep", "dom")),
            P(None, None, None, ("sweep", "dom")),
            P(None, ("sweep", "dom")),
            P(("sweep", "dom")),
            P(("sweep", "dom"), None),
            P(("sweep", "dom")),
            P(None, ("sweep", "dom")),
            P(("sweep", "dom")),
            P(("sweep", "dom"), None),
            P(("sweep", "dom")),
            P(("sweep", "dom"), None, None),
        ),
        out_specs=(P(None, ("sweep", "dom")), P(None, ("sweep", "dom")), P(None, ("sweep", "dom"))),
        check_vma=False,
    )
```

```python
import functools

import jax
import jax.numpy as jnp
from jax import lax
from jax.experimental import pallas as pl
from jax.experimental.pallas import tpu as pltpu
from jax.sharding import PartitionSpec as P

MESH = pl.DeviceIdType.MESH
OFFSETS = (-3, -2, -1, 1, 2, 3)
HIGH = lax.Precision.HIGHEST
F32 = jnp.float32
BF16 = jnp.bfloat16
I32 = jnp.int32
LANES = 128


def pick(row, where_at):
    return jnp.take_along_axis(
        jnp.broadcast_to(row, where_at.shape), where_at, axis=1, mode="promise_in_bounds"
    )


def iota(shape, dim):
    return lax.broadcasted_iota(I32, shape, dim)


def lanes(block):
    return pl.ds(pl.multiple_of(block * LANES, LANES), LANES)


def three_parts(value):
    high = value.astype(BF16)
    rest = value - high.astype(F32)
    middle = rest.astype(BF16)
    low = (rest - middle.astype(F32)).astype(BF16)
    return high, middle, low


def dot_nt(a, b, precision=None):
    return lax.dot_general(
        a, b, (((1,), (1,)), ((), ())), precision=precision, preferred_element_type=F32
    )


def offset_of(group, place):
    side = place // 2
    dz = 4 + (1 - 2 * (group % 2)) * ((group + 1) // 2)
    dy = 2 + (1 - 2 * (side % 2)) * ((side + 1) // 2)
    return dz, dy, 1 - place % 2


def slot_of(me, route):
    dz = ((route >> 3) - (me >> 3)) & 7
    dy = ((route >> 1) - (me >> 1)) & 3
    dc = (route - me) & 1
    group = jnp.where(dz < 4, 7 - 2 * dz, 2 * dz - 8)
    side = jnp.where(dy < 2, 3 - 2 * dy, 2 * dy - 4)
    return group * 8 + side * 2 + (1 - dc)


def gather_sends(fluid, send, index, found, out, beside=lambda g: None):
    for k in range(4):
        index[pl.ds(k, 6, stride=4), :] = send[:, k * LANES : (k + 1) * LANES]

    def part(g, carry):
        beside(g)
        rows = pl.ds(pl.multiple_of(g * 8, 8), 8)
        cell = index[rows, :]
        low, high = cell & (LANES - 1), cell >> 7

        def step(block, total):
            hit = high == block
            return tuple(
                jnp.where(hit, pick(fluid[pl.ds(c, 1), lanes(block)], low), total[c])
                for c in range(5)
            )

        total = lax.fori_loop(0, 128, step, (jnp.zeros((8, LANES), F32),) * 5, unroll=128)
        for c in range(5):
            found[c, rows, :] = total[c]
        return carry

    lax.fori_loop(0, 3, part, 0)
    for m in range(6):
        for c in range(5):
            out[m * 24 + c * 4 : m * 24 + c * 4 + 4, :] = found[c, m * 4 : m * 4 + 4, :]


def shift_table(fluid, table):
    left = iota((5, LANES), 1) < 64

    def step(block, before):
        here = pltpu.roll(fluid[:, lanes(block)], 64, 1)
        table[block, 0:5, :] = jnp.where(left, before, here)
        return here

    last = lax.fori_loop(0, 128, step, jnp.zeros((5, LANES), F32), unroll=32)
    table[128, 0:5, :] = last


def rank_faces(me, peers, route, relative, onehot, prefix, rank):
    relative[...] = slot_of(me, route[...])
    line = iota((peers, LANES), 0)
    for i in range(32):
        hit = jnp.broadcast_to(relative[i : i + 1, :], (peers, LANES)) == line
        onehot[i * peers : (i + 1) * peers, :] = jnp.where(hit, 1.0, 0.0).astype(BF16)
    upto = jnp.where(iota((LANES, LANES), 0) <= iota((LANES, LANES), 1), 1.0, 0.0)
    weights = jnp.concatenate([upto, jnp.ones((LANES, LANES), F32)], axis=1).astype(BF16)

    def count(part, carry):
        rows = pl.ds(pl.multiple_of(part * 512, 512), 512)
        prefix[rows, :] = jnp.dot(onehot[rows, :], weights, preferred_element_type=F32)
        return carry

    lax.fori_loop(0, 32 * peers // 512, count, 0, unroll=4)

    def step(i, before):
        rows = pl.ds(pl.multiple_of(i * peers, peers), peers)
        hit = onehot[rows, :].astype(F32)
        here = prefix[rows, 0:LANES] + before
        rank[pl.ds(i, 1), :] = jnp.sum(hit * here, axis=0, keepdims=True) - 1.0
        return before + prefix[rows, LANES : 2 * LANES]

    lax.fori_loop(0, 32, step, jnp.zeros((peers, LANES), F32), unroll=16)


def compact_faces(peers, onehot, rank, fnode, weight, area, face_at, slab, scale):
    line = iota((LANES, LANES), 0).astype(F32)
    lane = iota((peers, LANES), 1).astype(F32)

    def step(pair, total):
        left, right = [], []
        for half in range(2):
            i = pair * 2 + half
            hit = onehot[pl.ds(pl.multiple_of(i * peers, peers), peers), :].astype(F32)
            left.append(
                jnp.concatenate(
                    [hit * (i + 1).astype(F32), hit * lane], axis=0
                ).astype(BF16)
            )
            place = jnp.broadcast_to(rank[pl.ds(i, 1), :], (LANES, LANES)) == line
            right.append(jnp.where(place, 1.0, 0.0).astype(BF16))
        return total + dot_nt(jnp.concatenate(left, axis=1), jnp.concatenate(right, axis=1))

    found = lax.fori_loop(0, 16, step, jnp.zeros((2 * peers, LANES), F32), unroll=COMPACT_UNROLL)
    high = found[0:peers, :].astype(I32) - 1
    low = found[peers : 2 * peers, :].astype(I32)
    face_at[...] = (high << 7) + low

    def part(g, carry):
        rows = pl.ds(pl.multiple_of(g * 8, 8), 8)
        face = face_at[rows, :]
        h, l = face >> 7, face & (LANES - 1)

        def look(i, total):
            return jnp.where(h == i, pick(fnode[pl.ds(i, 1), :], l), total)

        node = lax.fori_loop(0, 32, look, jnp.zeros((8, LANES), I32), unroll=32)
        slab[rows, 3, :] = node.astype(F32)
        return carry

    lax.fori_loop(0, peers // 8, part, 0, unroll=2)

    def weigh(i, carry):
        scale[pl.ds(i, 3, stride=32), :] = weight[pl.ds(i, 1), :] * area[:, lanes(i)]
        return carry

    lax.fori_loop(0, 32, weigh, 0, unroll=8)


def halo_table(arrived, table):
    line, lane = iota((8, LANES), 0), iota((8, LANES), 1)
    where_at = line * 16 + (lane & 15)
    for c in range(5):
        for quarter in range(4):
            total = jnp.zeros((8, LANES), F32)
            for n in range(6):
                got = pick(arrived[n, c * 4 + quarter : c * 4 + quarter + 1, :], where_at)
                total = jnp.where((lane >> 4) == n, got, total)
            table[c, quarter * 8 : quarter * 8 + 8, :] = total


def window(cols, cells, q, j):
    col = cols[:, lanes(q * 4 + j)]
    shifted = col + 64 - q * 512
    far = col - cells
    far_at = (far >> 9) * 16 + (far & 511) - q * 16
    inside = col < cells
    where_at = jnp.where(inside, shifted, far_at) & (LANES - 1)
    return where_at, jnp.where(inside, shifted >> 7, 5)


def pick_local(c, where_at, chunk, table, q):
    total = pick(table[q * 4, c : c + 1, :], where_at)
    for k in range(1, 5):
        got = pick(table[q * 4 + k, c : c + 1, :], where_at)
        total = jnp.where(chunk == k, got, total)
    return total


def early_picks(cells, cols, table, picks):
    def step(q, carry):
        for j in range(4):
            where_at, chunk = window(cols, cells, q, j)
            for c in range(5):
                picks[c, q * 4 + j, 0:7, :] = pick_local(c, where_at, chunk, table, q)
        return carry

    lax.fori_loop(0, EARLY, step, 0, unroll=6)


def apply_system(fluid, base, jac, cols, dt, table, halo, sums, picks, residual, state):
    cells = fluid.shape[1]
    sums[...] = jnp.zeros(sums.shape, F32)

    def step(q, carry, early):
        for j in range(4):
            where_at, chunk = window(cols, cells, q, j)
            block = q * 4 + j
            at = lanes(block)
            picked = []
            for c in range(5):
                if early:
                    total = picks[c, block, 0:7, :]
                else:
                    total = pick_local(c, where_at, chunk, table, q)
                got = pick(halo[c, pl.ds(q, 1), :], where_at)
                picked.append(jnp.where(chunk == 5, got, total))
            for c in range(5):
                picks[c, block, 0:7, :] = picked[c]
            for r in (0, 1, 4):
                total = jac[r, 0, :, at].astype(F32) * picked[0]
                for c in range(1, 5):
                    total = total + jac[r, c, :, at].astype(F32) * picked[c]
                sums[j, r * 8 : r * 8 + 7, :] = total
            coupled = sums[j, pl.ds(0, 5, stride=8), :]
            for b in range(1, 7):
                coupled = coupled + sums[j, pl.ds(b, 5, stride=8), :]
            left = base[:, at] - coupled
            residual[:, at] = left
            state[pl.ds(pl.multiple_of(block * 8, 8), 5), :] = (
                fluid[:, at] + dt[pl.ds(block, 1), :] * left
            )
        return carry

    lax.fori_loop(0, EARLY, functools.partial(step, early=True), 0, unroll=6)
    lax.fori_loop(EARLY, cells // 512, functools.partial(step, early=False), 0, unroll=7)


def apply_rest(base, jac, picks, sums, residual):
    def step(quad, carry):
        for j in range(4):
            block = quad * 4 + j
            at = lanes(block)
            for r in (2, 3):
                total = jac[r, 0, :, at].astype(F32) * picks[0, block, 0:7, :]
                for c in range(1, 5):
                    total = total + jac[r, c, :, at].astype(F32) * picks[c, block, 0:7, :]
                sums[j, r * 8 : r * 8 + 7, :] = total
            coupled = sums[j, pl.ds(0, 5, stride=8), :]
            for b in range(1, 7):
                coupled = coupled + sums[j, pl.ds(b, 5, stride=8), :]
            residual[2:4, at] = (base[:, at] - coupled)[2:4, :]
        return carry

    lax.fori_loop(0, 32, step, 0)


def cell_pressures(state, pressure):
    def step(i, carry):
        first = pl.multiple_of(i * 64, 64)
        p0, p1, p4 = (state[pl.ds(first + r, 8, stride=8), :] for r in (0, 1, 4))
        pressure[pl.ds(pl.multiple_of(i * 8, 8), 8), :] = 0.4 * (p4 - 0.8 * p1 + 0.32 * p0)
        return carry

    lax.fori_loop(0, 16, step, 0, unroll=4)


def face_loads(pressure, fcell, scale, loads):
    def part(g, carry):
        first = pl.multiple_of(g * 8, 8)
        cell = fcell[pl.ds(first, 8), :]
        low, high = cell & (LANES - 1), cell >> 7

        def step(i, total):
            return jnp.where(high == i, pick(pressure[pl.ds(i, 1), :], low), total)

        found = lax.fori_loop(0, 128, step, jnp.zeros((8, LANES), F32), unroll=128)
        for c in range(3):
            rows = pl.ds(first + c * 32, 8)
            loads[rows, :] = scale[rows, :] * found
        return carry

    lax.fori_loop(0, 4, part, 0, unroll=2)


def fill_slabs(g, loads, face_at, slab):
    rows = pl.ds(pl.multiple_of(g * 8, 8), 8)
    face = face_at[rows, :]
    h, l = face >> 7, face & (LANES - 1)

    def look(i, total):
        hit = h == i
        return tuple(
            jnp.where(hit, pick(loads[pl.ds(c * 32 + i, 1), :], l), total[c]) for c in range(3)
        )

    total = lax.fori_loop(0, 32, look, (jnp.zeros((8, LANES), F32),) * 3, unroll=32)
    for c in range(3):
        slab[rows, c, :] = total[c]


def node_sums(groups, got):
    line = iota((LANES, LANES), 0)
    above = iota((8, LANES), 0) >> 2
    total = jnp.zeros((48, LANES), F32)
    for g in groups:
        left, right = [], []
        for s in range(8):
            piece = got[g * 8 + s]
            node = piece[3:4, :].astype(I32)
            twice = jnp.concatenate([piece, piece], axis=0)
            high = jnp.broadcast_to(node >> 7, (8, LANES))
            spread = jnp.concatenate(
                [jnp.where(high == above, twice, 0.0), jnp.where(high == above + 2, twice, 0.0)],
                axis=0,
            )
            left.append(jnp.concatenate(three_parts(spread), axis=0))
            hit = jnp.broadcast_to(node & (LANES - 1), (LANES, LANES)) == line
            right.append(jnp.where(hit, 1.0, 0.0).astype(BF16))
        total = total + dot_nt(jnp.concatenate(left, axis=1), jnp.concatenate(right, axis=1))
    return total


def split_compliance(compliance, high, middle):
    def step(i, carry):
        t, rows = i // 4, pl.ds(pl.multiple_of((i % 4) * 96, 96), 96)
        value = compliance[t, rows, :]
        top = value.astype(BF16)
        high[t, rows, :] = top
        middle[t, rows, :] = (value - top.astype(F32)).astype(BF16)
        return carry

    lax.fori_loop(0, 16, step, 0)


def tile_response(total, high, middle, moved, displacement):
    sums = total[0:16, :] + total[16:32, :] + total[32:48, :]
    for t in range(4):
        load = jnp.concatenate([sums[t * 4 + c : t * 4 + c + 1, :] for c in range(3)], axis=1)
        top, rest, last = (
            jnp.broadcast_to(part.astype(F32), (16, part.shape[1])) for part in three_parts(load)
        )
        line = iota(top.shape, 0)
        parts = jnp.where(line == 0, top, jnp.where(line == 1, rest, last)).astype(BF16)
        first = dot_nt(parts, high[t])
        second = dot_nt(parts, middle[t])
        out = first[0:1] + ((first[1:2] + second[0:1]) + (first[2:3] + second[1:2]))
        for c in range(3):
            row = out[:, c * LANES : (c + 1) * LANES]
            moved[c * 4 + t : c * 4 + t + 1, :] = row
            displacement[c : c + 1, t * LANES : (t + 1) * LANES] = row


def make_replies(g, got, moved, reply):
    rows = pl.ds(pl.multiple_of(g * 8, 8), 8)
    node = got[rows, 3, :].astype(I32)
    low, high = node & (LANES - 1), node >> 7
    for c in range(3):
        total = pick(moved[c * 4 : c * 4 + 1, :], low)
        for t in range(1, 4):
            total = jnp.where(high == t, pick(moved[c * 4 + t : c * 4 + t + 1, :], low), total)
        reply[rows, c, :] = total


def face_motions(groups, total, answer, relative, rank):
    total = list(total)
    for f in range(4):
        rows = slice(f * 8, f * 8 + 8)
        slot, peer = rank[rows, :].astype(I32), relative[rows, :]
        for g in groups:
            for s in range(8):
                hit = peer == g * 8 + s
                for c in range(3):
                    row = answer[g * 8 + s, c : c + 1, :]
                    total[c * 4 + f] = jnp.where(hit, pick(row, slot), total[c * 4 + f])
    return tuple(total)


def store_motions(total, weight, motion):
    for f in range(4):
        for c in range(3):
            out = total[c * 4 + f] * weight[f * 8 : f * 8 + 8, :]
            for s in range(8):
                at = (f * 8 + s) * LANES
                motion[c : c + 1, at : at + LANES] = out[s : s + 1, :]


EARLY = 18
BATCHES = ((7, 6, 5, 4), (3, 2, 1, 0))
COMPACT_UNROLL = 16
INPUTS = ("fluid", "base", "jac", "cols", "dt", "send", "fcell", "area", "weight", "route", "fnode", "comp")


def kernel(peers, *refs):
    count = len(INPUTS)
    hbm = dict(zip(INPUTS, refs[:count]))
    residual_out, displacement, motion = refs[count : count + 3]
    refs = refs[count + 3 :]
    v = dict(zip(INPUTS, refs[:count]))
    (
        index, found, sends, arrived, table, halo, relative, onehot, prefix, rank, face_at, scale,
        loads, slab, got, sums, picks, residual, state, pressure, comp_high, comp_middle, moved,
        reply, answer,
        in_sems, out_sem, halo_send, halo_recv, load_send, load_recv, back_send, back_recv,
    ) = refs[count:]
    me = lax.axis_index("dom")
    copies = {
        name: pltpu.make_async_copy(hbm[name], v[name], in_sems.at[i])
        for i, name in enumerate(INPUTS)
    }
    copies["fluid"].start()
    copies["send"].start()
    barrier = pltpu.get_barrier_semaphore()


    def peer_at(slot, sign):
        dz, dy, dc = offset_of(slot // 8, slot % 8)
        return (
            (((me >> 3) + sign * dz + 8) & 7) * 8
            + (((me >> 1) + sign * dy + 4) & 3) * 2
            + ((me + dc) & 1)
        )

    def greet(slot):
        pl.semaphore_signal(
            barrier, inc=1, device_id={"dom": peer_at(slot, 1)}, device_id_type=MESH
        )

    def greet_near(g):
        for place in range(9):
            greet(36 + g * 9 + place)

    for slot in range(36):
        greet(slot)
    for name in ("route", "fnode", "weight", "area", "cols", "fcell", "jac", "base", "dt", "comp"):
        copies[name].start()
    copies["send"].wait()
    copies["fluid"].wait()
    gather_sends(v["fluid"], v["send"], index, found, sends, greet_near)
    pl.semaphore_wait(barrier, peers - 1)

    halo_copies = []
    for m in range(6):
        copy = pltpu.make_async_remote_copy(
            src_ref=sends.at[pl.ds(24 * m, 24)],
            dst_ref=arrived.at[5 - m],
            send_sem=halo_send.at[m],
            recv_sem=halo_recv.at[5 - m],
            device_id={"dom": (me + OFFSETS[m] + peers) & (peers - 1)},
            device_id_type=MESH,
        )
        copy.start()
        halo_copies.append(copy)

    shift_table(v["fluid"], table)
    copies["route"].wait()
    rank_faces(me, peers, v["route"], relative, onehot, prefix, rank)
    for name in ("fnode", "weight", "area"):
        copies[name].wait()
    compact_faces(
        peers, onehot, rank, v["fnode"], v["weight"], v["area"], face_at, slab, scale
    )
    copies["cols"].wait()
    early_picks(v["fluid"].shape[1], v["cols"], table, picks)
    for copy in halo_copies:
        copy.wait()
    halo_table(arrived, halo)
    for name in ("jac", "base", "dt", "fcell"):
        copies[name].wait()
    apply_system(
        v["fluid"], v["base"], v["jac"], v["cols"], v["dt"], table, halo, sums, picks, residual, state
    )
    cell_pressures(state, pressure)
    face_loads(pressure, v["fcell"], scale, loads)

    def copy_of(source, target, send_sem, recv_sem, height, slots, to, group):
        rows = pl.ds(0, height)
        return pltpu.make_async_remote_copy(
            src_ref=source.at[slots, rows],
            dst_ref=target.at[slots, rows],
            send_sem=send_sem,
            recv_sem=recv_sem.at[group],
            device_id={"dom": to},
            device_id_type=MESH,
        )

    def send_group(source, target, send_sem, recv_sem, height, sign, group, amount):
        for place in range(amount):
            slot = group * 8 + place
            to = peer_at(slot, sign)
            copy_of(source, target, send_sem, recv_sem, height, slot, to, group).start()

    def received(source, target, send_sem, recv_sem, height, group, amount):
        slots = pl.ds(group * 8, amount)
        copy_of(source, target, send_sem, recv_sem, height, slots, me ^ 1, group).wait_recv()

    forth = (slab, got, load_send, load_recv, 4)
    back = (reply, answer, back_send, back_recv, 3)

    def send_loads(g, carry):
        fill_slabs(g, loads, face_at, slab)
        send_group(*forth, 1, g, 8)
        return carry

    lax.fori_loop(0, 7, send_loads, 0)
    fill_slabs(7, loads, face_at, slab)
    send_group(*forth, 1, 7, 7)
    got[63] = slab[63]

    apply_rest(v["base"], v["jac"], picks, sums, residual)
    residual_copy = pltpu.make_async_copy(residual, residual_out, out_sem)
    residual_copy.start()
    copies["comp"].wait()
    split_compliance(v["comp"], comp_high, comp_middle)

    total = jnp.zeros((48, LANES), F32)
    for groups in BATCHES:
        for g in groups:
            received(*forth, g, 8 if g < 7 else 7)
        total = total + node_sums(groups, got)
    tile_response(total, comp_high, comp_middle, moved, displacement)

    def send_replies(g, carry):
        make_replies(g, got, moved, reply)
        send_group(*back, -1, g, 8)
        return carry

    lax.fori_loop(0, 7, send_replies, 0)
    make_replies(7, got, moved, reply)
    send_group(*back, -1, 7, 7)
    answer[63] = reply[63]

    motions = (jnp.zeros((8, LANES), F32),) * 12
    for groups in BATCHES:
        for g in groups:
            received(*back, g, 8 if g < 7 else 7)
        motions = face_motions(groups, motions, answer, relative, rank)
    store_motions(motions, v["weight"], motion)
    for way in (forth, back):
        copy_of(*way, pl.ds(0, 63), me ^ 1, 0).wait_send()
    residual_copy.wait()


def per_device(
    fluid_state,
    residual_base,
    jacobian,
    columns,
    pseudo_step,
    send_cells,
    interface_face_cell,
    interface_face_area_vector,
    mortar_weight,
    face_route,
    face_node,
    compliance,
):
    peers = lax.axis_size("dom")
    operands = (
        fluid_state,
        residual_base,
        jnp.transpose(jacobian, (1, 2, 0, 3)),
        columns,
        pseudo_step.reshape(-1, LANES),
        send_cells,
        interface_face_cell.reshape(-1, LANES),
        interface_face_area_vector,
        mortar_weight.reshape(-1, LANES),
        face_route.reshape(-1, LANES),
        face_node.reshape(-1, LANES),
        compliance,
    )
    vmem = pltpu.VMEM
    dma = pltpu.SemaphoreType.DMA
    scratch = [vmem(x.shape, x.dtype) for x in operands] + [
        vmem((24, LANES), I32),
        vmem((5, 24, LANES), F32),
        vmem((192, LANES), F32),
        vmem((6, 24, LANES), F32),
        vmem((129, 8, LANES), F32),
        vmem((5, 32, LANES), F32),
        vmem((32, LANES), I32),
        vmem((32 * peers, LANES), BF16),
        vmem((32 * peers, 2 * LANES), F32),
        vmem((32, LANES), F32),
        vmem((peers, LANES), I32),
        vmem((96, LANES), F32),
        vmem((96, LANES), F32),
        vmem((peers, 4, LANES), F32),
        vmem((peers, 4, LANES), F32),
        vmem((4, 40, LANES), F32),
        vmem((5, 128, 8, LANES), F32),
        vmem(fluid_state.shape, F32),
        vmem((1024, LANES), F32),
        vmem((LANES, LANES), F32),
        vmem(compliance.shape, BF16),
        vmem(compliance.shape, BF16),
        vmem((16, LANES), F32),
        vmem((peers, 4, LANES), F32),
        vmem((peers, 4, LANES), F32),
        dma((len(INPUTS),)),
        dma,
        dma((6,)),
        dma((6,)),
        dma,
        dma((8,)),
        dma,
        dma((8,)),
    ]
    results = pl.pallas_call(
        functools.partial(kernel, peers),
        out_shape=(
            jax.ShapeDtypeStruct(fluid_state.shape, F32),
            jax.ShapeDtypeStruct((3, compliance.shape[0] * LANES), F32),
            jax.ShapeDtypeStruct(interface_face_area_vector.shape, F32),
        ),
        in_specs=[pl.BlockSpec(memory_space=pl.ANY)] * len(operands),
        out_specs=(
            pl.BlockSpec(memory_space=pl.ANY),
            pl.BlockSpec(memory_space=vmem),
            pl.BlockSpec(memory_space=vmem),
        ),
        scratch_shapes=scratch,
        compiler_params=pltpu.CompilerParams(
            collective_id=0, has_side_effects=True, vmem_limit_bytes=56 * 1024 * 1024
        ),
    )(*operands)
    return hand_over(*results)


def hand_over_kernel(*refs):
    sources, targets, holds, (sems_in, sems_out) = refs[:3], refs[3:6], refs[6:9], refs[9:]
    pieces = []
    for which, count in ((0, 4), (1, 1), (2, 1)):
        width = sources[which].shape[1] // count
        for piece in range(count):
            at = (slice(None), pl.ds(piece * width, width))
            n = len(pieces)
            pieces.append(
                (
                    pltpu.make_async_copy(
                        sources[which].at[at], holds[which].at[at], sems_in.at[n]
                    ),
                    pltpu.make_async_copy(
                        holds[which].at[at], targets[which].at[at], sems_out.at[n]
                    ),
                )
            )
    for copy_in, _ in pieces:
        copy_in.start()
    for copy_in, copy_out in pieces:
        copy_in.wait()
        copy_out.start()
    for _, copy_out in pieces:
        copy_out.wait()


def hand_over(*results):
    return pl.pallas_call(
        hand_over_kernel,
        out_shape=[jax.ShapeDtypeStruct(x.shape, x.dtype) for x in results],
        in_specs=[pl.BlockSpec(memory_space=pl.ANY)] * 3,
        out_specs=[pl.BlockSpec(memory_space=pl.ANY)] * 3,
        scratch_shapes=[pltpu.VMEM(x.shape, x.dtype) for x in results]
        + [pltpu.SemaphoreType.DMA((6,))] * 2,
        compiler_params=pltpu.CompilerParams(vmem_limit_bytes=60 * 1024 * 1024),
    )(*results)


def solution(mesh):
    return jax.shard_map(
        per_device,
        mesh=mesh,
        in_specs=(
            P(None, ("sweep", "dom")),
            P(None, ("sweep", "dom")),
            P(None, None, None, ("sweep", "dom")),
            P(None, ("sweep", "dom")),
            P(("sweep", "dom")),
            P(("sweep", "dom"), None),
            P(("sweep", "dom")),
            P(None, ("sweep", "dom")),
            P(("sweep", "dom")),
            P(("sweep", "dom"), None),
            P(("sweep", "dom")),
            P(("sweep", "dom"), None, None),
        ),
        out_specs=(P(None, ("sweep", "dom")), P(None, ("sweep", "dom")), P(None, ("sweep", "dom"))),
        check_vma=False,
    )
```
